32 devices in a mesh: scan: 2 (over x), tile: 8 (over z, y), row: 2 (over core).
Axes of the slice: x: 2, y: 2, z: 4, core: 2. Of those that a mesh axis runs over, the one named last changes fastest.
Arguments:
- object_tiles: float32 [16, 2, 256, 256], P(('scan', 'tile')), parts along dimension 0, may hold values from -6 to 6
- probe_modes: float32 [4, 2, 256, 256], P('row'), may hold values from -6 to 6
- amplitude: float32 [32, 256, 256], P(('scan', 'tile')), parts along dimension 0, may hold values from 0 to 4
- offsets: int32 [32, 2], P(('scan', 'tile')), parts along dimension 0, may hold values from 0 to 1792, as said below
- counts: int32 [16], P(('scan', 'tile')), parts along dimension 0, may hold values from 1 to 2, as said below
Outputs:
- new_object: float32 [16, 2, 256, 256], P(('scan', 'tile')), parts along dimension 0
- new_probe: float32 [8, 2, 256, 256], P(('scan', 'row')), parts along dimension 0
The draws below stay inside these ranges and needn't reach their ends.
There are 2 independent parts, one for each index of `scan`. The reference program is written for one: setup_inputs(seed, part) draws one part's arguments, and reference() takes and returns one part's arrays. A program takes and returns all parts, laid end to end along the dimension named above; an argument that names none is the same for every part. Nothing has to cross between parts.
Inputs may be any that keep to these rules, and one draw needn't show every extreme that they name: The patch of slot p lies inside the object, and its centre, offsets[p] + 128 in both coordinates, lies in tile p // 2. The first slot's patch sits at the object's top-left corner and the last tile's first slot's patch at its bottom-right corner. `counts`: at least one tile holds 2 live slots; a tile's live slots are its first ones.
All inputs are finite; a program needn't handle non-finite values.
Results may differ from the reference program's by a relative error of at most 0.0001.
Values sent between devices are 32-bit elements; how exact they have to be, the bound alone decides.
No kernel may reach another device: no remote copies, remote signals or barrier semaphores. Data moves between devices by JAX's collectives and lax.ppermute only.
A program may use at most 64 MiB of HBM per device.

```python
import jax
import jax.numpy as jnp
from jax import lax

S = 256
MODES = 4
TS = 256
GX = 8
ITERS = 2
POS_DEV = 2
TILES = 8
GY = 1
NPOS = 16


def draw_offsets(key, part):
    key = jax.random.fold_in(key, 11)
    half_width = S // 2
    slot_ids = jnp.arange(NPOS, dtype=jnp.int32)
    tile_ids = slot_ids // POS_DEV
    grid_row = tile_ids // GX
    grid_col = tile_ids % GX
    row_low = jnp.where(grid_row == 0, half_width, 0)
    row_high = jnp.where(grid_row == GY - 1, TS - half_width + 1, TS)
    col_low = jnp.where(grid_col == 0, half_width, 0)
    col_high = jnp.where(grid_col == GX - 1, TS - half_width + 1, TS)
    key_pair = jax.random.split(key)
    row_centre = jax.random.randint(key_pair[0], (NPOS,), row_low, row_high, dtype=jnp.int32)
    col_centre = jax.random.randint(key_pair[1], (NPOS,), col_low, col_high, dtype=jnp.int32)
    last_first = (TILES - 1) * POS_DEV
    row_centre = jnp.where(slot_ids == 0, row_low, jnp.where(slot_ids == last_first, row_high - 1, row_centre))
    col_centre = jnp.where(slot_ids == 0, col_low, jnp.where(slot_ids == last_first, col_high - 1, col_centre))
    row_corner = grid_row * TS + row_centre - half_width
    col_corner = grid_col * TS + col_centre - half_width
    return jnp.stack([row_corner, col_corner], axis=1).astype(jnp.int32)


def draw_counts(key, part):
    key = jax.random.fold_in(key, 23)
    key_pair = jax.random.split(key)
    drawn = jax.random.randint(key_pair[0], (TILES,), 1, POS_DEV + 1, dtype=jnp.int32)
    chosen = jax.random.randint(key_pair[1], (), 0, TILES, dtype=jnp.int32)
    tile_ids = jnp.arange(TILES, dtype=jnp.int32)
    return jnp.where(tile_ids == chosen, POS_DEV, drawn).astype(jnp.int32)


def shard_levels(rng, extent, shards, low, top_value):
    def one(position, blocks):
        steps = jax.random.uniform(jax.random.fold_in(jax.random.fold_in(rng, 6), position), (blocks,), jnp.float32, low / len(shards), top_value / len(shards))
        return jnp.repeat(jnp.exp(steps), extent[position] // blocks).reshape((-1,) + (1,) * (len(extent) - position - 1))

    gain = one(*shards[0])
    for cut in shards[1:]:
        gain = gain * one(*cut)
    return gain


def centred(rng, dims, width, limit, cuts=(), kind=jnp.bfloat16):
    values = width * jax.random.normal(rng, dims, jnp.float32)
    if cuts:
        values = values * shard_levels(rng, dims, cuts, -0.22, 0.18)
    return jnp.clip(values, -limit, limit).astype(kind)


def setup_inputs(seed: int = 0, part: int = 0) -> dict:
    seeds = jax.random.split(jax.random.key(seed), 6)
    own_keys = jax.random.split(jax.random.fold_in(seeds[5], part), 6)
    object_tiles = centred(own_keys[0], (TILES, 2, TS, TS), 1.0, 6.0, ((0, 8),), jnp.float32)
    probe_modes = centred(seeds[1], (MODES, 2, S, S), 1.0, 6.0, ((0, 2),), jnp.float32)
    amplitude = jnp.clip(4.0 * jax.random.uniform(own_keys[2], (NPOS, S, S), jnp.float32) ** shard_levels(own_keys[2], (NPOS, S, S), ((0, 8),), -0.2, 0.2), 0.0, 4.0)
    offsets = draw_offsets(jax.random.fold_in(jax.random.fold_in(seeds[5], part), 71), part)
    counts = draw_counts(jax.random.fold_in(jax.random.fold_in(seeds[5], part), 71), part)
    return {"object_tiles": object_tiles, "probe_modes": probe_modes, "amplitude": amplitude, "offsets": offsets, "counts": counts}


def reference(object_tiles, probe_modes, amplitude, offsets, counts):
    stacked = object_tiles.reshape(GY, GX, 2, TS, TS)
    assembled = jnp.transpose(stacked, (2, 0, 3, 1, 4)).reshape(2, GY * TS, GX * TS)
    field_now = lax.complex(assembled[0], assembled[1])
    probe_now = lax.complex(probe_modes[:, 0], probe_modes[:, 1])
    slot_ids = jnp.arange(NPOS, dtype=jnp.int32)
    live_mask = (slot_ids % POS_DEV < counts[slot_ids // POS_DEV]).astype(object_tiles.dtype)
    for iteration in range(ITERS):

        def visit(state, inputs):
            object_grad, probe_grad = state
            corner, measured, weight = inputs
            object_patch = lax.dynamic_slice(field_now, (corner[0], corner[1]), (S, S))
            exit_wave = probe_now * object_patch[None]
            far_field = jnp.fft.fft2(exit_wave, norm='ortho')
            power_sum = lax.optimization_barrier(jnp.sum(jnp.real(far_field) ** 2 + jnp.imag(far_field) ** 2, axis=0))
            factor = measured / (jnp.sqrt(power_sum) + 0.5)
            revised = jnp.fft.ifft2(far_field * factor[None], norm='ortho')
            update = (revised - exit_wave) * weight
            local_grad = lax.optimization_barrier(jnp.sum(jnp.conj(probe_now) * update, axis=0))
            current = lax.dynamic_slice(object_grad, (corner[0], corner[1]), (S, S))
            object_grad = lax.dynamic_update_slice(object_grad, current + local_grad, (corner[0], corner[1]))
            probe_grad = probe_grad + jnp.conj(object_patch)[None] * update
            return ((object_grad, probe_grad), None)
        start = (jnp.zeros_like(field_now), jnp.zeros_like(probe_now))
        (object_grad, probe_grad), unused = lax.scan(visit, start, (offsets, amplitude, live_mask))
        field_now = field_now + object_grad / MODES
        probe_now = probe_now + 4.0 / NPOS * probe_grad
    parts_both = jnp.stack([jnp.real(field_now), jnp.imag(field_now)])
    tiles_out = jnp.transpose(parts_both.reshape(2, GY, TS, GX, TS), (1, 3, 0, 2, 4)).reshape(GY * GX, 2, TS, TS)
    probe_out = jnp.stack([jnp.real(probe_now), jnp.imag(probe_now)], axis=1)
    return (tiles_out, probe_out)
```

```python
import functools
import math

import jax
import jax.numpy as jnp
import numpy as np
from jax import lax
from jax.experimental import pallas as pl
from jax.experimental.pallas import tpu as pltpu
from jax.sharding import PartitionSpec as P

MODES = 4
GX = 8
ITERS = 2
CHUNK_BITS = 3
CHUNKS = 1 << CHUNK_BITS
ORDERS = ((0, 1, 2), (1, 0, 2))

f32 = jnp.float32
bf16 = jnp.bfloat16


def tables(length):
    half = length // 2
    n = np.arange(half)
    out = []
    for odd in (0, 1):
        angle = 2.0 * math.pi * np.outer(2 * n + odd, n) / length
        c, s = np.cos(angle) / math.sqrt(length), np.sin(angle) / math.sqrt(length)
        out.append(np.block([[c, s], [-s, c]]))
    forward = np.stack(out)
    both = np.stack([forward, np.transpose(forward, (0, 2, 1))]).astype(np.float32)
    high = both.astype(bf16)
    low = (both - high.astype(np.float32)).astype(bf16)
    return np.stack([high, low], axis=2)


def deinterleave(length):
    half = length // 2
    out = np.zeros((length, length), np.float32)
    out[2 * np.arange(half), np.arange(half)] = 1.0
    out[2 * np.arange(half) + 1, half + np.arange(half)] = 1.0
    return np.stack([out, out.T]).astype(bf16)


def split(x):
    high = x.astype(bf16)
    return high, (x - high.astype(f32)).astype(bf16)


def dot(a, b):
    return jnp.dot(a, b, preferred_element_type=f32)


def mul_left(table, x):
    high, low = split(x)
    return dot(table[0], high) + (dot(table[1], high) + dot(table[0], low))


def mul_right(x, table):
    high, low = split(x)
    return dot(high, table[0]) + (dot(high, table[1]) + dot(low, table[0]))


def forward(xr, xi, tab):
    h = xr.shape[0] // 2
    even = jnp.concatenate([xr[:h] + xr[h:], xi[:h] + xi[h:]], 0)
    odd = jnp.concatenate([xr[:h] - xr[h:], xi[:h] - xi[h:]], 0)
    ye = mul_left((tab[0, 0, 0], tab[0, 0, 1]), even)
    yo = mul_left((tab[0, 1, 0], tab[0, 1, 1]), odd)
    yr = jnp.concatenate([ye[:h], yo[:h]], 0)
    yi = jnp.concatenate([ye[h:], yo[h:]], 0)
    even = jnp.concatenate([yr[:, :h] + yr[:, h:], yi[:, :h] + yi[:, h:]], 1)
    odd = jnp.concatenate([yr[:, :h] - yr[:, h:], yi[:, :h] - yi[:, h:]], 1)
    fe = mul_right(even, (tab[1, 0, 0], tab[1, 0, 1]))
    fo = mul_right(odd, (tab[1, 1, 0], tab[1, 1, 1]))
    return fe, fo


def inverse(fe, fo, tab):
    h = fe.shape[0] // 2
    he = mul_right(fe, (tab[0, 0, 0], tab[0, 0, 1]))
    ho = mul_right(fo, (tab[0, 1, 0], tab[0, 1, 1]))
    yr = jnp.concatenate([he[:, :h] + ho[:, :h], he[:, :h] - ho[:, :h]], 1)
    yi = jnp.concatenate([he[:, h:] + ho[:, h:], he[:, h:] - ho[:, h:]], 1)
    xe = mul_left((tab[1, 0, 0], tab[1, 0, 1]), jnp.concatenate([yr[:h], yi[:h]], 0))
    xo = mul_left((tab[1, 1, 0], tab[1, 1, 1]), jnp.concatenate([yr[h:], yi[h:]], 0))
    xr = jnp.concatenate([xe[:h] + xo[:h], xe[:h] - xo[:h]], 0)
    xi = jnp.concatenate([xe[h:] + xo[h:], xe[h:] - xo[h:]], 0)
    return xr, xi


def exact(x):
    high = x.astype(bf16)
    rest = x - high.astype(f32)
    mid = rest.astype(bf16)
    return high, mid, (rest - mid.astype(f32)).astype(bf16)


def amplitude_kernel(amp, perm, out):
    for s in range(amp.shape[0]):
        high, mid, low = exact(amp[s])
        rows = dot(perm[1], high) + (dot(perm[1], mid) + dot(perm[1], low))
        high, mid, low = exact(rows)
        out[s] = dot(high, perm[0]) + (dot(mid, perm[0]) + dot(low, perm[0]))


def update_probe(sm, old, pieces, coef, out):
    rows = old.shape[2] // CHUNKS
    for mode in range(len(pieces)):
        rel = 0
        for piece in pieces[mode]:
            for k in range(piece.shape[0]):
                start = pl.multiple_of((rel ^ sm[4 + mode]) * rows, rows)
                here = pl.ds(start, rows)
                out[mode, :, here, :] = old[mode, :, here, :] + coef * piece[k]
                rel += 1


def forward_kernel(slot, n_pieces, coef, tall, *refs):
    refs = list(refs)
    sm, near, far_half, probe, tab = refs[:5]
    refs = refs[5:]
    if n_pieces:
        modes = probe.shape[0]
        pieces = [refs[m * n_pieces : (m + 1) * n_pieces] for m in range(modes)]
        refs = refs[modes * n_pieces :]
        new_probe = refs.pop(3)
        update_probe(sm, probe, pieces, coef, new_probe)
        probe = new_probe
    far, power, patch, window = refs
    frame = probe.shape[-1]
    core = sm[6]
    window[core] = near[...]
    window[1 - core] = far_half[...]
    cols = window.shape[-1]
    for c in range(2):
        whole = jnp.concatenate([window[0, c], window[1, c]], 0)
        moved = pltpu.roll(whole, lax.rem(cols - sm[slot], cols), 1)[:, :frame]
        if tall:
            rows = whole.shape[0]
            moved = pltpu.roll(moved, lax.rem(rows - sm[2 + slot], rows), 0)[:frame]
        patch[c] = moved
    total = None
    for m in range(probe.shape[0]):
        pr, pi = probe[m, 0], probe[m, 1]
        exit_real = pr * patch[0] - pi * patch[1]
        exit_imag = pr * patch[1] + pi * patch[0]
        fe, fo = forward(exit_real, exit_imag, tab)
        far[m, 0] = fe
        far[m, 1] = fo
        h = frame // 2
        sq = jnp.concatenate(
            [fe[:, :h] * fe[:, :h] + fe[:, h:] * fe[:, h:], fo[:, :h] * fo[:, :h] + fo[:, h:] * fo[:, h:]], 1
        )
        total = sq if total is None else total + sq
    power[...] = total


def inverse_kernel(mode, last, tall, *refs):
    refs = list(refs)
    sm, tab, amp, probe = refs[:4]
    refs = refs[4:]
    slots = amp.shape[0]
    fars, powers, others, patches = (refs[i * slots : (i + 1) * slots] for i in range(4))
    refs = refs[4 * slots :]
    if mode:
        before = refs.pop(0)
    send, keep = refs[:2]
    refs = refs[2:]
    frame = probe.shape[-1]
    h = frame // 2
    pr, pi = probe[mode, 0], probe[mode, 1]
    probe_real = probe_imag = None
    windows = [None, None]
    for s in range(slots):
        live = (s < sm[7]).astype(f32)
        factor = amp[s] / (jnp.sqrt(powers[s][...] + others[s][...]) + 0.5)
        even = jnp.concatenate([factor[:, :h]] * 2, 1)
        odd = jnp.concatenate([factor[:, h:]] * 2, 1)
        xr, xi = inverse(fars[s][mode, 0] * even, fars[s][mode, 1] * odd, tab)
        ar, ai = patches[s][0], patches[s][1]
        ur = (xr - (pr * ar - pi * ai)) * live
        ui = (xi - (pr * ai + pi * ar)) * live
        gr = pr * ur + pi * ui
        gi = pr * ui - pi * ur
        qr = ar * ur + ai * ui
        qi = ar * ui - ai * ur
        probe_real = qr if probe_real is None else probe_real + qr
        probe_imag = qi if probe_imag is None else probe_imag + qi
        if mode:
            gr = gr + before[s, 0]
            gi = gi + before[s, 1]
        if not last:
            refs[0][s, 0] = gr
            refs[0][s, 1] = gi
        else:
            near, away = refs[0], refs[1]
            cols, rows = near.shape[-1], 2 * near.shape[1]
            for c, g in enumerate((gr, gi)):
                if tall:
                    g = jnp.concatenate([g, jnp.zeros((rows - frame, frame), f32)], 0)
                    g = pltpu.roll(g, sm[2 + s], 0)
                g = jnp.concatenate([g, jnp.zeros((rows, cols - frame), f32)], 1)
                g = pltpu.roll(g, sm[s], 1)
                windows[c] = g if windows[c] is None else windows[c] + g
    if last:
        near, away, both = refs
        core = sm[6]
        hr = near.shape[1]
        for c in range(2):
            both[0, c] = windows[c][:hr]
            both[1, c] = windows[c][hr:]
        near[...] = both[core]
        away[...] = both[1 - core]
    work = refs[-1] if not last else None
    rows = frame // CHUNKS
    quarter = CHUNKS // 2
    for c in range(CHUNKS):
        rel = c ^ sm[4 + mode]
        upper = rel >= quarter
        for k, q in enumerate((probe_real, probe_imag)):
            piece = q[c * rows : (c + 1) * rows]

            @pl.when(upper)
            def _():
                send[rel - quarter, k] = piece

            @pl.when(jnp.logical_not(upper))
            def _():
                keep[rel, k] = piece


def finish_kernel(n_pieces, coef, *refs):
    refs = list(refs)
    sm, near, away, probe = refs[:4]
    modes = probe.shape[0]
    pieces = [refs[4 + m * n_pieces : 4 + (m + 1) * n_pieces] for m in range(modes)]
    tile, new_probe = refs[-2:]
    update_probe(sm, probe, pieces, coef, new_probe)
    hr = near.shape[1]
    core = sm[6]
    tile[:, pl.ds(pl.multiple_of(core * hr, hr), hr), :] = near[...]
    tile[:, pl.ds(pl.multiple_of((1 - core) * hr, hr), hr), :] = away[...]


def vmem():
    return pl.BlockSpec(memory_space=pltpu.VMEM)


def call(kernel, outs, args, scratch=(), flops=0):
    size = sum(math.prod(a.shape) * a.dtype.itemsize for a in args)
    size += sum(math.prod(o) * 4 for o in outs)
    return pl.pallas_call(
        kernel,
        out_shape=[jax.ShapeDtypeStruct(o, f32) for o in outs],
        in_specs=[
            pl.BlockSpec(memory_space=pltpu.SMEM) if a.ndim == 1 else vmem() for a in args
        ],
        out_specs=[vmem() for _ in outs],
        scratch_shapes=list(scratch),
        cost_estimate=pl.CostEstimate(flops=flops, bytes_accessed=size, transcendentals=0),
        compiler_params=pltpu.CompilerParams(vmem_limit_bytes=40 * 1024 * 1024),
    )(*args)


def swap_rows(x):
    return lax.ppermute(x, "row", [(0, 1), (1, 0)])


def shift_cols(x, step, tiles):
    pairs = [(s, s + step) for s in range(tiles) if 0 <= s % GX + step < GX]
    return lax.ppermute(x, "tile", pairs)


def swap_vertical(x, tiles):
    pairs = [(2 * t, 2 * (t - GX) + 1) for t in range(GX, tiles)]
    pairs += [(2 * t + 1, 2 * (t + GX)) for t in range(tiles - GX)]
    return lax.ppermute(x, ("tile", "row"), pairs)


def exchange(x, bit, tiles):
    return lax.ppermute(x, "tile", [(s, s ^ (1 << bit)) for s in range(tiles)])


def reduce_chunks(send, keep, order, tiles):
    bits = int(math.log2(tiles))
    for i, bit in enumerate(order):
        got = exchange(send, bit, tiles)
        if i + 1 < len(order):
            n = keep.shape[0] // 2
            send, keep = keep[n:] + got[n:], keep[:n] + got[:n]
        else:
            keep = keep + got
    for bit in range(CHUNK_BITS, bits):
        keep = keep + exchange(keep, bit, tiles)
    pieces = [keep]
    for bit in reversed(order):
        block = pieces[0] if len(pieces) == 1 else jnp.concatenate(pieces, 0)
        pieces.append(exchange(block, bit, tiles))
    return pieces


def per_device(object_tiles, probe_modes, amplitude, offsets, counts):
    own_tile = object_tiles[0]
    size = own_tile.shape[-1]
    frame = probe_modes.shape[-1]
    half = frame // 2
    tiles = lax.axis_size("tile")
    tall = tiles > GX
    slots = offsets.shape[0]
    modes = probe_modes.shape[0]
    t = lax.axis_index("tile")
    core = lax.axis_index("row")
    hr = size // 2
    col0 = (t % GX) * size - half
    row0 = (t // GX) * size - (half if tall else 0)

    def key(order):
        return sum(((t >> bit) & 1) << (len(order) - 1 - i) for i, bit in enumerate(order))

    scalars = jnp.stack(
        [offsets[0, 1] - col0, offsets[1, 1] - col0, offsets[0, 0] - row0, offsets[1, 0] - row0]
        + [key(o) for o in ORDERS]
        + [core, counts[0]]
    ).astype(jnp.int32)
    tab = jnp.asarray(tables(frame))
    perm = jnp.asarray(deinterleave(frame))
    coef = 4.0 / (slots * tiles)

    mine = lax.dynamic_slice(own_tile, (0, core * hr, 0), (2, hr, size))
    from_left = shift_cols(mine[:, :, size - half :], 1, tiles)
    from_right = shift_cols(mine[:, :, :half], -1, tiles)
    near = jnp.concatenate([from_left, mine, from_right], 2)
    if tall:
        other = swap_vertical(near, tiles)
        near = jnp.where(core == 0, jnp.concatenate([other, near], 1), jnp.concatenate([near, other], 1))
    away = swap_rows(near)
    (amp,) = call(amplitude_kernel, [amplitude.shape], [amplitude, perm])

    matmul = 2 * 3 * 4 * frame**3
    probe = probe_modes
    pieces = None
    for iteration in range(ITERS):
        fars, powers, others, patches = [], [], [], []
        for s in range(slots):
            args = [scalars, near, away, probe, tab]
            outs = [(modes, 2, frame, frame), (frame, frame), (2, frame, frame)]
            count = 0
            if pieces is not None:
                count = len(pieces[0])
                args += [p for group in pieces for p in group]
                outs.append(probe.shape)
                pieces = None
            got = call(
                functools.partial(forward_kernel, s, count, coef, tall),
                outs,
                args,
                [pltpu.VMEM((2,) + near.shape, f32)],
                matmul * modes,
            )
            if count:
                probe = got[3]
            fars.append(got[0])
            powers.append(got[1])
            patches.append(got[2])
            others.append(swap_rows(got[1]))
        before = None
        pieces = []
        for m in range(modes):
            last = m == modes - 1
            args = [scalars, tab, amp, probe] + fars + powers + others + patches
            if m:
                args.append(before)
            part = (CHUNKS // 2, 2, frame // CHUNKS, frame)
            outs = [part, part]
            outs += [near.shape, near.shape] if last else [(slots, 2, frame, frame)]
            scratch = [pltpu.VMEM((2,) + near.shape, f32)] if last else []
            got = call(
                functools.partial(inverse_kernel, m, last, tall), outs, args, scratch, matmul * slots
            )
            before = got[2]
            pieces.append((got[0], got[1]))
        grad = got[2] + swap_rows(got[3])
        pieces = [reduce_chunks(a, b, o, tiles) for (a, b), o in zip(pieces, ORDERS)]
        if iteration + 1 < ITERS or tall:
            left, right = grad[:, :, :size], grad[:, :, size:]
            left = left + shift_cols(right, 1, tiles)
            right = right + shift_cols(grad[:, :, :size], -1, tiles)
            total = jnp.concatenate([left, right], 2)
            if tall:
                total = total + swap_vertical(total, tiles)
            near = near + total / MODES
            if iteration + 1 < ITERS:
                away = swap_rows(near)
            else:
                near = near[:, :, half : half + size]
                near = jnp.where(core == 0, near[:, half:], near[:, : size - half])
        else:
            got_left = shift_cols(grad[:, :, half + size :], 1, tiles)
            got_right = shift_cols(grad[:, :, :half], -1, tiles)
            total = grad[:, :, half : half + size] + jnp.concatenate([got_left, got_right], 2)
            near = near[:, :, half : half + size] + total / MODES
    away = swap_rows(near)
    args = [scalars, near, away, probe] + [p for group in pieces for p in group]
    tile, probe = call(
        functools.partial(finish_kernel, len(pieces[0]), coef), [own_tile.shape, probe.shape], args
    )
    return (tile[None], probe)


def solution(mesh):
    return jax.shard_map(
        per_device,
        mesh=mesh,
        in_specs=(
            P(("scan", "tile"), None, None, None),
            P("row", None, None, None),
            P(("scan", "tile"), None, None),
            P(("scan", "tile"), None),
            P(("scan", "tile")),
        ),
        out_specs=(P(("scan", "tile"), None, None, None), P(("scan", "row"), None, None, None)),
        check_vma=False,
    )
```

```python
import functools
import math

import jax
import jax.numpy as jnp
import numpy as np
from jax import lax
from jax.experimental import pallas as pl
from jax.experimental.pallas import tpu as pltpu
from jax.sharding import PartitionSpec as P

MODES = 4
GX = 8
ITERS = 2
HALVINGS = 2
CHUNKS = 1 << HALVINGS
ORDERS = ((0, 1, 2), (1, 0, 2))

f32 = jnp.float32
bf16 = jnp.bfloat16


def tables(length):
    half = length // 2
    n = np.arange(half)
    left, right = [], []
    for transposed in (False, True):
        for odd in (0, 1):
            angle = 2.0 * math.pi * np.outer(2 * n + odd, n) / length
            c, s = np.cos(angle) / math.sqrt(length), np.sin(angle) / math.sqrt(length)
            matrix = np.block([[c, s], [-s, c]])
            matrix = (matrix.T if transposed else matrix).astype(np.float32)
            high = matrix.astype(bf16)
            low = (matrix - high.astype(np.float32)).astype(bf16)
            left.append(np.concatenate([high, low, high], 1))
            right.append(np.concatenate([high, high, low], 0))
    return np.stack(left).reshape(2, 2, length, -1), np.stack(right).reshape(2, 2, -1, length)


def deinterleave(length):
    half = length // 2
    out = np.zeros((length, length), np.float32)
    out[2 * np.arange(half), np.arange(half)] = 1.0
    out[2 * np.arange(half) + 1, half + np.arange(half)] = 1.0
    return np.stack([out, out.T]).astype(bf16)


def split(x):
    high = x.astype(bf16)
    return high, (x - high.astype(f32)).astype(bf16)


def dot(a, b):
    return jnp.dot(a, b, preferred_element_type=f32)


def mul_left(table, x):
    high, low = split(x)
    return dot(table, jnp.concatenate([high, high, low], 0))


def mul_right(x, table):
    high, low = split(x)
    return dot(jnp.concatenate([high, low, high], 1), table)


def forward(fields, left, right):
    h = fields[0][0].shape[0] // 2
    width = 2 * h
    even = [jnp.concatenate([x[:h] + x[h:] for x in f], 0) for f in fields]
    odd = [jnp.concatenate([x[:h] - x[h:] for x in f], 0) for f in fields]
    ye = mul_left(left[0, 0], jnp.concatenate(even, 1))
    yo = mul_left(left[0, 1], jnp.concatenate(odd, 1))
    even, odd = [], []
    for i in range(len(fields)):
        at = slice(i * width, (i + 1) * width)
        parts = [jnp.concatenate([y[k * h : (k + 1) * h, at] for y in (ye, yo)], 0) for k in range(2)]
        even.append(jnp.concatenate([y[:, :h] + y[:, h:] for y in parts], 1))
        odd.append(jnp.concatenate([y[:, :h] - y[:, h:] for y in parts], 1))
    fe = mul_right(jnp.concatenate(even, 0), right[1, 0])
    fo = mul_right(jnp.concatenate(odd, 0), right[1, 1])
    return [(fe[i * width : (i + 1) * width], fo[i * width : (i + 1) * width]) for i in range(len(fields))]


def inverse(fields, left, right):
    h = fields[0][0].shape[0] // 2
    width = 2 * h
    he = mul_right(jnp.concatenate([f[0] for f in fields], 0), right[0, 0])
    ho = mul_right(jnp.concatenate([f[1] for f in fields], 0), right[0, 1])
    ys = [
        jnp.concatenate([he[:, k] + ho[:, k], he[:, k] - ho[:, k]], 1) for k in (slice(0, h), slice(h, width))
    ]
    even, odd = [], []
    for i in range(len(fields)):
        even.append(jnp.concatenate([y[i * width : i * width + h] for y in ys], 0))
        odd.append(jnp.concatenate([y[i * width + h : (i + 1) * width] for y in ys], 0))
    xe = mul_left(left[1, 0], jnp.concatenate(even, 1))
    xo = mul_left(left[1, 1], jnp.concatenate(odd, 1))
    parts = [
        jnp.concatenate([xe[k] + xo[k], xe[k] - xo[k]], 0) for k in (slice(0, h), slice(h, width))
    ]
    return [[x[:, i * width : (i + 1) * width] for x in parts] for i in range(len(fields))]


def exact(x):
    high = x.astype(bf16)
    rest = x - high.astype(f32)
    mid = rest.astype(bf16)
    return high, mid, (rest - mid.astype(f32)).astype(bf16)


def amplitude_kernel(amp, perm, out):
    for s in range(amp.shape[0]):
        high, mid, low = exact(amp[s])
        rows = dot(perm[1], high) + (dot(perm[1], mid) + dot(perm[1], low))
        high, mid, low = exact(rows)
        out[s] = dot(high, perm[0]) + (dot(mid, perm[0]) + dot(low, perm[0]))


def chunk_key(order):
    t = lax.axis_index("tile")
    return sum(((t >> order[i]) & 1) << (HALVINGS - 1 - i) for i in range(HALVINGS))


def corner(offsets, slot, dim, size, margin):
    t = lax.axis_index("tile")
    along = lax.rem(t, GX) if dim else lax.div(t, GX)
    return offsets[slot, dim] - along * size + margin


def update_probe(old, pieces, coef, out):
    rows = old.shape[2] // CHUNKS
    for mode in range(len(pieces)):
        key = chunk_key(ORDERS[mode])
        rel = 0
        for piece in pieces[mode]:
            for k in range(piece.shape[0]):
                here = pl.ds(pl.multiple_of((rel ^ key) * rows, rows), rows)
                out[mode, :, here, :] = old[mode, :, here, :] + coef * piece[k]
                rel += 1


def forward_kernel(slot, n_pieces, coef, tall, *refs):
    refs = list(refs)
    offsets, near, away, probe, left, right = refs[:6]
    refs = refs[6:]
    modes = probe.shape[0]
    if n_pieces:
        pieces = [refs[m * n_pieces : (m + 1) * n_pieces] for m in range(modes)]
        refs = refs[modes * n_pieces :]
        new_probe = refs.pop(3)
        update_probe(probe, pieces, coef, new_probe)
        probe = new_probe
    far, power, patch, window = refs
    frame = probe.shape[-1]
    h = frame // 2
    core = lax.axis_index("row")
    window[core] = near[...]
    window[1 - core] = away[...]
    cols = window.shape[-1]
    size = cols - 2 * h
    for c in range(2):
        whole = jnp.concatenate([window[0, c], window[1, c]], 0)
        moved = pltpu.roll(whole, lax.rem(cols - corner(offsets, slot, 1, size, h), cols), 1)[:, :frame]
        if tall:
            rows = whole.shape[0]
            moved = pltpu.roll(moved, lax.rem(rows - corner(offsets, slot, 0, size, h), rows), 0)[:frame]
        patch[c] = moved
    ar, ai = patch[0], patch[1]
    exits = [
        (probe[m, 0] * ar - probe[m, 1] * ai, probe[m, 0] * ai + probe[m, 1] * ar) for m in range(modes)
    ]
    total = None
    for m, pair in enumerate(forward(exits, left, right)):
        for k in range(2):
            far[m, k] = pair[k]
        sq = jnp.concatenate([f[:, :h] * f[:, :h] + f[:, h:] * f[:, h:] for f in pair], 1)
        total = sq if total is None else total + sq
    power[...] = total


def inverse_kernel(mode, last, tall, *refs):
    refs = list(refs)
    offsets, counts, left, right, amp, probe = refs[:6]
    refs = refs[6:]
    slots = amp.shape[0]
    fars, powers, others, patches = (refs[i * slots : (i + 1) * slots] for i in range(4))
    refs = refs[4 * slots :]
    before = refs.pop(0) if mode else None
    send, keep = refs[:2]
    refs = refs[2:]
    frame = probe.shape[-1]
    h = frame // 2
    pr, pi = probe[mode, 0], probe[mode, 1]
    fields = []
    for s in range(slots):
        factor = amp[s] / (jnp.sqrt(powers[s][...] + others[s][...]) + 0.5)
        fields.append(
            [fars[s][mode, k] * jnp.concatenate([factor[:, k * h : (k + 1) * h]] * 2, 1) for k in range(2)]
        )
    probe_grad = None
    windows = [None, None]
    for s, (xr, xi) in enumerate(inverse(fields, left, right)):
        live = (s < counts[0]).astype(f32)
        ar, ai = patches[s][0], patches[s][1]
        ur = (xr - (pr * ar - pi * ai)) * live
        ui = (xi - (pr * ai + pi * ar)) * live
        grad = [pr * ur + pi * ui, pr * ui - pi * ur]
        step = [ar * ur + ai * ui, ar * ui - ai * ur]
        probe_grad = step if s == 0 else [a + b for a, b in zip(probe_grad, step)]
        for c, g in enumerate(grad):
            if mode:
                g = g + before[s, c]
            if not last:
                refs[0][s, c] = g
                continue
            cols, rows = refs[0].shape[-1], 2 * refs[0].shape[1]
            size = cols - 2 * h
            if tall:
                g = jnp.concatenate([g, jnp.zeros((rows - frame, frame), f32)], 0)
                g = pltpu.roll(g, corner(offsets, s, 0, size, h), 0)
            g = jnp.concatenate([g, jnp.zeros((rows, cols - frame), f32)], 1)
            g = pltpu.roll(g, corner(offsets, s, 1, size, h), 1)
            windows[c] = g if s == 0 else windows[c] + g
    if last:
        near, away, both = refs
        core = lax.axis_index("row")
        hr = near.shape[1]
        for c in range(2):
            for k in range(2):
                both[k, c] = windows[c][k * hr : (k + 1) * hr]
        near[...] = both[core]
        away[...] = both[1 - core]
    rows = frame // CHUNKS
    part = CHUNKS // 2
    key = chunk_key(ORDERS[mode])
    for c in range(CHUNKS):
        rel = c ^ key
        for k in range(2):
            piece = probe_grad[k][c * rows : (c + 1) * rows]

            @pl.when(rel >= part)
            def _():
                send[rel - part, k] = piece

            @pl.when(rel < part)
            def _():
                keep[rel, k] = piece


def finish_kernel(n_pieces, coef, *refs):
    refs = list(refs)
    near, away, probe = refs[:3]
    pieces = [refs[3 + m * n_pieces : 3 + (m + 1) * n_pieces] for m in range(probe.shape[0])]
    tile, new_probe = refs[-2:]
    update_probe(probe, pieces, coef, new_probe)
    hr = near.shape[1]
    core = lax.axis_index("row")
    tile[:, pl.ds(pl.multiple_of(core * hr, hr), hr), :] = near[...]
    tile[:, pl.ds(pl.multiple_of((1 - core) * hr, hr), hr), :] = away[...]


def vmem():
    return pl.BlockSpec(memory_space=pltpu.VMEM)


def call(kernel, outs, args, scratch=(), flops=0):
    size = sum(math.prod(a.shape) * a.dtype.itemsize for a in args)
    size += sum(math.prod(o) * 4 for o in outs)
    return pl.pallas_call(
        kernel,
        out_shape=[jax.ShapeDtypeStruct(o, f32) for o in outs],
        in_specs=[
            pl.BlockSpec(memory_space=pltpu.SMEM) if a.dtype == jnp.int32 else vmem() for a in args
        ],
        out_specs=[vmem() for _ in outs],
        scratch_shapes=list(scratch),
        cost_estimate=pl.CostEstimate(flops=flops, bytes_accessed=size, transcendentals=0),
        compiler_params=pltpu.CompilerParams(vmem_limit_bytes=40 * 1024 * 1024),
    )(*args)


def swap_rows(x):
    return lax.ppermute(x, "row", [(0, 1), (1, 0)])


def shift_cols(x, step, tiles):
    pairs = [(s, s + step) for s in range(tiles) if 0 <= s % GX + step < GX]
    return lax.ppermute(x, "tile", pairs)


def swap_vertical(x, tiles):
    pairs = [(2 * t, 2 * (t - GX) + 1) for t in range(GX, tiles)]
    pairs += [(2 * t + 1, 2 * (t + GX)) for t in range(tiles - GX)]
    return lax.ppermute(x, ("tile", "row"), pairs)


def exchange(x, bit, tiles):
    return lax.ppermute(x, "tile", [(s, s ^ (1 << bit)) for s in range(tiles)])


def together(*groups):
    return lax.optimization_barrier(groups)


def window_sum(grad, size, half, tiles, tall, wide):
    if wide:
        left, right = grad[:, :, :size], grad[:, :, size:]
        right_side = shift_cols(left, -1, tiles)
        left_side = shift_cols(right, 1, tiles)
        total = jnp.concatenate([left + left_side, right + right_side], 2)
        return total + swap_vertical(total, tiles) if tall else total
    got_left = shift_cols(grad[:, :, half + size :], 1, tiles)
    got_right = shift_cols(grad[:, :, :half], -1, tiles)
    return grad[:, :, half : half + size] + jnp.concatenate([got_left, got_right], 2)


def reduce_all(parts, grad, tiles, window):
    bits = int(math.log2(tiles))
    parts = [list(p) for p in parts]
    for i in range(HALVINGS):
        got = [exchange(p[0], o[i], tiles) for p, o in zip(parts, ORDERS)]
        for p, g in zip(parts, got):
            if i + 1 < HALVINGS:
                n = g.shape[0] // 2
                p[:] = p[1][n:] + g[n:], p[1][:n] + g[:n]
            else:
                p[:] = [p[1] + g]
    held = [p[0] for p in parts]
    held, grad = together(held, grad)
    got = [exchange(h, o[-1], tiles) for h, o in zip(held, ORDERS)]
    near = window(grad)
    held = [h + g for h, g in zip(held, got)]
    for bit in range(len(ORDERS[0]), bits):
        held = [h + exchange(h, bit, tiles) for h in held]
    pieces = [[h] for h in held]
    for i in reversed(range(HALVINGS)):
        for p, o in zip(pieces, ORDERS):
            p.append(exchange(p[0] if len(p) == 1 else jnp.concatenate(p, 0), o[i], tiles))
    return pieces, near


def per_device(object_tiles, probe_modes, amplitude, offsets, counts):
    own_tile = object_tiles[0]
    size = own_tile.shape[-1]
    frame = probe_modes.shape[-1]
    half = frame // 2
    tiles = lax.axis_size("tile")
    tall = tiles > GX
    slots = offsets.shape[0]
    modes = probe_modes.shape[0]
    core = lax.axis_index("row")
    hr = size // 2
    left, right = (jnp.asarray(x) for x in tables(frame))
    perm = jnp.asarray(deinterleave(frame))
    coef = 4.0 / (slots * tiles)

    mine = lax.dynamic_slice(own_tile, (0, core * hr, 0), (2, hr, size))
    from_left = shift_cols(mine[:, :, size - half :], 1, tiles)
    from_right = shift_cols(mine[:, :, :half], -1, tiles)
    near = jnp.concatenate([from_left, mine, from_right], 2)
    if tall:
        other = swap_vertical(near, tiles)
        near = jnp.where(core == 0, jnp.concatenate([other, near], 1), jnp.concatenate([near, other], 1))
    (amp,) = call(amplitude_kernel, [amplitude.shape], [amplitude, perm])
    away = swap_rows(near)
    near, away, amp = together(near, away, amp)

    matmul = 4 * 2 * 3 * 4 * frame**3
    probe = probe_modes
    pieces = None
    for iteration in range(ITERS):
        final = iteration + 1 == ITERS
        fars, powers, others, patches = [], [], [], []
        for s in range(slots):
            args = [offsets, near, away, probe, left, right]
            outs = [(modes, 2, frame, frame), (frame, frame), (2, frame, frame)]
            count = 0
            if pieces is not None:
                count = len(pieces[0])
                args += [p for group in pieces for p in group]
                outs.append(probe.shape)
                pieces = None
            got = call(
                functools.partial(forward_kernel, s, count, coef, tall),
                outs,
                args,
                [pltpu.VMEM((2,) + near.shape, f32)],
                matmul * modes,
            )
            if count:
                probe = got[3]
            fars.append(got[0])
            powers.append(got[1])
            patches.append(got[2])
            others.append(swap_rows(got[1]))
        before = None
        parts = []
        for m in range(modes):
            last = m == modes - 1
            args = [offsets, counts, left, right, amp, probe] + fars + powers + others + patches
            if m:
                args.append(before)
            part = (CHUNKS // 2, 2, frame // CHUNKS, frame)
            outs = [part, part]
            outs += [near.shape, near.shape] if last else [(slots, 2, frame, frame)]
            scratch = [pltpu.VMEM((2,) + near.shape, f32)] if last else []
            got = call(
                functools.partial(inverse_kernel, m, last, tall), outs, args, scratch, matmul * slots
            )
            before = got[2]
            parts.append((got[0], got[1]))
        grad = got[2] + swap_rows(got[3])
        wide = tall or not final
        pieces, total = reduce_all(
            parts, grad, tiles, lambda g: window_sum(g, size, half, tiles, tall, wide)
        )
        if wide:
            near = near + total / MODES
        else:
            near = near[:, :, half : half + size] + total / MODES
        if tall and final:
            near = near[:, :, half : half + size]
            near = jnp.where(core == 0, near[:, half:], near[:, : size - half])
        away = swap_rows(near)
    args = [near, away, probe] + [p for group in pieces for p in group]
    tile, probe = call(
        functools.partial(finish_kernel, len(pieces[0]), coef), [own_tile.shape, probe.shape], args
    )
    return (tile[None], probe)


def solution(mesh):
    return jax.shard_map(
        per_device,
        mesh=mesh,
        in_specs=(
            P(("scan", "tile"), None, None, None),
            P("row", None, None, None),
            P(("scan", "tile"), None, None),
            P(("scan", "tile"), None),
            P(("scan", "tile")),
        ),
        out_specs=(P(("scan", "tile"), None, None, None), P(("scan", "row"), None, None, None)),
        check_vma=False,
    )
```

```python
import functools
import math

import jax
import jax.numpy as jnp
import numpy as np
from jax import lax
from jax.experimental import pallas as pl
from jax.experimental.pallas import tpu as pltpu
from jax.sharding import PartitionSpec as P

MODES = 4
GX = 8
ITERS = 2
HALVINGS = 2
CHUNKS = 1 << HALVINGS
STRIP = 16
ORDERS = ((0, 1, 2), (1, 0, 2))

f32 = jnp.float32
bf16 = jnp.bfloat16


def tables(length):
    half = length // 2
    n = np.arange(half)
    out = []
    for odd in (0, 1):
        angle = 2.0 * math.pi * np.outer(2 * n + odd, n) / length
        c, s = np.cos(angle) / math.sqrt(length), np.sin(angle) / math.sqrt(length)
        out.append(np.block([[c, s], [-s, c]]))
    both = np.stack([np.stack(out), np.stack([m.T for m in out])]).astype(np.float32)
    high = both.astype(bf16)
    return np.stack([high, (both - high.astype(np.float32)).astype(bf16)], axis=2)


def deinterleave(length):
    half = length // 2
    out = np.zeros((length, length), np.float32)
    out[2 * np.arange(half), np.arange(half)] = 1.0
    out[2 * np.arange(half) + 1, half + np.arange(half)] = 1.0
    return np.stack([out, out.T]).astype(bf16)


def split(x):
    high = x.astype(bf16)
    return high, (x - high.astype(f32)).astype(bf16)


def dot(a, b):
    return jnp.dot(a, b, preferred_element_type=f32)


def mul_left(table, x):
    return dot(jnp.concatenate([table[0], table[1], table[0]], 1), jnp.concatenate([x[0], x[0], x[1]], 0))


def mul_right(x, table):
    return dot(jnp.concatenate([x[0], x[1], x[0]], 1), jnp.concatenate([table[0], table[0], table[1]], 0))


def put(ref, where, rows, cols, x):
    for k, part in enumerate(split(x)):
        ref[where, k, rows, cols] = part


def strips(count, body):
    lax.fori_loop(0, count, lambda i, c: (body(i), c)[1], 0)


def at(start, length=STRIP):
    return pl.ds(pl.multiple_of(start, STRIP), length)


def exact(x):
    high = x.astype(bf16)
    rest = x - high.astype(f32)
    mid = rest.astype(bf16)
    return high, mid, (rest - mid.astype(f32)).astype(bf16)


def amplitude_kernel(amp, perm, out):
    for s in range(amp.shape[0]):
        high, mid, low = exact(amp[s])
        rows = dot(perm[1], high) + (dot(perm[1], mid) + dot(perm[1], low))
        high, mid, low = exact(rows)
        out[s] = dot(high, perm[0]) + (dot(mid, perm[0]) + dot(low, perm[0]))


def chunk_key(order):
    t = lax.axis_index("tile")
    return sum(((t >> order[i]) & 1) << (HALVINGS - 1 - i) for i in range(HALVINGS))


def corner(offsets, slot, dim, size, margin):
    t = lax.axis_index("tile")
    along = lax.rem(t, GX) if dim else lax.div(t, GX)
    return offsets[slot, dim] - along * size + margin


def update_probe(old, pieces, coef, out):
    rows = old.shape[2] // CHUNKS
    for mode in range(len(pieces)):
        key = chunk_key(ORDERS[mode])
        rel = 0
        for piece in pieces[mode]:
            for k in range(piece.shape[0]):
                here = pl.ds(pl.multiple_of((rel ^ key) * rows, rows), rows)
                out[mode, :, here, :] = old[mode, :, here, :] + coef * piece[k]
                rel += 1


def shift_in(offsets, slot, near, away, patch, tall):
    frame = patch.shape[-1]
    h = frame // 2
    cols, hr = near.shape[-1], near.shape[1]
    size = cols - 2 * h
    core = lax.axis_index("row")
    across = lax.rem(cols - corner(offsets, slot, 1, size, h), cols)
    if tall:
        down = lax.rem(2 * hr - corner(offsets, slot, 0, size, h), 2 * hr)
        for c in range(2):
            both = [jnp.where(core == k, near[c], away[c]) for k in range(2)]
            moved = pltpu.roll(jnp.concatenate(both, 0), across, 1)[:, :frame]
            patch[c] = pltpu.roll(moved, down, 0)[:frame]
        return

    def body(j):
        for ref, half in ((near, core), (away, 1 - core)):
            for c in range(2):
                x = pltpu.roll(ref[c, at(j * STRIP), :], across, 1)
                patch[c, at(half * hr + j * STRIP), :] = x[:, :frame]

    strips(hr // STRIP, body)


def forward_kernel(slot, n_pieces, coef, tall, *refs):
    refs = list(refs)
    offsets, near, away, probe, tab = refs[:5]
    refs = refs[5:]
    modes = probe.shape[0]
    if n_pieces:
        pieces = [refs[m * n_pieces : (m + 1) * n_pieces] for m in range(modes)]
        refs = refs[modes * n_pieces :]
        new_probe = refs.pop(3)
        update_probe(probe, pieces, coef, new_probe)
        probe = new_probe
    far, power, patch, tall_parts, wide_parts, product = refs
    frame = probe.shape[-1]
    h = frame // 2
    shift_in(offsets, slot, near, away, patch, tall)

    def exits(j):
        for m in range(modes):
            pair = []
            for start in (j * STRIP, h + j * STRIP):
                rows = at(start)
                pr, pi = probe[m, 0, rows, :], probe[m, 1, rows, :]
                ar, ai = patch[0, rows, :], patch[1, rows, :]
                pair.append((pr * ar - pi * ai, pr * ai + pi * ar))
            cols = slice(m * frame, (m + 1) * frame)
            for k in range(2):
                put(tall_parts, 0, at(k * h + j * STRIP), cols, pair[0][k] + pair[1][k])
                put(tall_parts, 1, at(k * h + j * STRIP), cols, pair[0][k] - pair[1][k])

    strips(h // STRIP, exits)
    for p in range(2):
        product[p] = mul_left(tab[0, p], tall_parts[p])

    def columns(j):
        for p in range(2):
            for m in range(modes):
                cols = slice(m * frame, (m + 1) * frame)
                y = [product[p, at(k * h + j * STRIP), cols] for k in range(2)]
                rows = at(m * frame + p * h + j * STRIP)
                put(wide_parts, 0, rows, slice(None), jnp.concatenate([v[:, :h] + v[:, h:] for v in y], 1))
                put(wide_parts, 1, rows, slice(None), jnp.concatenate([v[:, :h] - v[:, h:] for v in y], 1))

    strips(h // STRIP, columns)
    for q in range(2):
        out = mul_right(wide_parts[q], tab[1, q])
        for m in range(modes):
            far[m, q] = out[m * frame : (m + 1) * frame]

    def powers(j):
        rows = at(j * STRIP)
        for q in range(2):
            total = None
            for m in range(modes):
                f = far[m, q, rows, :]
                f = f * f
                f = f[:, :h] + f[:, h:]
                total = f if m == 0 else total + f
            power[rows, slice(q * h, (q + 1) * h)] = total

    strips(frame // STRIP, powers)


def inverse_kernel(mode, last, tall, *refs):
    refs = list(refs)
    offsets, counts, tab, amp, probe = refs[:5]
    refs = refs[5:]
    slots = amp.shape[0]
    fars, powers, others, patches = (refs[i * slots : (i + 1) * slots] for i in range(4))
    refs = refs[4 * slots :]
    before = refs.pop(0) if mode else None
    probe_grad, grads, tall_parts, wide_parts, product_wide, product_tall = refs[:6]
    frame = probe.shape[-1]
    h = frame // 2

    def factors(j):
        rows = at(j * STRIP)
        for s in range(slots):
            factor = amp[s, rows, :] / (jnp.sqrt(powers[s][rows, :] + others[s][rows, :]) + 0.5)
            for q in range(2):
                f = factor[:, q * h : (q + 1) * h]
                put(
                    wide_parts,
                    q,
                    at(s * frame + j * STRIP),
                    slice(None),
                    fars[s][mode, q, rows, :] * jnp.concatenate([f, f], 1),
                )

    strips(frame // STRIP, factors)
    for q in range(2):
        product_wide[q] = mul_right(wide_parts[q], tab[0, q])

    def columns(j):
        for p in range(2):
            for s in range(slots):
                rows = at(s * frame + p * h + j * STRIP)
                he, ho = product_wide[0, rows, :], product_wide[1, rows, :]
                cols = slice(s * frame, (s + 1) * frame)
                for k in range(2):
                    a, b = he[:, k * h : (k + 1) * h], ho[:, k * h : (k + 1) * h]
                    put(tall_parts, p, at(k * h + j * STRIP), cols, jnp.concatenate([a + b, a - b], 1))

    strips(h // STRIP, columns)
    for p in range(2):
        product_tall[p] = mul_left(tab[1, p], tall_parts[p])
    key = chunk_key(ORDERS[mode])
    chunk = frame // CHUNKS
    core = lax.axis_index("row")

    def results(j):
        x = [[product_tall[p, at(k * h + j * STRIP), :] for k in range(2)] for p in range(2)]
        for lower in range(2):
            rows = at(lower * h + j * STRIP)
            pr, pi = probe[mode, 0, rows, :], probe[mode, 1, rows, :]
            step = [None, None]
            window = [None, None]
            for s in range(slots):
                cols = slice(s * frame, (s + 1) * frame)
                xr, xi = (
                    x[0][k][:, cols] - x[1][k][:, cols] if lower else x[0][k][:, cols] + x[1][k][:, cols]
                    for k in range(2)
                )
                live = (s < counts[0]).astype(f32)
                ar, ai = patches[s][0, rows, :], patches[s][1, rows, :]
                ur = (xr - (pr * ar - pi * ai)) * live
                ui = (xi - (pr * ai + pi * ar)) * live
                for k, g in enumerate((ar * ur + ai * ui, ar * ui - ai * ur)):
                    step[k] = g if s == 0 else step[k] + g
                for k, g in enumerate((pr * ur + pi * ui, pr * ui - pi * ur)):
                    if mode:
                        g = g + before[s, k, rows, :]
                    if not last or tall:
                        grads[s, k, rows, :] = g
                        continue
                    wide = grads.shape[-1]
                    g = jnp.concatenate([g, jnp.zeros((STRIP, wide - frame), f32)], 1)
                    g = pltpu.roll(g, corner(offsets, s, 1, wide - 2 * h, h), 1)
                    window[k] = g if s == 0 else window[k] + g
            start = lower * h + j * STRIP
            rel = lax.div(start, chunk) ^ key
            for k in range(2):
                probe_grad[rel, k, at(lax.rem(start, chunk)), :] = step[k]
                if last and not tall:
                    grads[lower ^ core, k, at(j * STRIP), :] = window[k]

    strips(h // STRIP, results)


def place_kernel(offsets, grads, out):
    slots, _, frame, _ = grads.shape
    _, _, hr, cols = out.shape
    h = frame // 2
    size = cols - 2 * h
    core = lax.axis_index("row")
    for c in range(2):
        total = None
        for s in range(slots):
            g = jnp.concatenate([grads[s, c], jnp.zeros((2 * hr - frame, frame), f32)], 0)
            g = pltpu.roll(g, corner(offsets, s, 0, size, h), 0)
            g = jnp.concatenate([g, jnp.zeros((2 * hr, cols - frame), f32)], 1)
            g = pltpu.roll(g, corner(offsets, s, 1, size, h), 1)
            total = g if s == 0 else total + g
        for k in range(2):
            out[k ^ core, c] = total[k * hr : (k + 1) * hr]


def finish_kernel(n_pieces, coef, *refs):
    refs = list(refs)
    near, away, probe = refs[:3]
    pieces = [refs[3 + m * n_pieces : 3 + (m + 1) * n_pieces] for m in range(probe.shape[0])]
    tile, new_probe = refs[-2:]
    update_probe(probe, pieces, coef, new_probe)
    hr = near.shape[1]
    core = lax.axis_index("row")
    tile[:, pl.ds(pl.multiple_of(core * hr, hr), hr), :] = near[...]
    tile[:, pl.ds(pl.multiple_of((1 - core) * hr, hr), hr), :] = away[...]


def vmem():
    return pl.BlockSpec(memory_space=pltpu.VMEM)


def call(kernel, outs, args, scratch=(), flops=0):
    size = sum(math.prod(a.shape) * a.dtype.itemsize for a in args)
    size += sum(math.prod(o) * 4 for o in outs)
    return pl.pallas_call(
        kernel,
        out_shape=[jax.ShapeDtypeStruct(o, f32) for o in outs],
        in_specs=[
            pl.BlockSpec(memory_space=pltpu.SMEM) if a.dtype == jnp.int32 else vmem() for a in args
        ],
        out_specs=[vmem() for _ in outs],
        scratch_shapes=list(scratch),
        cost_estimate=pl.CostEstimate(flops=flops, bytes_accessed=size, transcendentals=0),
        compiler_params=pltpu.CompilerParams(vmem_limit_bytes=40 * 1024 * 1024),
    )(*args)


def swap_rows(x):
    return lax.ppermute(x, "row", [(0, 1), (1, 0)])


def shift_cols(x, step, tiles):
    pairs = [(s, s + step) for s in range(tiles) if 0 <= s % GX + step < GX]
    return lax.ppermute(x, "tile", pairs)


def swap_vertical(x, tiles):
    pairs = [(2 * t, 2 * (t - GX) + 1) for t in range(GX, tiles)]
    pairs += [(2 * t + 1, 2 * (t + GX)) for t in range(tiles - GX)]
    return lax.ppermute(x, ("tile", "row"), pairs)


def exchange(x, bit, tiles):
    return lax.ppermute(x, "tile", [(s, s ^ (1 << bit)) for s in range(tiles)])


def together(*groups):
    return lax.optimization_barrier(groups)


def window_sum(grad, size, half, tiles, tall, wide):
    if wide:
        left, right = grad[:, :, :size], grad[:, :, size:]
        right_side = shift_cols(left, -1, tiles)
        left_side = shift_cols(right, 1, tiles)
        total = jnp.concatenate([left + left_side, right + right_side], 2)
        return total + swap_vertical(total, tiles) if tall else total
    got_left = shift_cols(grad[:, :, half + size :], 1, tiles)
    got_right = shift_cols(grad[:, :, :half], -1, tiles)
    return grad[:, :, half : half + size] + jnp.concatenate([got_left, got_right], 2)


def reduce_all(parts, grad, tiles, window):
    bits = int(math.log2(tiles))
    held = list(parts)
    for i in range(HALVINGS):
        n = held[0].shape[0] // 2
        got = [exchange(h[n:], o[i], tiles) for h, o in zip(held, ORDERS)]
        held = [h[:n] + g for h, g in zip(held, got)]
    held, grad = together(held, grad)
    got = [exchange(h, o[-1], tiles) for h, o in zip(held, ORDERS)]
    near = window(grad)
    held = [h + g for h, g in zip(held, got)]
    for bit in range(len(ORDERS[0]), bits):
        held = [h + exchange(h, bit, tiles) for h in held]
    pieces = [[h] for h in held]
    for i in reversed(range(HALVINGS)):
        for p, o in zip(pieces, ORDERS):
            p.append(exchange(p[0] if len(p) == 1 else jnp.concatenate(p, 0), o[i], tiles))
    return pieces, near


def per_device(object_tiles, probe_modes, amplitude, offsets, counts):
    own_tile = object_tiles[0]
    size = own_tile.shape[-1]
    frame = probe_modes.shape[-1]
    half = frame // 2
    tiles = lax.axis_size("tile")
    tall = tiles > GX
    slots = offsets.shape[0]
    modes = probe_modes.shape[0]
    core = lax.axis_index("row")
    hr = size // 2
    tab = jnp.asarray(tables(frame))
    perm = jnp.asarray(deinterleave(frame))
    coef = 4.0 / (slots * tiles)

    mine = lax.dynamic_slice(own_tile, (0, core * hr, 0), (2, hr, size))
    from_left = shift_cols(mine[:, :, size - half :], 1, tiles)
    from_right = shift_cols(mine[:, :, :half], -1, tiles)
    near = jnp.concatenate([from_left, mine, from_right], 2)
    if tall:
        other = swap_vertical(near, tiles)
        near = jnp.where(core == 0, jnp.concatenate([other, near], 1), jnp.concatenate([near, other], 1))
    (amp,) = call(amplitude_kernel, [amplitude.shape], [amplitude, perm])
    away = swap_rows(near)
    near, away, amp = together(near, away, amp)

    def scratch(count):
        return [
            pltpu.VMEM((2, 2, frame, count * frame), bf16),
            pltpu.VMEM((2, 2, count * frame, frame), bf16),
        ]

    matmul = 4 * 2 * 3 * 4 * frame**3
    probe = probe_modes
    pieces = None
    for iteration in range(ITERS):
        final = iteration + 1 == ITERS
        fars, powers, others, patches = [], [], [], []
        for s in range(slots):
            args = [offsets, near, away, probe, tab]
            outs = [(modes, 2, frame, frame), (frame, frame), (2, frame, frame)]
            count = 0
            if pieces is not None:
                count = len(pieces[0])
                args += [p for group in pieces for p in group]
                outs.append(probe.shape)
                pieces = None
            got = call(
                functools.partial(forward_kernel, s, count, coef, tall),
                outs,
                args,
                scratch(modes) + [pltpu.VMEM((2, frame, modes * frame), f32)],
                matmul * modes,
            )
            if count:
                probe = got[3]
            fars.append(got[0])
            powers.append(got[1])
            patches.append(got[2])
            others.append(swap_rows(got[1]))
        before = None
        parts = []
        for m in range(modes):
            last = m == modes - 1
            args = [offsets, counts, tab, amp, probe] + fars + powers + others + patches
            if m:
                args.append(before)
            grads = (2,) + near.shape if last and not tall else (slots, 2, frame, frame)
            got = call(
                functools.partial(inverse_kernel, m, last, tall),
                [(CHUNKS, 2, frame // CHUNKS, frame), grads],
                args,
                scratch(slots)
                + [pltpu.VMEM((2, slots * frame, frame), f32), pltpu.VMEM((2, frame, slots * frame), f32)],
                matmul * slots,
            )
            parts.append(got[0])
            before = got[1]
        if tall:
            (before,) = call(place_kernel, [(2,) + near.shape], [offsets, before])
        grad = before[0] + swap_rows(before[1])
        wide = tall or not final
        pieces, total = reduce_all(
            parts, grad, tiles, lambda g: window_sum(g, size, half, tiles, tall, wide)
        )
        if wide:
            near = near + total / MODES
        else:
            near = near[:, :, half : half + size] + total / MODES
        if tall and final:
            near = near[:, :, half : half + size]
            near = jnp.where(core == 0, near[:, half:], near[:, : size - half])
        away = swap_rows(near)
    args = [near, away, probe] + [p for group in pieces for p in group]
    tile, probe = call(
        functools.partial(finish_kernel, len(pieces[0]), coef), [own_tile.shape, probe.shape], args
    )
    return (tile[None], probe)


def solution(mesh):
    return jax.shard_map(
        per_device,
        mesh=mesh,
        in_specs=(
            P(("scan", "tile"), None, None, None),
            P("row", None, None, None),
            P(("scan", "tile"), None, None),
            P(("scan", "tile"), None),
            P(("scan", "tile")),
        ),
        out_specs=(P(("scan", "tile"), None, None, None), P(("scan", "row"), None, None, None)),
        check_vma=False,
    )
```

```python
import functools
import math

import jax
import jax.numpy as jnp
import numpy as np
from jax import lax
from jax.experimental import pallas as pl
from jax.experimental.pallas import tpu as pltpu
from jax.sharding import PartitionSpec as P

MODES = 4
GX = 8
ITERS = 2
HALVINGS = 2
CHUNKS = 1 << HALVINGS
STRIP = 16
ORDERS = ((0, 1, 2), (1, 0, 2))

f32 = jnp.float32
bf16 = jnp.bfloat16


def tables(length):
    half = length // 2
    n = np.arange(half)
    out = []
    for odd in (0, 1):
        angle = 2.0 * math.pi * np.outer(2 * n + odd, n) / length
        c, s = np.cos(angle) / math.sqrt(length), np.sin(angle) / math.sqrt(length)
        out.append(np.block([[c, s], [-s, c]]))
    both = np.stack([np.stack(out), np.stack([m.T for m in out])]).astype(np.float32)
    high = both.astype(bf16)
    return np.stack([high, (both - high.astype(np.float32)).astype(bf16)], axis=2)


def deinterleave(length):
    half = length // 2
    out = np.zeros((length, length), np.float32)
    out[2 * np.arange(half), np.arange(half)] = 1.0
    out[2 * np.arange(half) + 1, half + np.arange(half)] = 1.0
    return np.stack([out, out.T]).astype(bf16)


def split(x):
    high = x.astype(bf16)
    return high, (x - high.astype(f32)).astype(bf16)


def dot(a, b):
    return jnp.dot(a, b, preferred_element_type=f32)


def mul_left(table, x):
    return dot(jnp.concatenate([table[0], table[1], table[0]], 1), jnp.concatenate([x[0], x[0], x[1]], 0))


def mul_right(x, table):
    return dot(jnp.concatenate([x[0], x[1], x[0]], 1), jnp.concatenate([table[0], table[0], table[1]], 0))


def put(ref, where, rows, cols, x):
    for k, part in enumerate(split(x)):
        ref[where, k, rows, cols] = part


def strips(count, body):
    for i in range(count):
        body(i)


def at(start, length=STRIP):
    return pl.ds(start if isinstance(start, int) else pl.multiple_of(start, STRIP), length)


def exact(x):
    high = x.astype(bf16)
    rest = x - high.astype(f32)
    mid = rest.astype(bf16)
    return high, mid, (rest - mid.astype(f32)).astype(bf16)


def amplitude_kernel(amp, perm, out):
    for s in range(amp.shape[0]):
        high, mid, low = exact(amp[s])
        rows = dot(perm[1], high) + (dot(perm[1], mid) + dot(perm[1], low))
        high, mid, low = exact(rows)
        out[s] = dot(high, perm[0]) + (dot(mid, perm[0]) + dot(low, perm[0]))


def chunk_key(order):
    t = lax.axis_index("tile")
    return sum(((t >> order[i]) & 1) << (HALVINGS - 1 - i) for i in range(HALVINGS))


def corner(offsets, slot, dim, size, margin):
    t = lax.axis_index("tile")
    along = lax.rem(t, GX) if dim else lax.div(t, GX)
    return offsets[slot, dim] - along * size + margin


def update_probe(old, pieces, coef, out):
    rows = old.shape[2] // CHUNKS
    for mode in range(len(pieces)):
        key = chunk_key(ORDERS[mode])
        rel = 0
        for piece in pieces[mode]:
            for k in range(piece.shape[0]):
                here = pl.ds(pl.multiple_of((rel ^ key) * rows, rows), rows)
                out[mode, :, here, :] = old[mode, :, here, :] + coef * piece[k]
                rel += 1


def shift_in(offsets, slot, near, away, patch, tall):
    frame = patch.shape[-1]
    h = frame // 2
    cols, hr = near.shape[-1], near.shape[1]
    size = cols - 2 * h
    core = lax.axis_index("row")
    across = lax.rem(cols - corner(offsets, slot, 1, size, h), cols)
    if tall:
        down = lax.rem(2 * hr - corner(offsets, slot, 0, size, h), 2 * hr)
        for c in range(2):
            both = [jnp.where(core == k, near[c], away[c]) for k in range(2)]
            moved = pltpu.roll(jnp.concatenate(both, 0), across, 1)[:, :frame]
            patch[c] = pltpu.roll(moved, down, 0)[:frame]
        return

    def body(j):
        for ref, half in ((near, core), (away, 1 - core)):
            for c in range(2):
                x = pltpu.roll(ref[c, at(j * STRIP), :], across, 1)
                patch[c, at(half * hr + j * STRIP), :] = x[:, :frame]

    strips(hr // STRIP, body)


def forward_kernel(slot, n_pieces, coef, tall, *refs):
    refs = list(refs)
    offsets, near, away, probe, tab = refs[:5]
    refs = refs[5:]
    modes = probe.shape[0]
    if n_pieces:
        pieces = [refs[m * n_pieces : (m + 1) * n_pieces] for m in range(modes)]
        refs = refs[modes * n_pieces :]
        new_probe = refs.pop(3)
        update_probe(probe, pieces, coef, new_probe)
        probe = new_probe
    far, power, patch, tall_parts, wide_parts, product = refs
    frame = probe.shape[-1]
    h = frame // 2
    shift_in(offsets, slot, near, away, patch, tall)

    def exits(j):
        for m in range(modes):
            pair = []
            for start in (j * STRIP, h + j * STRIP):
                rows = at(start)
                pr, pi = probe[m, 0, rows, :], probe[m, 1, rows, :]
                ar, ai = patch[0, rows, :], patch[1, rows, :]
                pair.append((pr * ar - pi * ai, pr * ai + pi * ar))
            cols = slice(m * frame, (m + 1) * frame)
            for k in range(2):
                put(tall_parts, 0, at(k * h + j * STRIP), cols, pair[0][k] + pair[1][k])
                put(tall_parts, 1, at(k * h + j * STRIP), cols, pair[0][k] - pair[1][k])

    strips(h // STRIP, exits)
    for p in range(2):
        product[p] = mul_left(tab[0, p], tall_parts[p])

    def columns(j):
        for p in range(2):
            for m in range(modes):
                cols = slice(m * frame, (m + 1) * frame)
                y = [product[p, at(k * h + j * STRIP), cols] for k in range(2)]
                rows = at(m * frame + p * h + j * STRIP)
                put(wide_parts, 0, rows, slice(None), jnp.concatenate([v[:, :h] + v[:, h:] for v in y], 1))
                put(wide_parts, 1, rows, slice(None), jnp.concatenate([v[:, :h] - v[:, h:] for v in y], 1))

    strips(h // STRIP, columns)
    for q in range(2):
        out = mul_right(wide_parts[q], tab[1, q])
        for m in range(modes):
            far[m, q] = out[m * frame : (m + 1) * frame]

    def powers(j):
        rows = at(j * STRIP)
        for q in range(2):
            total = None
            for m in range(modes):
                f = far[m, q, rows, :]
                f = f * f
                f = f[:, :h] + f[:, h:]
                total = f if m == 0 else total + f
            power[rows, slice(q * h, (q + 1) * h)] = total

    strips(frame // STRIP, powers)


def inverse_kernel(mode, last, tall, *refs):
    refs = list(refs)
    offsets, counts, tab, amp, probe = refs[:5]
    refs = refs[5:]
    slots = amp.shape[0]
    fars, powers, others, patches = (refs[i * slots : (i + 1) * slots] for i in range(4))
    refs = refs[4 * slots :]
    before = refs.pop(0) if mode else None
    probe_grad, grads, tall_parts, wide_parts, product_wide, product_tall = refs[:6]
    frame = probe.shape[-1]
    h = frame // 2

    def factors(j):
        rows = at(j * STRIP)
        for s in range(slots):
            factor = amp[s, rows, :] / (jnp.sqrt(powers[s][rows, :] + others[s][rows, :]) + 0.5)
            for q in range(2):
                f = factor[:, q * h : (q + 1) * h]
                put(
                    wide_parts,
                    q,
                    at(s * frame + j * STRIP),
                    slice(None),
                    fars[s][mode, q, rows, :] * jnp.concatenate([f, f], 1),
                )

    strips(frame // STRIP, factors)
    for q in range(2):
        product_wide[q] = mul_right(wide_parts[q], tab[0, q])

    def columns(j):
        for p in range(2):
            for s in range(slots):
                rows = at(s * frame + p * h + j * STRIP)
                he, ho = product_wide[0, rows, :], product_wide[1, rows, :]
                cols = slice(s * frame, (s + 1) * frame)
                for k in range(2):
                    a, b = he[:, k * h : (k + 1) * h], ho[:, k * h : (k + 1) * h]
                    put(tall_parts, p, at(k * h + j * STRIP), cols, jnp.concatenate([a + b, a - b], 1))

    strips(h // STRIP, columns)
    for p in range(2):
        product_tall[p] = mul_left(tab[1, p], tall_parts[p])
    key = chunk_key(ORDERS[mode])
    chunk = frame // CHUNKS
    core = lax.axis_index("row")

    def results(j):
        x = [[product_tall[p, at(k * h + j * STRIP), :] for k in range(2)] for p in range(2)]
        for lower in range(2):
            rows = at(lower * h + j * STRIP)
            pr, pi = probe[mode, 0, rows, :], probe[mode, 1, rows, :]
            step = [None, None]
            window = [None, None]
            for s in range(slots):
                cols = slice(s * frame, (s + 1) * frame)
                xr, xi = (
                    x[0][k][:, cols] - x[1][k][:, cols] if lower else x[0][k][:, cols] + x[1][k][:, cols]
                    for k in range(2)
                )
                live = (s < counts[0]).astype(f32)
                ar, ai = patches[s][0, rows, :], patches[s][1, rows, :]
                ur = (xr - (pr * ar - pi * ai)) * live
                ui = (xi - (pr * ai + pi * ar)) * live
                for k, g in enumerate((ar * ur + ai * ui, ar * ui - ai * ur)):
                    step[k] = g if s == 0 else step[k] + g
                for k, g in enumerate((pr * ur + pi * ui, pr * ui - pi * ur)):
                    if mode:
                        g = g + before[s, k, rows, :]
                    if not last or tall:
                        grads[s, k, rows, :] = g
                        continue
                    wide = grads.shape[-1]
                    g = jnp.concatenate([g, jnp.zeros((STRIP, wide - frame), f32)], 1)
                    g = pltpu.roll(g, corner(offsets, s, 1, wide - 2 * h, h), 1)
                    window[k] = g if s == 0 else window[k] + g
            start = lower * h + j * STRIP
            rel = (start // chunk) ^ key
            for k in range(2):
                probe_grad[rel, k, at(start % chunk), :] = step[k]
                if last and not tall:
                    grads[lower ^ core, k, at(j * STRIP), :] = window[k]

    strips(h // STRIP, results)


def place_kernel(offsets, grads, out):
    slots, _, frame, _ = grads.shape
    _, _, hr, cols = out.shape
    h = frame // 2
    size = cols - 2 * h
    core = lax.axis_index("row")
    for c in range(2):
        total = None
        for s in range(slots):
            g = jnp.concatenate([grads[s, c], jnp.zeros((2 * hr - frame, frame), f32)], 0)
            g = pltpu.roll(g, corner(offsets, s, 0, size, h), 0)
            g = jnp.concatenate([g, jnp.zeros((2 * hr, cols - frame), f32)], 1)
            g = pltpu.roll(g, corner(offsets, s, 1, size, h), 1)
            total = g if s == 0 else total + g
        for k in range(2):
            out[k ^ core, c] = total[k * hr : (k + 1) * hr]


def finish_kernel(n_pieces, coef, *refs):
    refs = list(refs)
    near, away, probe = refs[:3]
    pieces = [refs[3 + m * n_pieces : 3 + (m + 1) * n_pieces] for m in range(probe.shape[0])]
    tile, new_probe = refs[-2:]
    update_probe(probe, pieces, coef, new_probe)
    hr = near.shape[1]
    core = lax.axis_index("row")
    tile[:, pl.ds(pl.multiple_of(core * hr, hr), hr), :] = near[...]
    tile[:, pl.ds(pl.multiple_of((1 - core) * hr, hr), hr), :] = away[...]


def vmem():
    return pl.BlockSpec(memory_space=pltpu.VMEM)


def call(kernel, outs, args, scratch=(), flops=0):
    size = sum(math.prod(a.shape) * a.dtype.itemsize for a in args)
    size += sum(math.prod(o) * 4 for o in outs)
    return pl.pallas_call(
        kernel,
        out_shape=[jax.ShapeDtypeStruct(o, f32) for o in outs],
        in_specs=[
            pl.BlockSpec(memory_space=pltpu.SMEM) if a.dtype == jnp.int32 else vmem() for a in args
        ],
        out_specs=[vmem() for _ in outs],
        scratch_shapes=list(scratch),
        cost_estimate=pl.CostEstimate(flops=flops, bytes_accessed=size, transcendentals=0),
        compiler_params=pltpu.CompilerParams(vmem_limit_bytes=40 * 1024 * 1024),
    )(*args)


def swap_rows(x):
    return lax.ppermute(x, "row", [(0, 1), (1, 0)])


def shift_cols(x, step, tiles):
    pairs = [(s, s + step) for s in range(tiles) if 0 <= s % GX + step < GX]
    return lax.ppermute(x, "tile", pairs)


def swap_vertical(x, tiles):
    pairs = [(2 * t, 2 * (t - GX) + 1) for t in range(GX, tiles)]
    pairs += [(2 * t + 1, 2 * (t + GX)) for t in range(tiles - GX)]
    return lax.ppermute(x, ("tile", "row"), pairs)


def exchange(x, bit, tiles):
    return lax.ppermute(x, "tile", [(s, s ^ (1 << bit)) for s in range(tiles)])


def together(*groups):
    return lax.optimization_barrier(groups)


def window_sum(grad, size, half, tiles, tall, wide):
    if wide:
        left, right = grad[:, :, :size], grad[:, :, size:]
        right_side = shift_cols(left, -1, tiles)
        left_side = shift_cols(right, 1, tiles)
        total = jnp.concatenate([left + left_side, right + right_side], 2)
        return total + swap_vertical(total, tiles) if tall else total
    got_left = shift_cols(grad[:, :, half + size :], 1, tiles)
    got_right = shift_cols(grad[:, :, :half], -1, tiles)
    return grad[:, :, half : half + size] + jnp.concatenate([got_left, got_right], 2)


def reduce_all(parts, grad, tiles, window):
    bits = int(math.log2(tiles))
    held = list(parts)
    for i in range(HALVINGS):
        n = held[0].shape[0] // 2
        got = [exchange(h[n:], o[i], tiles) for h, o in zip(held, ORDERS)]
        held = [h[:n] + g for h, g in zip(held, got)]
    held, grad = together(held, grad)
    got = [exchange(h, o[-1], tiles) for h, o in zip(held, ORDERS)]
    near = window(grad)
    held = [h + g for h, g in zip(held, got)]
    for bit in range(len(ORDERS[0]), bits):
        held = [h + exchange(h, bit, tiles) for h in held]
    pieces = [[h] for h in held]
    for i in reversed(range(HALVINGS)):
        for p, o in zip(pieces, ORDERS):
            p.append(exchange(p[0] if len(p) == 1 else jnp.concatenate(p, 0), o[i], tiles))
    return pieces, near


def per_device(object_tiles, probe_modes, amplitude, offsets, counts):
    own_tile = object_tiles[0]
    size = own_tile.shape[-1]
    frame = probe_modes.shape[-1]
    half = frame // 2
    tiles = lax.axis_size("tile")
    tall = tiles > GX
    slots = offsets.shape[0]
    modes = probe_modes.shape[0]
    core = lax.axis_index("row")
    hr = size // 2
    tab = jnp.asarray(tables(frame))
    perm = jnp.asarray(deinterleave(frame))
    coef = 4.0 / (slots * tiles)

    mine = lax.dynamic_slice(own_tile, (0, core * hr, 0), (2, hr, size))
    from_left = shift_cols(mine[:, :, size - half :], 1, tiles)
    from_right = shift_cols(mine[:, :, :half], -1, tiles)
    near = jnp.concatenate([from_left, mine, from_right], 2)
    if tall:
        other = swap_vertical(near, tiles)
        near = jnp.where(core == 0, jnp.concatenate([other, near], 1), jnp.concatenate([near, other], 1))
    (amp,) = call(amplitude_kernel, [amplitude.shape], [amplitude, perm])
    away = swap_rows(near)
    near, away, amp = together(near, away, amp)

    def scratch(count):
        return [
            pltpu.VMEM((2, 2, frame, count * frame), bf16),
            pltpu.VMEM((2, 2, count * frame, frame), bf16),
        ]

    matmul = 4 * 2 * 3 * 4 * frame**3
    probe = probe_modes
    pieces = None
    for iteration in range(ITERS):
        final = iteration + 1 == ITERS
        fars, powers, others, patches = [], [], [], []
        for s in range(slots):
            args = [offsets, near, away, probe, tab]
            outs = [(modes, 2, frame, frame), (frame, frame), (2, frame, frame)]
            count = 0
            if pieces is not None:
                count = len(pieces[0])
                args += [p for group in pieces for p in group]
                outs.append(probe.shape)
                pieces = None
            got = call(
                functools.partial(forward_kernel, s, count, coef, tall),
                outs,
                args,
                scratch(modes) + [pltpu.VMEM((2, frame, modes * frame), f32)],
                matmul * modes,
            )
            if count:
                probe = got[3]
            fars.append(got[0])
            powers.append(got[1])
            patches.append(got[2])
            others.append(swap_rows(got[1]))
        before = None
        parts = []
        for m in range(modes):
            last = m == modes - 1
            args = [offsets, counts, tab, amp, probe] + fars + powers + others + patches
            if m:
                args.append(before)
            grads = (2,) + near.shape if last and not tall else (slots, 2, frame, frame)
            got = call(
                functools.partial(inverse_kernel, m, last, tall),
                [(CHUNKS, 2, frame // CHUNKS, frame), grads],
                args,
                scratch(slots)
                + [pltpu.VMEM((2, slots * frame, frame), f32), pltpu.VMEM((2, frame, slots * frame), f32)],
                matmul * slots,
            )
            parts.append(got[0])
            before = got[1]
        if tall:
            (before,) = call(place_kernel, [(2,) + near.shape], [offsets, before])
        grad = before[0] + swap_rows(before[1])
        wide = tall or not final
        pieces, total = reduce_all(
            parts, grad, tiles, lambda g: window_sum(g, size, half, tiles, tall, wide)
        )
        if wide:
            near = near + total / MODES
        else:
            near = near[:, :, half : half + size] + total / MODES
        if tall and final:
            near = near[:, :, half : half + size]
            near = jnp.where(core == 0, near[:, half:], near[:, : size - half])
        away = swap_rows(near)
    args = [near, away, probe] + [p for group in pieces for p in group]
    tile, probe = call(
        functools.partial(finish_kernel, len(pieces[0]), coef), [own_tile.shape, probe.shape], args
    )
    return (tile[None], probe)


def solution(mesh):
    return jax.shard_map(
        per_device,
        mesh=mesh,
        in_specs=(
            P(("scan", "tile"), None, None, None),
            P("row", None, None, None),
            P(("scan", "tile"), None, None),
            P(("scan", "tile"), None),
            P(("scan", "tile")),
        ),
        out_specs=(P(("scan", "tile"), None, None, None), P(("scan", "row"), None, None, None)),
        check_vma=False,
    )
```

```python
import functools
import math

import jax
import jax.numpy as jnp
import numpy as np
from jax import lax
from jax.experimental import pallas as pl
from jax.experimental.pallas import tpu as pltpu
from jax.sharding import PartitionSpec as P

MODES = 4
GX = 8
ITERS = 2
HALVINGS = 2
CHUNKS = 1 << HALVINGS
STRIP = 16
ORDERS = ((0, 1, 2), (1, 0, 2))

f32 = jnp.float32
bf16 = jnp.bfloat16


def tables(length):
    half = length // 2
    n = np.arange(half)
    out = []
    for odd in (0, 1):
        angle = 2.0 * math.pi * np.outer(2 * n + odd, n) / length
        c, s = np.cos(angle) / math.sqrt(length), np.sin(angle) / math.sqrt(length)
        out.append(np.block([[c, s], [-s, c]]))
    both = np.stack([np.stack(out), np.stack([m.T for m in out])]).astype(np.float32)
    high = both.astype(bf16)
    return np.stack([high, (both - high.astype(np.float32)).astype(bf16)], axis=2)


def deinterleave(length):
    half = length // 2
    out = np.zeros((length, length), np.float32)
    out[2 * np.arange(half), np.arange(half)] = 1.0
    out[2 * np.arange(half) + 1, half + np.arange(half)] = 1.0
    return np.stack([out, out.T]).astype(bf16)


def split(x):
    high = x.astype(bf16)
    return high, (x - high.astype(f32)).astype(bf16)


def dot(a, b):
    return jnp.dot(a, b, preferred_element_type=f32)


def mul_left(table, x):
    return dot(jnp.concatenate([table[0], table[1], table[0]], 1), jnp.concatenate([x[0], x[0], x[1]], 0))


def mul_right(x, table):
    return dot(jnp.concatenate([x[0], x[1], x[0]], 1), jnp.concatenate([table[0], table[0], table[1]], 0))


def put(ref, where, rows, cols, x):
    for k, part in enumerate(split(x)):
        ref[where, k, rows, cols] = part


def strips(count, body):
    for i in range(count):
        body(i)


def at(start, length=STRIP):
    return pl.ds(start if isinstance(start, int) else pl.multiple_of(start, STRIP), length)


def exact(x):
    high = x.astype(bf16)
    rest = x - high.astype(f32)
    mid = rest.astype(bf16)
    return high, mid, (rest - mid.astype(f32)).astype(bf16)


def amplitude_kernel(amp, perm, out):
    for s in range(amp.shape[0]):
        high, mid, low = exact(amp[s])
        rows = dot(perm[1], high) + (dot(perm[1], mid) + dot(perm[1], low))
        high, mid, low = exact(rows)
        out[s] = dot(high, perm[0]) + (dot(mid, perm[0]) + dot(low, perm[0]))


def chunk_key(order):
    t = lax.axis_index("tile")
    return sum(((t >> order[i]) & 1) << (HALVINGS - 1 - i) for i in range(HALVINGS))


def corner(offsets, slot, dim, size, margin):
    t = lax.axis_index("tile")
    along = lax.rem(t, GX) if dim else lax.div(t, GX)
    return offsets[slot, dim] - along * size + margin


def left_half():
    return 1 - lax.rem(lax.axis_index("tile"), 2)


def update_probe(old, streams, coef, out):
    rows = old.shape[2] // CHUNKS
    for i, pieces in enumerate(streams):
        mode, part = divmod(i, 2)
        key = chunk_key(ORDERS[part])
        rel = 0
        for piece in pieces:
            for k in range(piece.shape[0]):
                here = pl.ds(pl.multiple_of((rel ^ key) * rows, rows), rows)
                out[mode, part, here, :] = old[mode, part, here, :] + coef * piece[k]
                rel += 1


def grouped(refs, streams, per_stream):
    return [refs[i * per_stream : (i + 1) * per_stream] for i in range(streams)]


def shift_in(offsets, slot, near, away, patch, tall):
    frame = patch.shape[-1]
    h = frame // 2
    hr, cols = near.shape[2], 2 * near.shape[3]
    size = cols - 2 * h
    core = lax.axis_index("row")
    first = left_half()
    across = lax.rem(cols - corner(offsets, slot, 1, size, h), cols)

    def strip(ref, c, rows):
        x = jnp.concatenate([ref[first, c, rows, :], ref[1 - first, c, rows, :]], 1)
        return pltpu.roll(x, across, 1)[:, :frame]

    if tall:
        down = lax.rem(2 * hr - corner(offsets, slot, 0, size, h), 2 * hr)
        for c in range(2):
            halves = [strip(ref, c, slice(None)) for ref in (near, away)]
            both = [jnp.where(core == k, halves[0], halves[1]) for k in range(2)]
            patch[c] = pltpu.roll(jnp.concatenate(both, 0), down, 0)[:frame]
        return

    def body(j):
        for ref, half in ((near, core), (away, 1 - core)):
            for c in range(2):
                patch[c, at(half * hr + j * STRIP), :] = strip(ref, c, at(j * STRIP))

    strips(hr // STRIP, body)


def forward_kernel(slot, n_pieces, coef, tall, *refs):
    refs = list(refs)
    offsets, near, away, probe, tab = refs[:5]
    refs = refs[5:]
    modes = probe.shape[0]
    if n_pieces:
        streams = grouped(refs, 2 * modes, n_pieces)
        refs = refs[2 * modes * n_pieces :]
        new_probe = refs.pop(3)
        update_probe(probe, streams, coef, new_probe)
        probe = new_probe
    far, power, patch, tall_parts, wide_parts, product = refs
    frame = probe.shape[-1]
    h = frame // 2
    shift_in(offsets, slot, near, away, patch, tall)

    def exits(j):
        for m in range(modes):
            pair = []
            for start in (j * STRIP, h + j * STRIP):
                rows = at(start)
                pr, pi = probe[m, 0, rows, :], probe[m, 1, rows, :]
                ar, ai = patch[0, rows, :], patch[1, rows, :]
                pair.append((pr * ar - pi * ai, pr * ai + pi * ar))
            cols = slice(m * frame, (m + 1) * frame)
            for k in range(2):
                put(tall_parts, 0, at(k * h + j * STRIP), cols, pair[0][k] + pair[1][k])
                put(tall_parts, 1, at(k * h + j * STRIP), cols, pair[0][k] - pair[1][k])

    strips(h // STRIP, exits)
    for p in range(2):
        product[p] = mul_left(tab[0, p], tall_parts[p])

    def columns(j):
        for p in range(2):
            for m in range(modes):
                cols = slice(m * frame, (m + 1) * frame)
                y = [product[p, at(k * h + j * STRIP), cols] for k in range(2)]
                rows = at(m * frame + p * h + j * STRIP)
                put(wide_parts, 0, rows, slice(None), jnp.concatenate([v[:, :h] + v[:, h:] for v in y], 1))
                put(wide_parts, 1, rows, slice(None), jnp.concatenate([v[:, :h] - v[:, h:] for v in y], 1))

    strips(h // STRIP, columns)
    for q in range(2):
        out = mul_right(wide_parts[q], tab[1, q])
        for m in range(modes):
            far[m, q] = out[m * frame : (m + 1) * frame]

    def powers(j):
        rows = at(j * STRIP)
        for q in range(2):
            total = None
            for m in range(modes):
                f = far[m, q, rows, :]
                f = f * f
                f = f[:, :h] + f[:, h:]
                total = f if m == 0 else total + f
            power[rows, slice(q * h, (q + 1) * h)] = total

    strips(frame // STRIP, powers)


def inverse_kernel(mode, last, tall, *refs):
    refs = list(refs)
    offsets, counts, tab, amp, probe = refs[:5]
    refs = refs[5:]
    slots = amp.shape[0]
    fars, powers, others, patches = (refs[i * slots : (i + 1) * slots] for i in range(4))
    refs = refs[4 * slots :]
    before = refs.pop(0) if mode else None
    probe_grad, refs = refs[:2], refs[2:]
    grads, tall_parts, wide_parts, product_wide, product_tall = refs
    frame = probe.shape[-1]
    h = frame // 2

    def factors(j):
        rows = at(j * STRIP)
        for s in range(slots):
            factor = amp[s, rows, :] / (jnp.sqrt(powers[s][rows, :] + others[s][rows, :]) + 0.5)
            for q in range(2):
                f = factor[:, q * h : (q + 1) * h]
                put(
                    wide_parts,
                    q,
                    at(s * frame + j * STRIP),
                    slice(None),
                    fars[s][mode, q, rows, :] * jnp.concatenate([f, f], 1),
                )

    strips(frame // STRIP, factors)
    for q in range(2):
        product_wide[q] = mul_right(wide_parts[q], tab[0, q])

    def columns(j):
        for p in range(2):
            for s in range(slots):
                rows = at(s * frame + p * h + j * STRIP)
                he, ho = product_wide[0, rows, :], product_wide[1, rows, :]
                cols = slice(s * frame, (s + 1) * frame)
                for k in range(2):
                    a, b = he[:, k * h : (k + 1) * h], ho[:, k * h : (k + 1) * h]
                    put(tall_parts, p, at(k * h + j * STRIP), cols, jnp.concatenate([a + b, a - b], 1))

    strips(h // STRIP, columns)
    for p in range(2):
        product_tall[p] = mul_left(tab[1, p], tall_parts[p])
    keys = [chunk_key(o) for o in ORDERS]
    chunk = frame // CHUNKS
    core = lax.axis_index("row")
    first = left_half()

    def results(j):
        x = [[product_tall[p, at(k * h + j * STRIP), :] for k in range(2)] for p in range(2)]
        for lower in range(2):
            rows = at(lower * h + j * STRIP)
            pr, pi = probe[mode, 0, rows, :], probe[mode, 1, rows, :]
            step = [None, None]
            window = [None, None]
            for s in range(slots):
                cols = slice(s * frame, (s + 1) * frame)
                xr, xi = (
                    x[0][k][:, cols] - x[1][k][:, cols] if lower else x[0][k][:, cols] + x[1][k][:, cols]
                    for k in range(2)
                )
                live = (s < counts[0]).astype(f32)
                ar, ai = patches[s][0, rows, :], patches[s][1, rows, :]
                ur = (xr - (pr * ar - pi * ai)) * live
                ui = (xi - (pr * ai + pi * ar)) * live
                for k, g in enumerate((ar * ur + ai * ui, ar * ui - ai * ur)):
                    step[k] = g if s == 0 else step[k] + g
                for k, g in enumerate((pr * ur + pi * ui, pr * ui - pi * ur)):
                    if mode:
                        g = g + before[s, k, rows, :]
                    if not last or tall:
                        grads[s, k, rows, :] = g
                        continue
                    wide = 2 * grads.shape[-1]
                    g = jnp.concatenate([g, jnp.zeros((STRIP, wide - frame), f32)], 1)
                    g = pltpu.roll(g, corner(offsets, s, 1, wide - 2 * h, h), 1)
                    window[k] = g if s == 0 else window[k] + g
            start = lower * h + j * STRIP
            for k in range(2):
                probe_grad[k][(start // chunk) ^ keys[k], at(start % chunk), :] = step[k]
                if last and not tall:
                    half = window[k].shape[1] // 2
                    grads[lower ^ core, first, k, at(j * STRIP), :] = window[k][:, :half]
                    grads[lower ^ core, 1 - first, k, at(j * STRIP), :] = window[k][:, half:]

    strips(h // STRIP, results)


def place_kernel(offsets, grads, out):
    slots, _, frame, _ = grads.shape
    _, _, _, hr, half = out.shape
    cols = 2 * half
    h = frame // 2
    size = cols - 2 * h
    core = lax.axis_index("row")
    first = left_half()
    for c in range(2):
        total = None
        for s in range(slots):
            g = jnp.concatenate([grads[s, c], jnp.zeros((2 * hr - frame, frame), f32)], 0)
            g = pltpu.roll(g, corner(offsets, s, 0, size, h), 0)
            g = jnp.concatenate([g, jnp.zeros((2 * hr, cols - frame), f32)], 1)
            g = pltpu.roll(g, corner(offsets, s, 1, size, h), 1)
            total = g if s == 0 else total + g
        for k in range(2):
            out[k ^ core, first, c] = total[k * hr : (k + 1) * hr, :half]
            out[k ^ core, 1 - first, c] = total[k * hr : (k + 1) * hr, half:]


def finish_kernel(n_pieces, coef, *refs):
    refs = list(refs)
    near, away, probe = refs[:3]
    streams = grouped(refs[3:], 2 * probe.shape[0], n_pieces)
    tile, new_probe = refs[-2:]
    update_probe(probe, streams, coef, new_probe)
    _, _, hr, half = near.shape
    core = lax.axis_index("row")
    first = left_half()
    for ref, part in ((near, core), (away, 1 - core)):
        rows = pl.ds(pl.multiple_of(part * hr, hr), hr)
        tile[:, rows, :half] = ref[first]
        tile[:, rows, half:] = ref[1 - first]


def vmem():
    return pl.BlockSpec(memory_space=pltpu.VMEM)


def call(kernel, outs, args, scratch=(), flops=0):
    size = sum(math.prod(a.shape) * a.dtype.itemsize for a in args)
    size += sum(math.prod(o) * 4 for o in outs)
    return pl.pallas_call(
        kernel,
        out_shape=[jax.ShapeDtypeStruct(o, f32) for o in outs],
        in_specs=[
            pl.BlockSpec(memory_space=pltpu.SMEM) if a.dtype == jnp.int32 else vmem() for a in args
        ],
        out_specs=[vmem() for _ in outs],
        scratch_shapes=list(scratch),
        cost_estimate=pl.CostEstimate(flops=flops, bytes_accessed=size, transcendentals=0),
        compiler_params=pltpu.CompilerParams(vmem_limit_bytes=40 * 1024 * 1024),
    )(*args)


def swap_rows(x):
    return lax.ppermute(x, "row", [(0, 1), (1, 0)])


def beside(x, inner, tiles):
    pairs = []
    for t in range(tiles):
        other = t + 1 if (t % 2 == 0) == inner else t - 1
        if 0 <= other < tiles and other // GX == t // GX:
            pairs.append((t, other))
    return lax.ppermute(x, "tile", pairs)


def swap_vertical(x, tiles):
    pairs = [(2 * t, 2 * (t - GX) + 1) for t in range(GX, tiles)]
    pairs += [(2 * t + 1, 2 * (t + GX)) for t in range(tiles - GX)]
    return lax.ppermute(x, ("tile", "row"), pairs)


def exchange(x, bit, tiles):
    return lax.ppermute(x, "tile", [(s, s ^ (1 << bit)) for s in range(tiles)])


def together(*groups):
    return lax.optimization_barrier(groups)


def halves(x, even, inner):
    half = x.shape[-1] // 2
    own_first = even == inner
    a, b = x[..., :half], x[..., half:]
    return jnp.where(own_first, a, b), jnp.where(own_first, b, a)


def joined(own, other, even, inner):
    own_first = even == inner
    return jnp.concatenate([jnp.where(own_first, own, other), jnp.where(own_first, other, own)], -1)


def window_sum(grad, even, tiles, tall, wide):
    if wide:
        got = [beside(grad[1], False, tiles), beside(grad[0], True, tiles)]
        total = jnp.stack([grad[0] + got[1], grad[1] + got[0]])
        return total + swap_vertical(total, tiles) if tall else total
    own, other = zip(*(halves(grad[k], even, k == 0) for k in range(2)))
    got = [beside(other[1], False, tiles), beside(other[0], True, tiles)]
    return jnp.stack([own[0] + got[1], own[1] + got[0]])


def reduce_all(parts, grad, tiles, window):
    bits = int(math.log2(tiles))
    held = list(parts)
    orders = [ORDERS[i % 2] for i in range(len(parts))]
    near = None
    for i in range(HALVINGS):
        n = held[0].shape[0] // 2
        got = [exchange(h[n:], o[i], tiles) for h, o in zip(held, orders)]
        held = [h[:n] + g for h, g in zip(held, got)]
        if i == 0:
            held[-1], grad = together(held[-1], grad)
            near = window(grad)
    got = [exchange(h, o[-1], tiles) for h, o in zip(held, orders)]
    held = [h + g for h, g in zip(held, got)]
    for bit in range(len(ORDERS[0]), bits):
        held = [h + exchange(h, bit, tiles) for h in held]
    pieces = [[h] for h in held]
    for i in reversed(range(HALVINGS)):
        for p, o in zip(pieces, orders):
            p.append(exchange(p[0] if len(p) == 1 else jnp.concatenate(p, 0), o[i], tiles))
    return pieces, near


def per_device(object_tiles, probe_modes, amplitude, offsets, counts):
    own_tile = object_tiles[0]
    size = own_tile.shape[-1]
    frame = probe_modes.shape[-1]
    half = frame // 2
    tiles = lax.axis_size("tile")
    tall = tiles > GX
    slots = offsets.shape[0]
    modes = probe_modes.shape[0]
    core = lax.axis_index("row")
    even = lax.axis_index("tile") % 2 == 0
    hr = size // 2
    tab = jnp.asarray(tables(frame))
    perm = jnp.asarray(deinterleave(frame))
    coef = 4.0 / (slots * tiles)

    mine = lax.dynamic_slice(own_tile, (0, core * hr, 0), (2, hr, size))
    own = [jnp.where(even == inner, mine[:, :, half:], mine[:, :, :half]) for inner in (True, False)]
    got = [beside(own[1], False, tiles), beside(own[0], True, tiles)]
    near = jnp.stack([joined(own[0], got[1], even, True), joined(own[1], got[0], even, False)])
    if tall:
        other = swap_vertical(near, tiles)
        near = jnp.where(core == 0, jnp.concatenate([other, near], 2), jnp.concatenate([near, other], 2))
    (amp,) = call(amplitude_kernel, [amplitude.shape], [amplitude, perm])
    away = swap_rows(near)
    near, away, amp = together(near, away, amp)

    def scratch(count):
        return [
            pltpu.VMEM((2, 2, frame, count * frame), bf16),
            pltpu.VMEM((2, 2, count * frame, frame), bf16),
        ]

    matmul = 4 * 2 * 3 * 4 * frame**3
    probe = probe_modes
    streams = None
    for iteration in range(ITERS):
        final = iteration + 1 == ITERS
        fars, powers, others, patches = [], [], [], []
        for s in range(slots):
            args = [offsets, near, away, probe, tab]
            outs = [(modes, 2, frame, frame), (frame, frame), (2, frame, frame)]
            count = 0
            if streams is not None:
                count = len(streams[0])
                args += [p for group in streams for p in group]
                outs.append(probe.shape)
                streams = None
            got = call(
                functools.partial(forward_kernel, s, count, coef, tall),
                outs,
                args,
                scratch(modes) + [pltpu.VMEM((2, frame, modes * frame), f32)],
                matmul * modes,
            )
            if count:
                probe = got[3]
            fars.append(got[0])
            powers.append(got[1])
            patches.append(got[2])
            others.append(swap_rows(got[1]))
        before = None
        parts = []
        for m in range(modes):
            last = m == modes - 1
            args = [offsets, counts, tab, amp, probe] + fars + powers + others + patches
            if m:
                args.append(before)
            grads = (2,) + near.shape if last and not tall else (slots, 2, frame, frame)
            part = (CHUNKS, frame // CHUNKS, frame)
            got = call(
                functools.partial(inverse_kernel, m, last, tall),
                [part, part, grads],
                args,
                scratch(slots)
                + [pltpu.VMEM((2, slots * frame, frame), f32), pltpu.VMEM((2, frame, slots * frame), f32)],
                matmul * slots,
            )
            parts += got[:2]
            before = got[2]
        if tall:
            (before,) = call(place_kernel, [(2,) + near.shape], [offsets, before])
        grad = before[0] + swap_rows(before[1])
        wide = tall or not final
        streams, total = reduce_all(parts, grad, tiles, lambda g: window_sum(g, even, tiles, tall, wide))
        if wide:
            near = near + total / MODES
        if final:
            near = jnp.stack([halves(near[k], even, k == 0)[0] for k in range(2)])
            if not wide:
                near = near + total / MODES
            if tall:
                near = jnp.where(core == 0, near[:, :, half:], near[:, :, : size - half])
        away = swap_rows(near)
    args = [near, away, probe] + [p for group in streams for p in group]
    tile, probe = call(
        functools.partial(finish_kernel, len(streams[0]), coef), [own_tile.shape, probe.shape], args
    )
    return (tile[None], probe)


def solution(mesh):
    return jax.shard_map(
        per_device,
        mesh=mesh,
        in_specs=(
            P(("scan", "tile"), None, None, None),
            P("row", None, None, None),
            P(("scan", "tile"), None, None),
            P(("scan", "tile"), None),
            P(("scan", "tile")),
        ),
        out_specs=(P(("scan", "tile"), None, None, None), P(("scan", "row"), None, None, None)),
        check_vma=False,
    )
```

```python
import functools
import math

import jax
import jax.numpy as jnp
import numpy as np
from jax import lax
from jax.experimental import pallas as pl
from jax.experimental.pallas import tpu as pltpu
from jax.sharding import PartitionSpec as P

MODES = 4
GX = 8
ITERS = 2
HALVINGS = 2
CHUNKS = 1 << HALVINGS
STRIP = 16
ORDERS = ((0, 1, 2), (1, 0, 2))

f32 = jnp.float32
bf16 = jnp.bfloat16


def tables(length):
    half = length // 2
    n = np.arange(half)
    out = []
    for odd in (0, 1):
        angle = 2.0 * math.pi * np.outer(2 * n + odd, n) / length
        c, s = np.cos(angle) / math.sqrt(length), np.sin(angle) / math.sqrt(length)
        out.append(np.block([[c, s], [-s, c]]))
    both = np.stack([np.stack(out), np.stack([m.T for m in out])]).astype(np.float32)
    high = both.astype(bf16)
    return np.stack([high, (both - high.astype(np.float32)).astype(bf16)], axis=2)


def deinterleave(length):
    half = length // 2
    out = np.zeros((length, length), np.float32)
    out[2 * np.arange(half), np.arange(half)] = 1.0
    out[2 * np.arange(half) + 1, half + np.arange(half)] = 1.0
    return np.stack([out, out.T]).astype(bf16)


def split(x):
    high = x.astype(bf16)
    return high, (x - high.astype(f32)).astype(bf16)


def dot(a, b):
    return jnp.dot(a, b, preferred_element_type=f32)


def mul_left(table, x):
    return dot(jnp.concatenate([table[0], table[1], table[0]], 1), jnp.concatenate([x[0], x[0], x[1]], 0))


def mul_right(x, table):
    return dot(jnp.concatenate([x[0], x[1], x[0]], 1), jnp.concatenate([table[0], table[0], table[1]], 0))


def put(ref, where, rows, cols, x):
    for k, part in enumerate(split(x)):
        ref[where, k, rows, cols] = part


def strips(count, body):
    for i in range(count):
        body(i)


def at(start, length=STRIP):
    return pl.ds(start if isinstance(start, int) else pl.multiple_of(start, STRIP), length)


def exact(x):
    high = x.astype(bf16)
    rest = x - high.astype(f32)
    mid = rest.astype(bf16)
    return high, mid, (rest - mid.astype(f32)).astype(bf16)


def amplitude_kernel(amp, perm, out):
    for s in range(amp.shape[0]):
        high, mid, low = exact(amp[s])
        rows = dot(perm[1], high) + (dot(perm[1], mid) + dot(perm[1], low))
        high, mid, low = exact(rows)
        out[s] = dot(high, perm[0]) + (dot(mid, perm[0]) + dot(low, perm[0]))


def chunk_key(order):
    t = lax.axis_index("tile")
    return sum(((t >> order[i]) & 1) << (HALVINGS - 1 - i) for i in range(HALVINGS))


def corner(offsets, slot, dim, size, margin):
    t = lax.axis_index("tile")
    along = lax.rem(t, GX) if dim else lax.div(t, GX)
    return offsets[slot, dim] - along * size + margin


def left_half():
    return 1 - lax.rem(lax.axis_index("tile"), 2)


def update_probe(old, streams, coef, out):
    rows = old.shape[2] // CHUNKS
    for mode, pieces in enumerate(streams):
        key = chunk_key(ORDERS[mode])
        rel = 0
        for piece in pieces:
            for k in range(piece.shape[0]):
                here = pl.ds(pl.multiple_of((rel ^ key) * rows, rows), rows)
                out[mode, :, here, :] = old[mode, :, here, :] + coef * piece[k]
                rel += 1


def grouped(refs, streams, per_stream):
    return [refs[i * per_stream : (i + 1) * per_stream] for i in range(streams)]


def shift_in(offsets, slot, near, away, patch, tall):
    frame = patch.shape[-1]
    h = frame // 2
    hr, cols = near.shape[2], 2 * near.shape[3]
    size = cols - 2 * h
    core = lax.axis_index("row")
    first = left_half()
    across = lax.rem(cols - corner(offsets, slot, 1, size, h), cols)

    def strip(ref, c, rows):
        x = jnp.concatenate([ref[first, c, rows, :], ref[1 - first, c, rows, :]], 1)
        return pltpu.roll(x, across, 1)[:, :frame]

    if tall:
        down = lax.rem(2 * hr - corner(offsets, slot, 0, size, h), 2 * hr)
        for c in range(2):
            halves = [strip(ref, c, slice(None)) for ref in (near, away)]
            both = [jnp.where(core == k, halves[0], halves[1]) for k in range(2)]
            patch[c] = pltpu.roll(jnp.concatenate(both, 0), down, 0)[:frame]
        return

    def body(j):
        for ref, half in ((near, core), (away, 1 - core)):
            for c in range(2):
                patch[c, at(half * hr + j * STRIP), :] = strip(ref, c, at(j * STRIP))

    strips(hr // STRIP, body)


def forward_kernel(slot, n_pieces, coef, tall, *refs):
    refs = list(refs)
    offsets, near, away, probe, tab = refs[:5]
    refs = refs[5:]
    modes = probe.shape[0]
    if n_pieces:
        streams = grouped(refs, modes, n_pieces)
        refs = refs[modes * n_pieces :]
        new_probe = refs.pop(3)
        update_probe(probe, streams, coef, new_probe)
        probe = new_probe
    far, power, patch, tall_parts, wide_parts, product = refs
    frame = probe.shape[-1]
    h = frame // 2
    shift_in(offsets, slot, near, away, patch, tall)

    def exits(j):
        for m in range(modes):
            pair = []
            for start in (j * STRIP, h + j * STRIP):
                rows = at(start)
                pr, pi = probe[m, 0, rows, :], probe[m, 1, rows, :]
                ar, ai = patch[0, rows, :], patch[1, rows, :]
                pair.append((pr * ar - pi * ai, pr * ai + pi * ar))
            cols = slice(m * frame, (m + 1) * frame)
            for k in range(2):
                put(tall_parts, 0, at(k * h + j * STRIP), cols, pair[0][k] + pair[1][k])
                put(tall_parts, 1, at(k * h + j * STRIP), cols, pair[0][k] - pair[1][k])

    strips(h // STRIP, exits)
    for p in range(2):
        product[p] = mul_left(tab[0, p], tall_parts[p])

    def columns(j):
        for p in range(2):
            for m in range(modes):
                cols = slice(m * frame, (m + 1) * frame)
                y = [product[p, at(k * h + j * STRIP), cols] for k in range(2)]
                rows = at(m * frame + p * h + j * STRIP)
                put(wide_parts, 0, rows, slice(None), jnp.concatenate([v[:, :h] + v[:, h:] for v in y], 1))
                put(wide_parts, 1, rows, slice(None), jnp.concatenate([v[:, :h] - v[:, h:] for v in y], 1))

    strips(h // STRIP, columns)
    for q in range(2):
        out = mul_right(wide_parts[q], tab[1, q])
        for m in range(modes):
            far[m, q] = out[m * frame : (m + 1) * frame]

    def powers(j):
        rows = at(j * STRIP)
        for q in range(2):
            total = None
            for m in range(modes):
                f = far[m, q, rows, :]
                f = f * f
                f = f[:, :h] + f[:, h:]
                total = f if m == 0 else total + f
            power[rows, slice(q * h, (q + 1) * h)] = total

    strips(frame // STRIP, powers)


def inverse_kernel(mode, last, tall, *refs):
    refs = list(refs)
    offsets, counts, tab, amp, probe = refs[:5]
    refs = refs[5:]
    slots = amp.shape[0]
    fars, powers, others, patches = (refs[i * slots : (i + 1) * slots] for i in range(4))
    refs = refs[4 * slots :]
    before = refs.pop(0) if mode else None
    probe_grad, grads, tall_parts, wide_parts, product_wide, product_tall = refs
    frame = probe.shape[-1]
    h = frame // 2

    def factors(j):
        rows = at(j * STRIP)
        for s in range(slots):
            factor = amp[s, rows, :] / (jnp.sqrt(powers[s][rows, :] + others[s][rows, :]) + 0.5)
            for q in range(2):
                f = factor[:, q * h : (q + 1) * h]
                put(
                    wide_parts,
                    q,
                    at(s * frame + j * STRIP),
                    slice(None),
                    fars[s][mode, q, rows, :] * jnp.concatenate([f, f], 1),
                )

    strips(frame // STRIP, factors)
    for q in range(2):
        product_wide[q] = mul_right(wide_parts[q], tab[0, q])

    def columns(j):
        for p in range(2):
            for s in range(slots):
                rows = at(s * frame + p * h + j * STRIP)
                he, ho = product_wide[0, rows, :], product_wide[1, rows, :]
                cols = slice(s * frame, (s + 1) * frame)
                for k in range(2):
                    a, b = he[:, k * h : (k + 1) * h], ho[:, k * h : (k + 1) * h]
                    put(tall_parts, p, at(k * h + j * STRIP), cols, jnp.concatenate([a + b, a - b], 1))

    strips(h // STRIP, columns)
    for p in range(2):
        product_tall[p] = mul_left(tab[1, p], tall_parts[p])
    key = chunk_key(ORDERS[mode])
    chunk = frame // CHUNKS
    core = lax.axis_index("row")
    first = left_half()

    def results(j):
        x = [[product_tall[p, at(k * h + j * STRIP), :] for k in range(2)] for p in range(2)]
        for lower in range(2):
            rows = at(lower * h + j * STRIP)
            pr, pi = probe[mode, 0, rows, :], probe[mode, 1, rows, :]
            step = [None, None]
            window = [None, None]
            for s in range(slots):
                cols = slice(s * frame, (s + 1) * frame)
                xr, xi = (
                    x[0][k][:, cols] - x[1][k][:, cols] if lower else x[0][k][:, cols] + x[1][k][:, cols]
                    for k in range(2)
                )
                live = (s < counts[0]).astype(f32)
                ar, ai = patches[s][0, rows, :], patches[s][1, rows, :]
                ur = (xr - (pr * ar - pi * ai)) * live
                ui = (xi - (pr * ai + pi * ar)) * live
                for k, g in enumerate((ar * ur + ai * ui, ar * ui - ai * ur)):
                    step[k] = g if s == 0 else step[k] + g
                for k, g in enumerate((pr * ur + pi * ui, pr * ui - pi * ur)):
                    if mode:
                        g = g + before[s, k, rows, :]
                    if not last or tall:
                        grads[s, k, rows, :] = g
                        continue
                    wide = 2 * grads.shape[-1]
                    g = jnp.concatenate([g, jnp.zeros((STRIP, wide - frame), f32)], 1)
                    g = pltpu.roll(g, corner(offsets, s, 1, wide - 2 * h, h), 1)
                    window[k] = g if s == 0 else window[k] + g
            start = lower * h + j * STRIP
            for k in range(2):
                probe_grad[(start // chunk) ^ key, k, at(start % chunk), :] = step[k]
                if last and not tall:
                    half = window[k].shape[1] // 2
                    grads[lower ^ core, first, k, at(j * STRIP), :] = window[k][:, :half]
                    grads[lower ^ core, 1 - first, k, at(j * STRIP), :] = window[k][:, half:]

    strips(h // STRIP, results)


def place_kernel(offsets, grads, out):
    slots, _, frame, _ = grads.shape
    _, _, _, hr, half = out.shape
    cols = 2 * half
    h = frame // 2
    size = cols - 2 * h
    core = lax.axis_index("row")
    first = left_half()
    for c in range(2):
        total = None
        for s in range(slots):
            g = jnp.concatenate([grads[s, c], jnp.zeros((2 * hr - frame, frame), f32)], 0)
            g = pltpu.roll(g, corner(offsets, s, 0, size, h), 0)
            g = jnp.concatenate([g, jnp.zeros((2 * hr, cols - frame), f32)], 1)
            g = pltpu.roll(g, corner(offsets, s, 1, size, h), 1)
            total = g if s == 0 else total + g
        for k in range(2):
            out[k ^ core, first, c] = total[k * hr : (k + 1) * hr, :half]
            out[k ^ core, 1 - first, c] = total[k * hr : (k + 1) * hr, half:]


def finish_kernel(n_pieces, coef, *refs):
    refs = list(refs)
    near, away, probe = refs[:3]
    streams = grouped(refs[3:], probe.shape[0], n_pieces)
    tile, new_probe = refs[-2:]
    update_probe(probe, streams, coef, new_probe)
    _, _, hr, half = near.shape
    core = lax.axis_index("row")
    first = left_half()
    for ref, part in ((near, core), (away, 1 - core)):
        rows = pl.ds(pl.multiple_of(part * hr, hr), hr)
        tile[:, rows, :half] = ref[first]
        tile[:, rows, half:] = ref[1 - first]


def vmem():
    return pl.BlockSpec(memory_space=pltpu.VMEM)


def call(kernel, outs, args, scratch=(), flops=0):
    size = sum(math.prod(a.shape) * a.dtype.itemsize for a in args)
    size += sum(math.prod(o) * 4 for o in outs)
    return pl.pallas_call(
        kernel,
        out_shape=[jax.ShapeDtypeStruct(o, f32) for o in outs],
        in_specs=[
            pl.BlockSpec(memory_space=pltpu.SMEM) if a.dtype == jnp.int32 else vmem() for a in args
        ],
        out_specs=[vmem() for _ in outs],
        scratch_shapes=list(scratch),
        cost_estimate=pl.CostEstimate(flops=flops, bytes_accessed=size, transcendentals=0),
        compiler_params=pltpu.CompilerParams(vmem_limit_bytes=40 * 1024 * 1024),
    )(*args)


def swap_rows(x):
    return lax.ppermute(x, "row", [(0, 1), (1, 0)])


def beside(x, inner, tiles):
    pairs = []
    for t in range(tiles):
        other = t + 1 if (t % 2 == 0) == inner else t - 1
        if 0 <= other < tiles and other // GX == t // GX:
            pairs.append((t, other))
    return lax.ppermute(x, "tile", pairs)


def swap_vertical(x, tiles):
    pairs = [(2 * t, 2 * (t - GX) + 1) for t in range(GX, tiles)]
    pairs += [(2 * t + 1, 2 * (t + GX)) for t in range(tiles - GX)]
    return lax.ppermute(x, ("tile", "row"), pairs)


def exchange(x, bit, tiles):
    return lax.ppermute(x, "tile", [(s, s ^ (1 << bit)) for s in range(tiles)])


def together(*groups):
    return lax.optimization_barrier(groups)


def halves(x, even, inner):
    half = x.shape[-1] // 2
    own_first = even == inner
    a, b = x[..., :half], x[..., half:]
    return jnp.where(own_first, a, b), jnp.where(own_first, b, a)


def joined(own, other, even, inner):
    own_first = even == inner
    return jnp.concatenate([jnp.where(own_first, own, other), jnp.where(own_first, other, own)], -1)


def window_parts(grad, even, wide):
    if wide:
        return [grad[0], grad[1]], [grad[0], grad[1]]
    return zip(*(halves(grad[k], even, k == 0) for k in range(2)))


def reduce_all(parts, grad, even, tiles, wide):
    bits = int(math.log2(tiles))
    held = list(parts)
    stay, go = window_parts(grad, even, wide)
    go = list(go)
    got = [None, None]
    for i in range(HALVINGS):
        n = held[0].shape[0] // 2
        held = [h[:n] + exchange(h[n:], o[i], tiles) for h, o in zip(held, ORDERS)]
        held[-1], go[1 - i] = together(held[-1], go[1 - i])
        got[1 - i] = beside(go[1 - i], i == 1, tiles)
    total = jnp.stack([stay[0] + got[0], stay[1] + got[1]])
    held = [h + exchange(h, o[-1], tiles) for h, o in zip(held, ORDERS)]
    for bit in range(len(ORDERS[0]), bits):
        held = [h + exchange(h, bit, tiles) for h in held]
    pieces = [[h] for h in held]
    for i in reversed(range(HALVINGS)):
        for p, o in zip(pieces, ORDERS):
            p.append(exchange(p[0] if len(p) == 1 else jnp.concatenate(p, 0), o[i], tiles))
    return pieces, total


def per_device(object_tiles, probe_modes, amplitude, offsets, counts):
    own_tile = object_tiles[0]
    size = own_tile.shape[-1]
    frame = probe_modes.shape[-1]
    half = frame // 2
    tiles = lax.axis_size("tile")
    tall = tiles > GX
    slots = offsets.shape[0]
    modes = probe_modes.shape[0]
    core = lax.axis_index("row")
    even = lax.axis_index("tile") % 2 == 0
    hr = size // 2
    tab = jnp.asarray(tables(frame))
    perm = jnp.asarray(deinterleave(frame))
    coef = 4.0 / (slots * tiles)

    mine = lax.dynamic_slice(own_tile, (0, core * hr, 0), (2, hr, size))
    own = [jnp.where(even == inner, mine[:, :, half:], mine[:, :, :half]) for inner in (True, False)]
    got = [beside(own[1], False, tiles), beside(own[0], True, tiles)]
    near = jnp.stack([joined(own[0], got[1], even, True), joined(own[1], got[0], even, False)])
    if tall:
        other = swap_vertical(near, tiles)
        near = jnp.where(core == 0, jnp.concatenate([other, near], 2), jnp.concatenate([near, other], 2))
    (amp,) = call(amplitude_kernel, [amplitude.shape], [amplitude, perm])
    away = swap_rows(near)
    near, away, amp = together(near, away, amp)

    def scratch(count):
        return [
            pltpu.VMEM((2, 2, frame, count * frame), bf16),
            pltpu.VMEM((2, 2, count * frame, frame), bf16),
        ]

    matmul = 4 * 2 * 3 * 4 * frame**3
    probe = probe_modes
    streams = None
    for iteration in range(ITERS):
        final = iteration + 1 == ITERS
        fars, powers, others, patches = [], [], [], []
        for s in range(slots):
            args = [offsets, near, away, probe, tab]
            outs = [(modes, 2, frame, frame), (frame, frame), (2, frame, frame)]
            count = 0
            if streams is not None:
                count = len(streams[0])
                args += [p for group in streams for p in group]
                outs.append(probe.shape)
                streams = None
            got = call(
                functools.partial(forward_kernel, s, count, coef, tall),
                outs,
                args,
                scratch(modes) + [pltpu.VMEM((2, frame, modes * frame), f32)],
                matmul * modes,
            )
            if count:
                probe = got[3]
            fars.append(got[0])
            powers.append(got[1])
            patches.append(got[2])
            others.append(swap_rows(got[1]))
        before = None
        parts = []
        for m in range(modes):
            last = m == modes - 1
            args = [offsets, counts, tab, amp, probe] + fars + powers + others + patches
            if m:
                args.append(before)
            grads = (2,) + near.shape if last and not tall else (slots, 2, frame, frame)
            part = (CHUNKS, 2, frame // CHUNKS, frame)
            got = call(
                functools.partial(inverse_kernel, m, last, tall),
                [part, grads],
                args,
                scratch(slots)
                + [pltpu.VMEM((2, slots * frame, frame), f32), pltpu.VMEM((2, frame, slots * frame), f32)],
                matmul * slots,
            )
            parts.append(got[0])
            before = got[1]
        if tall:
            (before,) = call(place_kernel, [(2,) + near.shape], [offsets, before])
        grad = before[0] + swap_rows(before[1])
        wide = tall or not final
        streams, total = reduce_all(parts, grad, even, tiles, wide)
        if tall:
            total = total + swap_vertical(total, tiles)
        if wide:
            near = near + total / MODES
        if final:
            near = jnp.stack([halves(near[k], even, k == 0)[0] for k in range(2)])
            if not wide:
                near = near + total / MODES
            if tall:
                near = jnp.where(core == 0, near[:, :, half:], near[:, :, : size - half])
        away = swap_rows(near)
    args = [near, away, probe] + [p for group in streams for p in group]
    tile, probe = call(
        functools.partial(finish_kernel, len(streams[0]), coef), [own_tile.shape, probe.shape], args
    )
    return (tile[None], probe)


def solution(mesh):
    return jax.shard_map(
        per_device,
        mesh=mesh,
        in_specs=(
            P(("scan", "tile"), None, None, None),
            P("row", None, None, None),
            P(("scan", "tile"), None, None),
            P(("scan", "tile"), None),
            P(("scan", "tile")),
        ),
        out_specs=(P(("scan", "tile"), None, None, None), P(("scan", "row"), None, None, None)),
        check_vma=False,
    )
```

```python
import functools
import math

import jax
import jax.numpy as jnp
import numpy as np
from jax import lax
from jax.experimental import pallas as pl
from jax.experimental.pallas import tpu as pltpu
from jax.sharding import PartitionSpec as P

MODES = 4
GX = 8
ITERS = 2
BLOCK_BITS = 2
CHUNKS = 1 << BLOCK_BITS
STRIP = 16
ORDERS = ((0, 1, 2), (1, 0, 2))

f32 = jnp.float32
bf16 = jnp.bfloat16


def tables(length):
    half = length // 2
    n = np.arange(half)
    out = []
    for odd in (0, 1):
        angle = 2.0 * math.pi * np.outer(2 * n + odd, n) / length
        c, s = np.cos(angle) / math.sqrt(length), np.sin(angle) / math.sqrt(length)
        out.append(np.block([[c, s], [-s, c]]))
    both = np.stack([np.stack(out), np.stack([m.T for m in out])]).astype(np.float32)
    high = both.astype(bf16)
    return np.stack([high, (both - high.astype(np.float32)).astype(bf16)], axis=2)


def deinterleave(length):
    half = length // 2
    out = np.zeros((length, length), np.float32)
    out[2 * np.arange(half), np.arange(half)] = 1.0
    out[2 * np.arange(half) + 1, half + np.arange(half)] = 1.0
    return np.stack([out, out.T]).astype(bf16)


def split(x):
    high = x.astype(bf16)
    return high, (x - high.astype(f32)).astype(bf16)


def dot(a, b):
    return jnp.dot(a, b, preferred_element_type=f32)


def mul_left(table, x):
    return dot(jnp.concatenate([table[0], table[1], table[0]], 1), jnp.concatenate([x[0], x[0], x[1]], 0))


def mul_right(x, table):
    return dot(jnp.concatenate([x[0], x[1], x[0]], 1), jnp.concatenate([table[0], table[0], table[1]], 0))


def put(ref, where, rows, cols, x):
    for k, part in enumerate(split(x)):
        ref[where, k, rows, cols] = part


def strips(count, body):
    for i in range(count):
        body(i)


def at(start, length=STRIP):
    return pl.ds(start if isinstance(start, int) else pl.multiple_of(start, STRIP), length)


def exact(x):
    high = x.astype(bf16)
    rest = x - high.astype(f32)
    mid = rest.astype(bf16)
    return high, mid, (rest - mid.astype(f32)).astype(bf16)


def amplitude_kernel(amp, perm, out):
    for s in range(amp.shape[0]):
        high, mid, low = exact(amp[s])
        rows = dot(perm[1], high) + (dot(perm[1], mid) + dot(perm[1], low))
        high, mid, low = exact(rows)
        out[s] = dot(high, perm[0]) + (dot(mid, perm[0]) + dot(low, perm[0]))


def chunk_key():
    return lax.rem(lax.axis_index("tile"), CHUNKS)


def corner(offsets, slot, dim, size, margin):
    t = lax.axis_index("tile")
    along = lax.rem(t, GX) if dim else lax.div(t, GX)
    return offsets[slot, dim] - along * size + margin


def left_half():
    return 1 - lax.rem(lax.axis_index("tile"), 2)


def update_probe(old, streams, coef, out):
    rows = old.shape[2] // CHUNKS
    key = chunk_key()
    for mode, pieces in enumerate(streams):
        rel = 0
        for piece in pieces:
            for k in range(piece.shape[0]):
                here = pl.ds(pl.multiple_of((rel ^ key) * rows, rows), rows)
                out[mode, :, here, :] = old[mode, :, here, :] + coef * piece[k]
                rel += 1


def grouped(refs, streams, per_stream):
    return [refs[i * per_stream : (i + 1) * per_stream] for i in range(streams)]


def shift_in(offsets, slot, near, away, patch, tall):
    frame = patch.shape[-1]
    h = frame // 2
    hr, cols = near.shape[2], 2 * near.shape[3]
    size = cols - 2 * h
    core = lax.axis_index("row")
    first = left_half()
    across = lax.rem(cols - corner(offsets, slot, 1, size, h), cols)

    def strip(ref, c, rows):
        x = jnp.concatenate([ref[first, c, rows, :], ref[1 - first, c, rows, :]], 1)
        return pltpu.roll(x, across, 1)[:, :frame]

    if tall:
        down = lax.rem(2 * hr - corner(offsets, slot, 0, size, h), 2 * hr)
        for c in range(2):
            halves = [strip(ref, c, slice(None)) for ref in (near, away)]
            both = [jnp.where(core == k, halves[0], halves[1]) for k in range(2)]
            patch[c] = pltpu.roll(jnp.concatenate(both, 0), down, 0)[:frame]
        return

    def body(j):
        for ref, half in ((near, core), (away, 1 - core)):
            for c in range(2):
                patch[c, at(half * hr + j * STRIP), :] = strip(ref, c, at(j * STRIP))

    strips(hr // STRIP, body)


def forward_kernel(slot, n_pieces, coef, tall, *refs):
    refs = list(refs)
    offsets, near, away, probe, tab = refs[:5]
    refs = refs[5:]
    modes = probe.shape[0]
    if n_pieces:
        streams = grouped(refs, modes, n_pieces)
        refs = refs[modes * n_pieces :]
        new_probe = refs.pop(3)
        update_probe(probe, streams, coef, new_probe)
        probe = new_probe
    far, power, patch, tall_parts, wide_parts, product = refs
    frame = probe.shape[-1]
    h = frame // 2
    shift_in(offsets, slot, near, away, patch, tall)

    def exits(j):
        for m in range(modes):
            pair = []
            for start in (j * STRIP, h + j * STRIP):
                rows = at(start)
                pr, pi = probe[m, 0, rows, :], probe[m, 1, rows, :]
                ar, ai = patch[0, rows, :], patch[1, rows, :]
                pair.append((pr * ar - pi * ai, pr * ai + pi * ar))
            cols = slice(m * frame, (m + 1) * frame)
            for k in range(2):
                put(tall_parts, 0, at(k * h + j * STRIP), cols, pair[0][k] + pair[1][k])
                put(tall_parts, 1, at(k * h + j * STRIP), cols, pair[0][k] - pair[1][k])

    strips(h // STRIP, exits)
    for p in range(2):
        product[p] = mul_left(tab[0, p], tall_parts[p])

    def columns(j):
        for p in range(2):
            for m in range(modes):
                cols = slice(m * frame, (m + 1) * frame)
                y = [product[p, at(k * h + j * STRIP), cols] for k in range(2)]
                rows = at(m * frame + p * h + j * STRIP)
                put(wide_parts, 0, rows, slice(None), jnp.concatenate([v[:, :h] + v[:, h:] for v in y], 1))
                put(wide_parts, 1, rows, slice(None), jnp.concatenate([v[:, :h] - v[:, h:] for v in y], 1))

    strips(h // STRIP, columns)
    for q in range(2):
        out = mul_right(wide_parts[q], tab[1, q])
        for m in range(modes):
            far[m, q] = out[m * frame : (m + 1) * frame]

    def powers(j):
        rows = at(j * STRIP)
        for q in range(2):
            total = None
            for m in range(modes):
                f = far[m, q, rows, :]
                f = f * f
                f = f[:, :h] + f[:, h:]
                total = f if m == 0 else total + f
            power[rows, slice(q * h, (q + 1) * h)] = total

    strips(frame // STRIP, powers)


def inverse_kernel(mode, last, tall, *refs):
    refs = list(refs)
    offsets, counts, tab, amp, probe = refs[:5]
    refs = refs[5:]
    slots = amp.shape[0]
    fars, powers, others, patches = (refs[i * slots : (i + 1) * slots] for i in range(4))
    refs = refs[4 * slots :]
    before = refs.pop(0) if mode else None
    probe_grad, grads, tall_parts, wide_parts, product_wide, product_tall = refs
    frame = probe.shape[-1]
    h = frame // 2

    def factors(j):
        rows = at(j * STRIP)
        for s in range(slots):
            factor = amp[s, rows, :] / (jnp.sqrt(powers[s][rows, :] + others[s][rows, :]) + 0.5)
            for q in range(2):
                f = factor[:, q * h : (q + 1) * h]
                put(
                    wide_parts,
                    q,
                    at(s * frame + j * STRIP),
                    slice(None),
                    fars[s][mode, q, rows, :] * jnp.concatenate([f, f], 1),
                )

    strips(frame // STRIP, factors)
    for q in range(2):
        product_wide[q] = mul_right(wide_parts[q], tab[0, q])

    def columns(j):
        for p in range(2):
            for s in range(slots):
                rows = at(s * frame + p * h + j * STRIP)
                he, ho = product_wide[0, rows, :], product_wide[1, rows, :]
                cols = slice(s * frame, (s + 1) * frame)
                for k in range(2):
                    a, b = he[:, k * h : (k + 1) * h], ho[:, k * h : (k + 1) * h]
                    put(tall_parts, p, at(k * h + j * STRIP), cols, jnp.concatenate([a + b, a - b], 1))

    strips(h // STRIP, columns)
    for p in range(2):
        product_tall[p] = mul_left(tab[1, p], tall_parts[p])
    key = chunk_key()
    chunk = frame // CHUNKS
    core = lax.axis_index("row")
    first = left_half()

    def results(j):
        x = [[product_tall[p, at(k * h + j * STRIP), :] for k in range(2)] for p in range(2)]
        for lower in range(2):
            rows = at(lower * h + j * STRIP)
            pr, pi = probe[mode, 0, rows, :], probe[mode, 1, rows, :]
            step = [None, None]
            window = [None, None]
            for s in range(slots):
                cols = slice(s * frame, (s + 1) * frame)
                xr, xi = (
                    x[0][k][:, cols] - x[1][k][:, cols] if lower else x[0][k][:, cols] + x[1][k][:, cols]
                    for k in range(2)
                )
                live = (s < counts[0]).astype(f32)
                ar, ai = patches[s][0, rows, :], patches[s][1, rows, :]
                ur = (xr - (pr * ar - pi * ai)) * live
                ui = (xi - (pr * ai + pi * ar)) * live
                for k, g in enumerate((ar * ur + ai * ui, ar * ui - ai * ur)):
                    step[k] = g if s == 0 else step[k] + g
                for k, g in enumerate((pr * ur + pi * ui, pr * ui - pi * ur)):
                    if mode:
                        g = g + before[s, k, rows, :]
                    if not last or tall:
                        grads[s, k, rows, :] = g
                        continue
                    wide = 2 * grads.shape[-1]
                    g = jnp.concatenate([g, jnp.zeros((STRIP, wide - frame), f32)], 1)
                    g = pltpu.roll(g, corner(offsets, s, 1, wide - 2 * h, h), 1)
                    window[k] = g if s == 0 else window[k] + g
            start = lower * h + j * STRIP
            for k in range(2):
                probe_grad[(start // chunk) ^ key, k, at(start % chunk), :] = step[k]
                if last and not tall:
                    half = window[k].shape[1] // 2
                    grads[lower ^ core, first, k, at(j * STRIP), :] = window[k][:, :half]
                    grads[lower ^ core, 1 - first, k, at(j * STRIP), :] = window[k][:, half:]

    strips(h // STRIP, results)


def place_kernel(offsets, grads, out):
    slots, _, frame, _ = grads.shape
    _, _, _, hr, half = out.shape
    cols = 2 * half
    h = frame // 2
    size = cols - 2 * h
    core = lax.axis_index("row")
    first = left_half()
    for c in range(2):
        total = None
        for s in range(slots):
            g = jnp.concatenate([grads[s, c], jnp.zeros((2 * hr - frame, frame), f32)], 0)
            g = pltpu.roll(g, corner(offsets, s, 0, size, h), 0)
            g = jnp.concatenate([g, jnp.zeros((2 * hr, cols - frame), f32)], 1)
            g = pltpu.roll(g, corner(offsets, s, 1, size, h), 1)
            total = g if s == 0 else total + g
        for k in range(2):
            out[k ^ core, first, c] = total[k * hr : (k + 1) * hr, :half]
            out[k ^ core, 1 - first, c] = total[k * hr : (k + 1) * hr, half:]


def finish_kernel(n_pieces, coef, *refs):
    refs = list(refs)
    near, away, probe = refs[:3]
    streams = grouped(refs[3:], probe.shape[0], n_pieces)
    tile, new_probe = refs[-2:]
    update_probe(probe, streams, coef, new_probe)
    _, _, hr, half = near.shape
    core = lax.axis_index("row")
    first = left_half()
    for ref, part in ((near, core), (away, 1 - core)):
        rows = pl.ds(pl.multiple_of(part * hr, hr), hr)
        tile[:, rows, :half] = ref[first]
        tile[:, rows, half:] = ref[1 - first]


def vmem():
    return pl.BlockSpec(memory_space=pltpu.VMEM)


def call(kernel, outs, args, scratch=(), flops=0):
    size = sum(math.prod(a.shape) * a.dtype.itemsize for a in args)
    size += sum(math.prod(o) * 4 for o in outs)
    return pl.pallas_call(
        kernel,
        out_shape=[jax.ShapeDtypeStruct(o, f32) for o in outs],
        in_specs=[
            pl.BlockSpec(memory_space=pltpu.SMEM) if a.dtype == jnp.int32 else vmem() for a in args
        ],
        out_specs=[vmem() for _ in outs],
        scratch_shapes=list(scratch),
        cost_estimate=pl.CostEstimate(flops=flops, bytes_accessed=size, transcendentals=0),
        compiler_params=pltpu.CompilerParams(vmem_limit_bytes=40 * 1024 * 1024),
    )(*args)


def swap_rows(x):
    return lax.ppermute(x, "row", [(0, 1), (1, 0)])


def beside(x, inner, tiles):
    pairs = []
    for t in range(tiles):
        other = t + 1 if (t % 2 == 0) == inner else t - 1
        if 0 <= other < tiles and other // GX == t // GX:
            pairs.append((t, other))
    return lax.ppermute(x, "tile", pairs)


def swap_vertical(x, tiles):
    pairs = [(2 * t, 2 * (t - GX) + 1) for t in range(GX, tiles)]
    pairs += [(2 * t + 1, 2 * (t + GX)) for t in range(tiles - GX)]
    return lax.ppermute(x, ("tile", "row"), pairs)


def exchange(x, mask, tiles):
    return lax.ppermute(x, "tile", [(s, s ^ mask) for s in range(tiles)])


def together(*groups):
    return lax.optimization_barrier(groups)


def halves(x, even, inner):
    half = x.shape[-1] // 2
    own_first = even == inner
    a, b = x[..., :half], x[..., half:]
    return jnp.where(own_first, a, b), jnp.where(own_first, b, a)


def joined(own, other, even, inner):
    own_first = even == inner
    return jnp.concatenate([jnp.where(own_first, own, other), jnp.where(own_first, other, own)], -1)


def window_parts(grad, even, wide):
    if wide:
        return [grad[0], grad[1]], [grad[0], grad[1]]
    return zip(*(halves(grad[k], even, k == 0) for k in range(2)))


def reduce_all(parts, grad, even, tiles, wide):
    stay, go = window_parts(grad, even, wide)
    got = [[p[:1]] + [exchange(p[k : k + 1], k, tiles) for k in range(1, CHUNKS)] for p in parts]
    streams = []
    for m in range(len(parts)):
        held = sum(got[m][1:], got[m][0])
        if m == 0:
            held, go = together(held, tuple(go))
            outer = beside(go[1], False, tiles)
            inner = beside(go[0], True, tiles)
        mask = CHUNKS
        while mask < tiles:
            held = held + exchange(held, mask, tiles)
            mask *= 2
        if m + 1 < len(parts):
            held, got[m + 1] = together(held, got[m + 1])
        streams.append([held] + [exchange(held, k, tiles) for k in range(1, CHUNKS)])
    return streams, jnp.stack([stay[0] + inner, stay[1] + outer])


def per_device(object_tiles, probe_modes, amplitude, offsets, counts):
    own_tile = object_tiles[0]
    size = own_tile.shape[-1]
    frame = probe_modes.shape[-1]
    half = frame // 2
    tiles = lax.axis_size("tile")
    tall = tiles > GX
    slots = offsets.shape[0]
    modes = probe_modes.shape[0]
    core = lax.axis_index("row")
    even = lax.axis_index("tile") % 2 == 0
    hr = size // 2
    tab = jnp.asarray(tables(frame))
    perm = jnp.asarray(deinterleave(frame))
    coef = 4.0 / (slots * tiles)

    mine = lax.dynamic_slice(own_tile, (0, core * hr, 0), (2, hr, size))
    own = [jnp.where(even == inner, mine[:, :, half:], mine[:, :, :half]) for inner in (True, False)]
    got = [beside(own[1], False, tiles), beside(own[0], True, tiles)]
    near = jnp.stack([joined(own[0], got[1], even, True), joined(own[1], got[0], even, False)])
    if tall:
        other = swap_vertical(near, tiles)
        near = jnp.where(core == 0, jnp.concatenate([other, near], 2), jnp.concatenate([near, other], 2))
    (amp,) = call(amplitude_kernel, [amplitude.shape], [amplitude, perm])
    away = swap_rows(near)
    near, away, amp = together(near, away, amp)

    def scratch(count):
        return [
            pltpu.VMEM((2, 2, frame, count * frame), bf16),
            pltpu.VMEM((2, 2, count * frame, frame), bf16),
        ]

    matmul = 4 * 2 * 3 * 4 * frame**3
    probe = probe_modes
    streams = None
    for iteration in range(ITERS):
        final = iteration + 1 == ITERS
        fars, powers, others, patches = [], [], [], []
        for s in range(slots):
            args = [offsets, near, away, probe, tab]
            outs = [(modes, 2, frame, frame), (frame, frame), (2, frame, frame)]
            count = 0
            if streams is not None:
                count = len(streams[0])
                args += [p for group in streams for p in group]
                outs.append(probe.shape)
                streams = None
            got = call(
                functools.partial(forward_kernel, s, count, coef, tall),
                outs,
                args,
                scratch(modes) + [pltpu.VMEM((2, frame, modes * frame), f32)],
                matmul * modes,
            )
            if count:
                probe = got[3]
            fars.append(got[0])
            powers.append(got[1])
            patches.append(got[2])
            others.append(swap_rows(got[1]))
        before = None
        parts = []
        for m in range(modes):
            last = m == modes - 1
            args = [offsets, counts, tab, amp, probe] + fars + powers + others + patches
            if m:
                args.append(before)
            grads = (2,) + near.shape if last and not tall else (slots, 2, frame, frame)
            part = (CHUNKS, 2, frame // CHUNKS, frame)
            got = call(
                functools.partial(inverse_kernel, m, last, tall),
                [part, grads],
                args,
                scratch(slots)
                + [pltpu.VMEM((2, slots * frame, frame), f32), pltpu.VMEM((2, frame, slots * frame), f32)],
                matmul * slots,
            )
            parts.append(got[0])
            before = got[1]
        if tall:
            (before,) = call(place_kernel, [(2,) + near.shape], [offsets, before])
        grad = before[0] + swap_rows(before[1])
        wide = tall or not final
        streams, total = reduce_all(parts, grad, even, tiles, wide)
        if tall:
            total = total + swap_vertical(total, tiles)
        if wide:
            near = near + total / MODES
        if final:
            near = jnp.stack([halves(near[k], even, k == 0)[0] for k in range(2)])
            if not wide:
                near = near + total / MODES
            if tall:
                near = jnp.where(core == 0, near[:, :, half:], near[:, :, : size - half])
        away = swap_rows(near)
    args = [near, away, probe] + [p for group in streams for p in group]
    tile, probe = call(
        functools.partial(finish_kernel, len(streams[0]), coef), [own_tile.shape, probe.shape], args
    )
    return (tile[None], probe)


def solution(mesh):
    return jax.shard_map(
        per_device,
        mesh=mesh,
        in_specs=(
            P(("scan", "tile"), None, None, None),
            P("row", None, None, None),
            P(("scan", "tile"), None, None),
            P(("scan", "tile"), None),
            P(("scan", "tile")),
        ),
        out_specs=(P(("scan", "tile"), None, None, None), P(("scan", "row"), None, None, None)),
        check_vma=False,
    )
```

```python
import functools
import math

import jax
import jax.numpy as jnp
import numpy as np
from jax import lax
from jax.experimental import pallas as pl
from jax.experimental.pallas import tpu as pltpu
from jax.sharding import PartitionSpec as P

MODES = 4
GX = 8
ITERS = 2
BLOCK_BITS = 2
CHUNKS = 1 << BLOCK_BITS
STRIP = 16
ORDERS = ((0, 1, 2), (1, 0, 2))

f32 = jnp.float32
bf16 = jnp.bfloat16


def tables(length):
    half = length // 2
    n = np.arange(half)
    out = []
    for odd in (0, 1):
        angle = 2.0 * math.pi * np.outer(2 * n + odd, n) / length
        c, s = np.cos(angle) / math.sqrt(length), np.sin(angle) / math.sqrt(length)
        out.append(np.block([[c, s], [-s, c]]))
    both = np.stack([np.stack(out), np.stack([m.T for m in out])]).astype(np.float32)
    high = both.astype(bf16)
    return np.stack([high, (both - high.astype(np.float32)).astype(bf16)], axis=2)


def deinterleave(length):
    half = length // 2
    out = np.zeros((length, length), np.float32)
    out[2 * np.arange(half), np.arange(half)] = 1.0
    out[2 * np.arange(half) + 1, half + np.arange(half)] = 1.0
    return np.stack([out, out.T]).astype(bf16)


def split(x):
    high = x.astype(bf16)
    return high, (x - high.astype(f32)).astype(bf16)


def dot(a, b):
    return jnp.dot(a, b, preferred_element_type=f32)


def mul_left(table, x):
    return dot(jnp.concatenate([table[0], table[1], table[0]], 1), jnp.concatenate([x[0], x[0], x[1]], 0))


def mul_right(x, table):
    return dot(jnp.concatenate([x[0], x[1], x[0]], 1), jnp.concatenate([table[0], table[0], table[1]], 0))


def put(ref, item, where, rows, x):
    for k, part in enumerate(split(x)):
        ref[item, where, k, rows, :] = part


def strips(count, body):
    for i in range(count):
        body(i)


def at(start, length=STRIP):
    return pl.ds(start if isinstance(start, int) else pl.multiple_of(start, STRIP), length)


def exact(x):
    high = x.astype(bf16)
    rest = x - high.astype(f32)
    mid = rest.astype(bf16)
    return high, mid, (rest - mid.astype(f32)).astype(bf16)


def amplitude_kernel(amp, perm, out):
    for s in range(amp.shape[0]):
        high, mid, low = exact(amp[s])
        rows = dot(perm[1], high) + (dot(perm[1], mid) + dot(perm[1], low))
        high, mid, low = exact(rows)
        out[s] = dot(high, perm[0]) + (dot(mid, perm[0]) + dot(low, perm[0]))


def chunk_key():
    return lax.rem(lax.axis_index("tile"), CHUNKS)


def corner(offsets, slot, dim, size, margin):
    t = lax.axis_index("tile")
    along = lax.rem(t, GX) if dim else lax.div(t, GX)
    return offsets[slot, dim] - along * size + margin


def left_half():
    return 1 - lax.rem(lax.axis_index("tile"), 2)


def update_probe(old, streams, coef, out):
    rows = old.shape[2] // CHUNKS
    key = chunk_key()
    for mode, pieces in enumerate(streams):
        rel = 0
        for piece in pieces:
            for k in range(piece.shape[0]):
                here = pl.ds(pl.multiple_of((rel ^ key) * rows, rows), rows)
                out[mode, :, here, :] = old[mode, :, here, :] + coef * piece[k]
                rel += 1


def grouped(refs, streams, per_stream):
    return [refs[i * per_stream : (i + 1) * per_stream] for i in range(streams)]


def shift_in(offsets, slot, near, away, patch, tall):
    frame = patch.shape[-1]
    h = frame // 2
    hr, cols = near.shape[2], 2 * near.shape[3]
    size = cols - 2 * h
    core = lax.axis_index("row")
    first = left_half()
    across = lax.rem(cols - corner(offsets, slot, 1, size, h), cols)

    def strip(ref, c, rows):
        x = jnp.concatenate([ref[first, c, rows, :], ref[1 - first, c, rows, :]], 1)
        return pltpu.roll(x, across, 1)[:, :frame]

    if tall:
        down = lax.rem(2 * hr - corner(offsets, slot, 0, size, h), 2 * hr)
        for c in range(2):
            halves = [strip(ref, c, slice(None)) for ref in (near, away)]
            both = [jnp.where(core == k, halves[0], halves[1]) for k in range(2)]
            patch[c] = pltpu.roll(jnp.concatenate(both, 0), down, 0)[:frame]
        return

    def body(j):
        for ref, half in ((near, core), (away, 1 - core)):
            for c in range(2):
                patch[c, at(half * hr + j * STRIP), :] = strip(ref, c, at(j * STRIP))

    strips(hr // STRIP, body)


def forward_kernel(slot, n_pieces, coef, tall, *refs):
    refs = list(refs)
    offsets, near, away, probe, tab = refs[:5]
    refs = refs[5:]
    modes = probe.shape[0]
    if n_pieces:
        streams = grouped(refs, modes, n_pieces)
        refs = refs[modes * n_pieces :]
        new_probe = refs.pop(3)
        update_probe(probe, streams, coef, new_probe)
        probe = new_probe
    far, power, patch, tall_parts, wide_parts, product = refs
    frame = probe.shape[-1]
    h = frame // 2
    shift_in(offsets, slot, near, away, patch, tall)

    def exits(m, j):
        pair = []
        for start in (j * STRIP, h + j * STRIP):
            rows = at(start)
            pr, pi = probe[m, 0, rows, :], probe[m, 1, rows, :]
            ar, ai = patch[0, rows, :], patch[1, rows, :]
            pair.append((pr * ar - pi * ai, pr * ai + pi * ar))
        for k in range(2):
            put(tall_parts, m, 0, at(k * h + j * STRIP), pair[0][k] + pair[1][k])
            put(tall_parts, m, 1, at(k * h + j * STRIP), pair[0][k] - pair[1][k])

    def columns(m, j):
        for p in range(2):
            y = [product[m, p, at(k * h + j * STRIP), :] for k in range(2)]
            rows = at(p * h + j * STRIP)
            put(wide_parts, m, 0, rows, jnp.concatenate([v[:, :h] + v[:, h:] for v in y], 1))
            put(wide_parts, m, 1, rows, jnp.concatenate([v[:, :h] - v[:, h:] for v in y], 1))

    for m in range(modes):
        strips(h // STRIP, functools.partial(exits, m))
        for p in range(2):
            product[m, p] = mul_left(tab[0, p], tall_parts[m, p])
    for m in range(modes):
        strips(h // STRIP, functools.partial(columns, m))
        for q in range(2):
            far[m, q] = mul_right(wide_parts[m, q], tab[1, q])

    def powers(j):
        rows = at(j * STRIP)
        for q in range(2):
            total = None
            for m in range(modes):
                f = far[m, q, rows, :]
                f = f * f
                f = f[:, :h] + f[:, h:]
                total = f if m == 0 else total + f
            power[rows, slice(q * h, (q + 1) * h)] = total

    strips(frame // STRIP, powers)


def inverse_kernel(mode, last, tall, *refs):
    refs = list(refs)
    offsets, counts, tab, amp, probe = refs[:5]
    refs = refs[5:]
    slots = amp.shape[0]
    fars, powers, others, patches = (refs[i * slots : (i + 1) * slots] for i in range(4))
    refs = refs[4 * slots :]
    before = refs.pop(0) if mode else None
    probe_grad, grads, tall_parts, wide_parts, product_wide, product_tall = refs
    frame = probe.shape[-1]
    h = frame // 2

    def factors(s, j):
        rows = at(j * STRIP)
        factor = amp[s, rows, :] / (jnp.sqrt(powers[s][rows, :] + others[s][rows, :]) + 0.5)
        for q in range(2):
            f = factor[:, q * h : (q + 1) * h]
            put(wide_parts, s, q, rows, fars[s][mode, q, rows, :] * jnp.concatenate([f, f], 1))

    def columns(s, j):
        for p in range(2):
            he, ho = (product_wide[s, q, at(p * h + j * STRIP), :] for q in range(2))
            for k in range(2):
                a, b = he[:, k * h : (k + 1) * h], ho[:, k * h : (k + 1) * h]
                put(tall_parts, s, p, at(k * h + j * STRIP), jnp.concatenate([a + b, a - b], 1))

    for s in range(slots):
        strips(frame // STRIP, functools.partial(factors, s))
        for q in range(2):
            product_wide[s, q] = mul_right(wide_parts[s, q], tab[0, q])
    for s in range(slots):
        strips(h // STRIP, functools.partial(columns, s))
        for p in range(2):
            product_tall[s, p] = mul_left(tab[1, p], tall_parts[s, p])
    key = chunk_key()
    chunk = frame // CHUNKS
    core = lax.axis_index("row")
    first = left_half()

    def results(j):
        x = [
            [[product_tall[s, p, at(k * h + j * STRIP), :] for k in range(2)] for p in range(2)]
            for s in range(slots)
        ]
        for lower in range(2):
            rows = at(lower * h + j * STRIP)
            pr, pi = probe[mode, 0, rows, :], probe[mode, 1, rows, :]
            step = [None, None]
            window = [None, None]
            for s in range(slots):
                even, odd = x[s]
                xr, xi = (even[k] - odd[k] if lower else even[k] + odd[k] for k in range(2))
                live = (s < counts[0]).astype(f32)
                ar, ai = patches[s][0, rows, :], patches[s][1, rows, :]
                ur = (xr - (pr * ar - pi * ai)) * live
                ui = (xi - (pr * ai + pi * ar)) * live
                for k, g in enumerate((ar * ur + ai * ui, ar * ui - ai * ur)):
                    step[k] = g if s == 0 else step[k] + g
                for k, g in enumerate((pr * ur + pi * ui, pr * ui - pi * ur)):
                    if mode:
                        g = g + before[s, k, rows, :]
                    if not last or tall:
                        grads[s, k, rows, :] = g
                        continue
                    wide = 2 * grads.shape[-1]
                    g = jnp.concatenate([g, jnp.zeros((STRIP, wide - frame), f32)], 1)
                    g = pltpu.roll(g, corner(offsets, s, 1, wide - 2 * h, h), 1)
                    window[k] = g if s == 0 else window[k] + g
            start = lower * h + j * STRIP
            for k in range(2):
                probe_grad[(start // chunk) ^ key, k, at(start % chunk), :] = step[k]
                if last and not tall:
                    half = window[k].shape[1] // 2
                    grads[lower ^ core, first, k, at(j * STRIP), :] = window[k][:, :half]
                    grads[lower ^ core, 1 - first, k, at(j * STRIP), :] = window[k][:, half:]

    strips(h // STRIP, results)


def place_kernel(offsets, grads, out):
    slots, _, frame, _ = grads.shape
    _, _, _, hr, half = out.shape
    cols = 2 * half
    h = frame // 2
    size = cols - 2 * h
    core = lax.axis_index("row")
    first = left_half()
    for c in range(2):
        total = None
        for s in range(slots):
            g = jnp.concatenate([grads[s, c], jnp.zeros((2 * hr - frame, frame), f32)], 0)
            g = pltpu.roll(g, corner(offsets, s, 0, size, h), 0)
            g = jnp.concatenate([g, jnp.zeros((2 * hr, cols - frame), f32)], 1)
            g = pltpu.roll(g, corner(offsets, s, 1, size, h), 1)
            total = g if s == 0 else total + g
        for k in range(2):
            out[k ^ core, first, c] = total[k * hr : (k + 1) * hr, :half]
            out[k ^ core, 1 - first, c] = total[k * hr : (k + 1) * hr, half:]


def finish_kernel(n_pieces, coef, *refs):
    refs = list(refs)
    near, away, probe = refs[:3]
    streams = grouped(refs[3:], probe.shape[0], n_pieces)
    tile, new_probe = refs[-2:]
    update_probe(probe, streams, coef, new_probe)
    _, _, hr, half = near.shape
    core = lax.axis_index("row")
    first = left_half()
    for ref, part in ((near, core), (away, 1 - core)):
        rows = pl.ds(pl.multiple_of(part * hr, hr), hr)
        tile[:, rows, :half] = ref[first]
        tile[:, rows, half:] = ref[1 - first]


def vmem():
    return pl.BlockSpec(memory_space=pltpu.VMEM)


def call(kernel, outs, args, scratch=(), flops=0):
    size = sum(math.prod(a.shape) * a.dtype.itemsize for a in args)
    size += sum(math.prod(o) * 4 for o in outs)
    return pl.pallas_call(
        kernel,
        out_shape=[jax.ShapeDtypeStruct(o, f32) for o in outs],
        in_specs=[
            pl.BlockSpec(memory_space=pltpu.SMEM) if a.dtype == jnp.int32 else vmem() for a in args
        ],
        out_specs=[vmem() for _ in outs],
        scratch_shapes=list(scratch),
        cost_estimate=pl.CostEstimate(flops=flops, bytes_accessed=size, transcendentals=0),
        compiler_params=pltpu.CompilerParams(vmem_limit_bytes=40 * 1024 * 1024),
    )(*args)


def swap_rows(x):
    return lax.ppermute(x, "row", [(0, 1), (1, 0)])


def beside(x, inner, tiles):
    pairs = []
    for t in range(tiles):
        other = t + 1 if (t % 2 == 0) == inner else t - 1
        if 0 <= other < tiles and other // GX == t // GX:
            pairs.append((t, other))
    return lax.ppermute(x, "tile", pairs)


def swap_vertical(x, tiles):
    pairs = [(2 * t, 2 * (t - GX) + 1) for t in range(GX, tiles)]
    pairs += [(2 * t + 1, 2 * (t + GX)) for t in range(tiles - GX)]
    return lax.ppermute(x, ("tile", "row"), pairs)


def exchange(x, mask, tiles):
    return lax.ppermute(x, "tile", [(s, s ^ mask) for s in range(tiles)])


def together(*groups):
    return lax.optimization_barrier(groups)


def halves(x, even, inner):
    half = x.shape[-1] // 2
    own_first = even == inner
    a, b = x[..., :half], x[..., half:]
    return jnp.where(own_first, a, b), jnp.where(own_first, b, a)


def joined(own, other, even, inner):
    own_first = even == inner
    return jnp.concatenate([jnp.where(own_first, own, other), jnp.where(own_first, other, own)], -1)


def window_parts(grad, even, wide):
    if wide:
        return [grad[0], grad[1]], [grad[0], grad[1]]
    return zip(*(halves(grad[k], even, k == 0) for k in range(2)))


def reduce_all(parts, grad, even, tiles, wide):
    stay, go = window_parts(grad, even, wide)
    got = [[p[:1]] + [exchange(p[k : k + 1], k, tiles) for k in range(1, CHUNKS)] for p in parts]
    streams = []
    for m in range(len(parts)):
        held = sum(got[m][1:], got[m][0])
        if m == 0:
            held, go = together(held, tuple(go))
            outer = beside(go[1], False, tiles)
            inner = beside(go[0], True, tiles)
        mask = CHUNKS
        while mask < tiles:
            held = held + exchange(held, mask, tiles)
            mask *= 2
        if m + 1 < len(parts):
            held, got[m + 1] = together(held, got[m + 1])
        else:
            held, inner, outer, *streams = together(held, inner, outer, *streams)
        streams.append([held] + [exchange(held, k, tiles) for k in range(1, CHUNKS)])
    return streams, jnp.stack([stay[0] + inner, stay[1] + outer])


def per_device(object_tiles, probe_modes, amplitude, offsets, counts):
    own_tile = object_tiles[0]
    size = own_tile.shape[-1]
    frame = probe_modes.shape[-1]
    half = frame // 2
    tiles = lax.axis_size("tile")
    tall = tiles > GX
    slots = offsets.shape[0]
    modes = probe_modes.shape[0]
    core = lax.axis_index("row")
    even = lax.axis_index("tile") % 2 == 0
    hr = size // 2
    tab = jnp.asarray(tables(frame))
    perm = jnp.asarray(deinterleave(frame))
    coef = 4.0 / (slots * tiles)

    mine = lax.dynamic_slice(own_tile, (0, core * hr, 0), (2, hr, size))
    own = [jnp.where(even == inner, mine[:, :, half:], mine[:, :, :half]) for inner in (True, False)]
    got = [beside(own[1], False, tiles), beside(own[0], True, tiles)]
    near = jnp.stack([joined(own[0], got[1], even, True), joined(own[1], got[0], even, False)])
    if tall:
        other = swap_vertical(near, tiles)
        near = jnp.where(core == 0, jnp.concatenate([other, near], 2), jnp.concatenate([near, other], 2))
    (amp,) = call(amplitude_kernel, [amplitude.shape], [amplitude, perm])
    away = swap_rows(near)
    near, away, amp = together(near, away, amp)

    def scratch(count):
        return [pltpu.VMEM((count, 2, 2, frame, frame), bf16) for _ in range(2)]

    matmul = 4 * 2 * 3 * 4 * frame**3
    probe = probe_modes
    streams = None
    for iteration in range(ITERS):
        final = iteration + 1 == ITERS
        fars, powers, others, patches = [], [], [], []
        for s in range(slots):
            args = [offsets, near, away, probe, tab]
            outs = [(modes, 2, frame, frame), (frame, frame), (2, frame, frame)]
            count = 0
            if streams is not None:
                count = len(streams[0])
                args += [p for group in streams for p in group]
                outs.append(probe.shape)
                streams = None
            got = call(
                functools.partial(forward_kernel, s, count, coef, tall),
                outs,
                args,
                scratch(modes) + [pltpu.VMEM((modes, 2, frame, frame), f32)],
                matmul * modes,
            )
            if count:
                probe = got[3]
            fars.append(got[0])
            powers.append(got[1])
            patches.append(got[2])
            others.append(swap_rows(got[1]))
        before = None
        parts = []
        for m in range(modes):
            last = m == modes - 1
            args = [offsets, counts, tab, amp, probe] + fars + powers + others + patches
            if m:
                args.append(before)
            grads = (2,) + near.shape if last and not tall else (slots, 2, frame, frame)
            part = (CHUNKS, 2, frame // CHUNKS, frame)
            got = call(
                functools.partial(inverse_kernel, m, last, tall),
                [part, grads],
                args,
                scratch(slots) + [pltpu.VMEM((slots, 2, frame, frame), f32) for _ in range(2)],
                matmul * slots,
            )
            parts.append(got[0])
            before = got[1]
        if tall:
            (before,) = call(place_kernel, [(2,) + near.shape], [offsets, before])
        grad = before[0] + swap_rows(before[1])
        wide = tall or not final
        streams, total = reduce_all(parts, grad, even, tiles, wide)
        if tall:
            total = total + swap_vertical(total, tiles)
        if wide:
            near = near + total / MODES
        if final:
            near = jnp.stack([halves(near[k], even, k == 0)[0] for k in range(2)])
            if not wide:
                near = near + total / MODES
            if tall:
                near = jnp.where(core == 0, near[:, :, half:], near[:, :, : size - half])
        away = swap_rows(near)
    args = [near, away, probe] + [p for group in streams for p in group]
    tile, probe = call(
        functools.partial(finish_kernel, len(streams[0]), coef), [own_tile.shape, probe.shape], args
    )
    return (tile[None], probe)


def solution(mesh):
    return jax.shard_map(
        per_device,
        mesh=mesh,
        in_specs=(
            P(("scan", "tile"), None, None, None),
            P("row", None, None, None),
            P(("scan", "tile"), None, None),
            P(("scan", "tile"), None),
            P(("scan", "tile")),
        ),
        out_specs=(P(("scan", "tile"), None, None, None), P(("scan", "row"), None, None, None)),
        check_vma=False,
    )
```

```python
import functools
import math

import jax
import jax.numpy as jnp
import numpy as np
from jax import lax
from jax.experimental import pallas as pl
from jax.experimental.pallas import tpu as pltpu
from jax.sharding import PartitionSpec as P

MODES = 4
GX = 8
ITERS = 2
HALVINGS = 2
CHUNKS = 1 << HALVINGS
ORDERS = ((0, 1, 2), (1, 0, 2))
STRIP = 16
ORDERS = ((0, 1, 2), (1, 0, 2))

f32 = jnp.float32
bf16 = jnp.bfloat16


def tables(length):
    half = length // 2
    n = np.arange(half)
    out = []
    for odd in (0, 1):
        angle = 2.0 * math.pi * np.outer(2 * n + odd, n) / length
        c, s = np.cos(angle) / math.sqrt(length), np.sin(angle) / math.sqrt(length)
        out.append(np.block([[c, s], [-s, c]]))
    both = np.stack([np.stack(out), np.stack([m.T for m in out])]).astype(np.float32)
    high = both.astype(bf16)
    return np.stack([high, (both - high.astype(np.float32)).astype(bf16)], axis=2)


def deinterleave(length):
    half = length // 2
    out = np.zeros((length, length), np.float32)
    out[2 * np.arange(half), np.arange(half)] = 1.0
    out[2 * np.arange(half) + 1, half + np.arange(half)] = 1.0
    return np.stack([out, out.T]).astype(bf16)


def split(x):
    high = x.astype(bf16)
    return high, (x - high.astype(f32)).astype(bf16)


def dot(a, b):
    return jnp.dot(a, b, preferred_element_type=f32)


def mul_left(table, x):
    return dot(jnp.concatenate([table[0], table[1], table[0]], 1), jnp.concatenate([x[0], x[0], x[1]], 0))


def mul_right(x, table):
    return dot(jnp.concatenate([x[0], x[1], x[0]], 1), jnp.concatenate([table[0], table[0], table[1]], 0))


def put(ref, item, where, rows, x):
    for k, part in enumerate(split(x)):
        ref[item, where, k, rows, :] = part


def strips(count, body):
    for i in range(count):
        body(i)


def at(start, length=STRIP):
    return pl.ds(start if isinstance(start, int) else pl.multiple_of(start, STRIP), length)


def exact(x):
    high = x.astype(bf16)
    rest = x - high.astype(f32)
    mid = rest.astype(bf16)
    return high, mid, (rest - mid.astype(f32)).astype(bf16)


def amplitude_kernel(amp, perm, out):
    for s in range(amp.shape[0]):
        high, mid, low = exact(amp[s])
        rows = dot(perm[1], high) + (dot(perm[1], mid) + dot(perm[1], low))
        high, mid, low = exact(rows)
        out[s] = dot(high, perm[0]) + (dot(mid, perm[0]) + dot(low, perm[0]))


def chunk_key(order):
    t = lax.axis_index("tile")
    return sum(((t >> order[i]) & 1) << (HALVINGS - 1 - i) for i in range(HALVINGS))


def corner(offsets, slot, dim, size, margin):
    t = lax.axis_index("tile")
    along = lax.rem(t, GX) if dim else lax.div(t, GX)
    return offsets[slot, dim] - along * size + margin


def left_half():
    return 1 - lax.rem(lax.axis_index("tile"), 2)


def update_probe(old, streams, coef, out):
    rows = old.shape[2] // CHUNKS
    for mode, pieces in enumerate(streams):
        key = chunk_key(ORDERS[mode])
        rel = 0
        for piece in pieces:
            for k in range(piece.shape[0]):
                here = pl.ds(pl.multiple_of((rel ^ key) * rows, rows), rows)
                out[mode, :, here, :] = old[mode, :, here, :] + coef * piece[k]
                rel += 1


def grouped(refs, streams, per_stream):
    return [refs[i * per_stream : (i + 1) * per_stream] for i in range(streams)]


def shift_in(offsets, slot, near, away, patch, tall):
    frame = patch.shape[-1]
    h = frame // 2
    hr, cols = near.shape[2], 2 * near.shape[3]
    size = cols - 2 * h
    core = lax.axis_index("row")
    first = left_half()
    across = lax.rem(cols - corner(offsets, slot, 1, size, h), cols)

    def strip(ref, c, rows):
        x = jnp.concatenate([ref[first, c, rows, :], ref[1 - first, c, rows, :]], 1)
        return pltpu.roll(x, across, 1)[:, :frame]

    if tall:
        down = lax.rem(2 * hr - corner(offsets, slot, 0, size, h), 2 * hr)
        for c in range(2):
            halves = [strip(ref, c, slice(None)) for ref in (near, away)]
            both = [jnp.where(core == k, halves[0], halves[1]) for k in range(2)]
            patch[c] = pltpu.roll(jnp.concatenate(both, 0), down, 0)[:frame]
        return

    def body(j):
        for ref, half in ((near, core), (away, 1 - core)):
            for c in range(2):
                patch[c, at(half * hr + j * STRIP), :] = strip(ref, c, at(j * STRIP))

    strips(hr // STRIP, body)


def forward_kernel(slot, n_pieces, coef, tall, *refs):
    refs = list(refs)
    offsets, near, away, probe, tab = refs[:5]
    refs = refs[5:]
    modes = probe.shape[0]
    if n_pieces:
        streams = grouped(refs, modes, n_pieces)
        refs = refs[modes * n_pieces :]
        new_probe = refs.pop(3)
        update_probe(probe, streams, coef, new_probe)
        probe = new_probe
    far, power, patch, tall_parts, wide_parts, product = refs
    frame = probe.shape[-1]
    h = frame // 2
    shift_in(offsets, slot, near, away, patch, tall)

    def exits(m, j):
        pair = []
        for start in (j * STRIP, h + j * STRIP):
            rows = at(start)
            pr, pi = probe[m, 0, rows, :], probe[m, 1, rows, :]
            ar, ai = patch[0, rows, :], patch[1, rows, :]
            pair.append((pr * ar - pi * ai, pr * ai + pi * ar))
        for k in range(2):
            put(tall_parts, m, 0, at(k * h + j * STRIP), pair[0][k] + pair[1][k])
            put(tall_parts, m, 1, at(k * h + j * STRIP), pair[0][k] - pair[1][k])

    def columns(m, j):
        for p in range(2):
            y = [product[m, p, at(k * h + j * STRIP), :] for k in range(2)]
            rows = at(p * h + j * STRIP)
            put(wide_parts, m, 0, rows, jnp.concatenate([v[:, :h] + v[:, h:] for v in y], 1))
            put(wide_parts, m, 1, rows, jnp.concatenate([v[:, :h] - v[:, h:] for v in y], 1))

    for m in range(modes):
        strips(h // STRIP, functools.partial(exits, m))
        for p in range(2):
            product[m, p] = mul_left(tab[0, p], tall_parts[m, p])
    for m in range(modes):
        strips(h // STRIP, functools.partial(columns, m))
        for q in range(2):
            far[m, q] = mul_right(wide_parts[m, q], tab[1, q])

    def powers(j):
        rows = at(j * STRIP)
        for q in range(2):
            total = None
            for m in range(modes):
                f = far[m, q, rows, :]
                f = f * f
                f = f[:, :h] + f[:, h:]
                total = f if m == 0 else total + f
            power[rows, slice(q * h, (q + 1) * h)] = total

    strips(frame // STRIP, powers)


def inverse_kernel(mode, last, tall, *refs):
    refs = list(refs)
    offsets, counts, tab, amp, probe = refs[:5]
    refs = refs[5:]
    slots = amp.shape[0]
    fars, powers, others, patches = (refs[i * slots : (i + 1) * slots] for i in range(4))
    refs = refs[4 * slots :]
    before = refs.pop(0) if mode else None
    probe_grad, grads, tall_parts, wide_parts, product_wide, product_tall = refs
    frame = probe.shape[-1]
    h = frame // 2

    def factors(s, j):
        rows = at(j * STRIP)
        factor = amp[s, rows, :] / (jnp.sqrt(powers[s][rows, :] + others[s][rows, :]) + 0.5)
        for q in range(2):
            f = factor[:, q * h : (q + 1) * h]
            put(wide_parts, s, q, rows, fars[s][mode, q, rows, :] * jnp.concatenate([f, f], 1))

    def columns(s, j):
        for p in range(2):
            he, ho = (product_wide[s, q, at(p * h + j * STRIP), :] for q in range(2))
            for k in range(2):
                a, b = he[:, k * h : (k + 1) * h], ho[:, k * h : (k + 1) * h]
                put(tall_parts, s, p, at(k * h + j * STRIP), jnp.concatenate([a + b, a - b], 1))

    for s in range(slots):
        strips(frame // STRIP, functools.partial(factors, s))
        for q in range(2):
            product_wide[s, q] = mul_right(wide_parts[s, q], tab[0, q])
    for s in range(slots):
        strips(h // STRIP, functools.partial(columns, s))
        for p in range(2):
            product_tall[s, p] = mul_left(tab[1, p], tall_parts[s, p])
    key = chunk_key(ORDERS[mode])
    chunk = frame // CHUNKS
    core = lax.axis_index("row")
    first = left_half()

    def results(j):
        x = [
            [[product_tall[s, p, at(k * h + j * STRIP), :] for k in range(2)] for p in range(2)]
            for s in range(slots)
        ]
        for lower in range(2):
            rows = at(lower * h + j * STRIP)
            pr, pi = probe[mode, 0, rows, :], probe[mode, 1, rows, :]
            step = [None, None]
            window = [None, None]
            for s in range(slots):
                even, odd = x[s]
                xr, xi = (even[k] - odd[k] if lower else even[k] + odd[k] for k in range(2))
                live = (s < counts[0]).astype(f32)
                ar, ai = patches[s][0, rows, :], patches[s][1, rows, :]
                ur = (xr - (pr * ar - pi * ai)) * live
                ui = (xi - (pr * ai + pi * ar)) * live
                for k, g in enumerate((ar * ur + ai * ui, ar * ui - ai * ur)):
                    step[k] = g if s == 0 else step[k] + g
                for k, g in enumerate((pr * ur + pi * ui, pr * ui - pi * ur)):
                    if mode:
                        g = g + before[s, k, rows, :]
                    if not last or tall:
                        grads[s, k, rows, :] = g
                        continue
                    wide = 2 * grads.shape[-1]
                    g = jnp.concatenate([g, jnp.zeros((STRIP, wide - frame), f32)], 1)
                    g = pltpu.roll(g, corner(offsets, s, 1, wide - 2 * h, h), 1)
                    window[k] = g if s == 0 else window[k] + g
            start = lower * h + j * STRIP
            for k in range(2):
                probe_grad[(start // chunk) ^ key, k, at(start % chunk), :] = step[k]
                if last and not tall:
                    half = window[k].shape[1] // 2
                    grads[lower ^ core, first, k, at(j * STRIP), :] = window[k][:, :half]
                    grads[lower ^ core, 1 - first, k, at(j * STRIP), :] = window[k][:, half:]

    strips(h // STRIP, results)


def place_kernel(offsets, grads, out):
    slots, _, frame, _ = grads.shape
    _, _, _, hr, half = out.shape
    cols = 2 * half
    h = frame // 2
    size = cols - 2 * h
    core = lax.axis_index("row")
    first = left_half()
    for c in range(2):
        total = None
        for s in range(slots):
            g = jnp.concatenate([grads[s, c], jnp.zeros((2 * hr - frame, frame), f32)], 0)
            g = pltpu.roll(g, corner(offsets, s, 0, size, h), 0)
            g = jnp.concatenate([g, jnp.zeros((2 * hr, cols - frame), f32)], 1)
            g = pltpu.roll(g, corner(offsets, s, 1, size, h), 1)
            total = g if s == 0 else total + g
        for k in range(2):
            out[k ^ core, first, c] = total[k * hr : (k + 1) * hr, :half]
            out[k ^ core, 1 - first, c] = total[k * hr : (k + 1) * hr, half:]


def finish_kernel(n_pieces, coef, *refs):
    refs = list(refs)
    near, away, probe = refs[:3]
    streams = grouped(refs[3:], probe.shape[0], n_pieces)
    tile, new_probe = refs[-2:]
    update_probe(probe, streams, coef, new_probe)
    _, _, hr, half = near.shape
    core = lax.axis_index("row")
    first = left_half()
    for ref, part in ((near, core), (away, 1 - core)):
        rows = pl.ds(pl.multiple_of(part * hr, hr), hr)
        tile[:, rows, :half] = ref[first]
        tile[:, rows, half:] = ref[1 - first]


def vmem():
    return pl.BlockSpec(memory_space=pltpu.VMEM)


def call(kernel, outs, args, scratch=(), flops=0):
    size = sum(math.prod(a.shape) * a.dtype.itemsize for a in args)
    size += sum(math.prod(o) * 4 for o in outs)
    return pl.pallas_call(
        kernel,
        out_shape=[jax.ShapeDtypeStruct(o, f32) for o in outs],
        in_specs=[
            pl.BlockSpec(memory_space=pltpu.SMEM) if a.dtype == jnp.int32 else vmem() for a in args
        ],
        out_specs=[vmem() for _ in outs],
        scratch_shapes=list(scratch),
        cost_estimate=pl.CostEstimate(flops=flops, bytes_accessed=size, transcendentals=0),
        compiler_params=pltpu.CompilerParams(vmem_limit_bytes=40 * 1024 * 1024),
    )(*args)


def swap_rows(x):
    return lax.ppermute(x, "row", [(0, 1), (1, 0)])


def beside(x, inner, tiles):
    pairs = []
    for t in range(tiles):
        other = t + 1 if (t % 2 == 0) == inner else t - 1
        if 0 <= other < tiles and other // GX == t // GX:
            pairs.append((t, other))
    return lax.ppermute(x, "tile", pairs)


def swap_vertical(x, tiles):
    pairs = [(2 * t, 2 * (t - GX) + 1) for t in range(GX, tiles)]
    pairs += [(2 * t + 1, 2 * (t + GX)) for t in range(tiles - GX)]
    return lax.ppermute(x, ("tile", "row"), pairs)


def exchange(x, bit, tiles):
    return lax.ppermute(x, "tile", [(s, s ^ (1 << bit)) for s in range(tiles)])


def together(*groups):
    return lax.optimization_barrier(groups)


def halves(x, even, inner):
    half = x.shape[-1] // 2
    own_first = even == inner
    a, b = x[..., :half], x[..., half:]
    return jnp.where(own_first, a, b), jnp.where(own_first, b, a)


def joined(own, other, even, inner):
    own_first = even == inner
    return jnp.concatenate([jnp.where(own_first, own, other), jnp.where(own_first, other, own)], -1)


def window_parts(grad, even, wide):
    if wide:
        return [grad[0], grad[1]], [grad[0], grad[1]]
    return zip(*(halves(grad[k], even, k == 0) for k in range(2)))


def reduce_all(parts, grad, even, tiles, wide):
    bits = int(math.log2(tiles))
    stay, go = window_parts(grad, even, wide)
    held = list(parts)
    go, got = list(go), [None, None]
    for i in range(HALVINGS):
        n = held[0].shape[0] // 2
        held = [h[:n] + exchange(h[n:], o[i], tiles) for h, o in zip(held, ORDERS)]
        held, go[1 - i] = together(held, go[1 - i])
        got[1 - i] = beside(go[1 - i], i == 1, tiles)
    held = [h + exchange(h, o[-1], tiles) for h, o in zip(held, ORDERS)]
    held, got = together(held, got)
    for bit in range(len(ORDERS[0]), bits):
        held = [h + exchange(h, bit, tiles) for h in held]
    pieces = [[h] for h in held]
    for i in reversed(range(HALVINGS)):
        for p, o in zip(pieces, ORDERS):
            p.append(exchange(p[0] if len(p) == 1 else jnp.concatenate(p, 0), o[i], tiles))
        if i:
            (pieces,) = together(pieces)
    return pieces, jnp.stack([a + b for a, b in zip(stay, got)])


def per_device(object_tiles, probe_modes, amplitude, offsets, counts):
    own_tile = object_tiles[0]
    size = own_tile.shape[-1]
    frame = probe_modes.shape[-1]
    half = frame // 2
    tiles = lax.axis_size("tile")
    tall = tiles > GX
    slots = offsets.shape[0]
    modes = probe_modes.shape[0]
    core = lax.axis_index("row")
    even = lax.axis_index("tile") % 2 == 0
    hr = size // 2
    tab = jnp.asarray(tables(frame))
    perm = jnp.asarray(deinterleave(frame))
    coef = 4.0 / (slots * tiles)

    mine = lax.dynamic_slice(own_tile, (0, core * hr, 0), (2, hr, size))
    own = [jnp.where(even == inner, mine[:, :, half:], mine[:, :, :half]) for inner in (True, False)]
    got = [beside(own[1], False, tiles), beside(own[0], True, tiles)]
    near = jnp.stack([joined(own[0], got[1], even, True), joined(own[1], got[0], even, False)])
    if tall:
        other = swap_vertical(near, tiles)
        near = jnp.where(core == 0, jnp.concatenate([other, near], 2), jnp.concatenate([near, other], 2))
    (amp,) = call(amplitude_kernel, [amplitude.shape], [amplitude, perm])
    away = swap_rows(near)
    near, away, amp = together(near, away, amp)

    def scratch(count):
        return [pltpu.VMEM((count, 2, 2, frame, frame), bf16) for _ in range(2)]

    matmul = 4 * 2 * 3 * 4 * frame**3
    probe = probe_modes
    streams = None
    for iteration in range(ITERS):
        final = iteration + 1 == ITERS
        fars, powers, others, patches = [], [], [], []
        for s in range(slots):
            args = [offsets, near, away, probe, tab]
            outs = [(modes, 2, frame, frame), (frame, frame), (2, frame, frame)]
            count = 0
            if streams is not None:
                count = len(streams[0])
                args += [p for group in streams for p in group]
                outs.append(probe.shape)
                streams = None
            got = call(
                functools.partial(forward_kernel, s, count, coef, tall),
                outs,
                args,
                scratch(modes) + [pltpu.VMEM((modes, 2, frame, frame), f32)],
                matmul * modes,
            )
            if count:
                probe = got[3]
            fars.append(got[0])
            powers.append(got[1])
            patches.append(got[2])
            others.append(swap_rows(got[1]))
        before = None
        parts = []
        for m in range(modes):
            last = m == modes - 1
            args = [offsets, counts, tab, amp, probe] + fars + powers + others + patches
            if m:
                args.append(before)
            grads = (2,) + near.shape if last and not tall else (slots, 2, frame, frame)
            part = (CHUNKS, 2, frame // CHUNKS, frame)
            got = call(
                functools.partial(inverse_kernel, m, last, tall),
                [part, grads],
                args,
                scratch(slots) + [pltpu.VMEM((slots, 2, frame, frame), f32) for _ in range(2)],
                matmul * slots,
            )
            parts.append(got[0])
            before = got[1]
        if tall:
            (before,) = call(place_kernel, [(2,) + near.shape], [offsets, before])
        grad = before[0] + swap_rows(before[1])
        wide = tall or not final
        streams, total = reduce_all(parts, grad, even, tiles, wide)
        if tall:
            total = total + swap_vertical(total, tiles)
        if wide:
            near = near + total / MODES
        if final:
            near = jnp.stack([halves(near[k], even, k == 0)[0] for k in range(2)])
            if not wide:
                near = near + total / MODES
            if tall:
                near = jnp.where(core == 0, near[:, :, half:], near[:, :, : size - half])
        away = swap_rows(near)
    args = [near, away, probe] + [p for group in streams for p in group]
    tile, probe = call(
        functools.partial(finish_kernel, len(streams[0]), coef), [own_tile.shape, probe.shape], args
    )
    return (tile[None], probe)


def solution(mesh):
    return jax.shard_map(
        per_device,
        mesh=mesh,
        in_specs=(
            P(("scan", "tile"), None, None, None),
            P("row", None, None, None),
            P(("scan", "tile"), None, None),
            P(("scan", "tile"), None),
            P(("scan", "tile")),
        ),
        out_specs=(P(("scan", "tile"), None, None, None), P(("scan", "row"), None, None, None)),
        check_vma=False,
    )
```

```python
import functools
import math

import jax
import jax.numpy as jnp
import numpy as np
from jax import lax
from jax.experimental import pallas as pl
from jax.experimental.pallas import tpu as pltpu
from jax.sharding import PartitionSpec as P

MODES = 4
GX = 8
ITERS = 2
HALVINGS = 2
CHUNKS = 1 << HALVINGS
ORDERS = ((0, 1, 2), (1, 0, 2))
STRIP = 16
ORDERS = ((0, 1, 2), (1, 0, 2))

f32 = jnp.float32
bf16 = jnp.bfloat16


def tables(length):
    half = length // 2
    n = np.arange(half)
    out = []
    for odd in (0, 1):
        angle = 2.0 * math.pi * np.outer(2 * n + odd, n) / length
        c, s = np.cos(angle) / math.sqrt(length), np.sin(angle) / math.sqrt(length)
        out.append(np.block([[c, s], [-s, c]]))
    both = np.stack([np.stack(out), np.stack([m.T for m in out])]).astype(np.float32)
    high = both.astype(bf16)
    return np.stack([high, (both - high.astype(np.float32)).astype(bf16)], axis=2)


def deinterleave(length):
    half = length // 2
    out = np.zeros((length, length), np.float32)
    out[2 * np.arange(half), np.arange(half)] = 1.0
    out[2 * np.arange(half) + 1, half + np.arange(half)] = 1.0
    return np.stack([out, out.T]).astype(bf16)


def split(x):
    high = x.astype(bf16)
    return high, (x - high.astype(f32)).astype(bf16)


def dot(a, b):
    return jnp.dot(a, b, preferred_element_type=f32)


def mul_left(table, x):
    return dot(jnp.concatenate([table[0], table[1], table[0]], 1), jnp.concatenate([x[0], x[0], x[1]], 0))


def mul_right(x, table):
    return dot(jnp.concatenate([x[0], x[1], x[0]], 1), jnp.concatenate([table[0], table[0], table[1]], 0))


def put(ref, item, where, rows, x):
    for k, part in enumerate(split(x)):
        ref[item, where, k, rows, :] = part


def strips(count, body):
    for i in range(count):
        body(i)


def at(start, length=STRIP):
    return pl.ds(start if isinstance(start, int) else pl.multiple_of(start, STRIP), length)


def exact(x):
    high = x.astype(bf16)
    rest = x - high.astype(f32)
    mid = rest.astype(bf16)
    return high, mid, (rest - mid.astype(f32)).astype(bf16)


def amplitude_kernel(amp, perm, out):
    for s in range(amp.shape[0]):
        high, mid, low = exact(amp[s])
        rows = dot(perm[1], high) + (dot(perm[1], mid) + dot(perm[1], low))
        high, mid, low = exact(rows)
        out[s] = dot(high, perm[0]) + (dot(mid, perm[0]) + dot(low, perm[0]))


def chunk_key(order):
    t = lax.axis_index("tile")
    return sum(((t >> order[i]) & 1) << (HALVINGS - 1 - i) for i in range(HALVINGS))


def corner(offsets, slot, dim, size, margin):
    t = lax.axis_index("tile")
    along = lax.rem(t, GX) if dim else lax.div(t, GX)
    return offsets[slot, dim] - along * size + margin


def left_half():
    return 1 - lax.rem(lax.axis_index("tile"), 2)


def update_probe(old, streams, coef, out):
    rows = old.shape[2] // CHUNKS
    for mode, pieces in enumerate(streams):
        key = chunk_key(ORDERS[mode])
        rel = 0
        for piece in pieces:
            for k in range(piece.shape[0]):
                here = pl.ds(pl.multiple_of((rel ^ key) * rows, rows), rows)
                out[mode, :, here, :] = old[mode, :, here, :] + coef * piece[k]
                rel += 1


def grouped(refs, streams, per_stream):
    return [refs[i * per_stream : (i + 1) * per_stream] for i in range(streams)]


def shift_in(offsets, slot, near, away, patch, tall):
    frame = patch.shape[-1]
    h = frame // 2
    hr, cols = near.shape[2], 2 * near.shape[3]
    size = cols - 2 * h
    core = lax.axis_index("row")
    first = left_half()
    across = lax.rem(cols - corner(offsets, slot, 1, size, h), cols)

    def strip(ref, c, rows):
        x = jnp.concatenate([ref[first, c, rows, :], ref[1 - first, c, rows, :]], 1)
        return pltpu.roll(x, across, 1)[:, :frame]

    if tall:
        down = lax.rem(2 * hr - corner(offsets, slot, 0, size, h), 2 * hr)
        for c in range(2):
            halves = [strip(ref, c, slice(None)) for ref in (near, away)]
            both = [jnp.where(core == k, halves[0], halves[1]) for k in range(2)]
            patch[c] = pltpu.roll(jnp.concatenate(both, 0), down, 0)[:frame]
        return

    def body(j):
        for ref, half in ((near, core), (away, 1 - core)):
            for c in range(2):
                patch[c, at(half * hr + j * STRIP), :] = strip(ref, c, at(j * STRIP))

    strips(hr // STRIP, body)


def forward_kernel(slot, n_pieces, coef, tall, *refs):
    refs = list(refs)
    offsets, near, away, probe, tab = refs[:5]
    refs = refs[5:]
    modes = probe.shape[0]
    if n_pieces:
        streams = grouped(refs, modes, n_pieces)
        refs = refs[modes * n_pieces :]
        new_probe = refs.pop(3)
        update_probe(probe, streams, coef, new_probe)
        probe = new_probe
    far, power, patch, tall_parts, wide_parts, product = refs
    frame = probe.shape[-1]
    h = frame // 2
    shift_in(offsets, slot, near, away, patch, tall)

    def exits(m, j):
        pair = []
        for start in (j * STRIP, h + j * STRIP):
            rows = at(start)
            pr, pi = probe[m, 0, rows, :], probe[m, 1, rows, :]
            ar, ai = patch[0, rows, :], patch[1, rows, :]
            pair.append((pr * ar - pi * ai, pr * ai + pi * ar))
        for k in range(2):
            put(tall_parts, m, 0, at(k * h + j * STRIP), pair[0][k] + pair[1][k])
            put(tall_parts, m, 1, at(k * h + j * STRIP), pair[0][k] - pair[1][k])

    def columns(m, j):
        for p in range(2):
            y = [product[m, p, at(k * h + j * STRIP), :] for k in range(2)]
            rows = at(p * h + j * STRIP)
            put(wide_parts, m, 0, rows, jnp.concatenate([v[:, :h] + v[:, h:] for v in y], 1))
            put(wide_parts, m, 1, rows, jnp.concatenate([v[:, :h] - v[:, h:] for v in y], 1))

    for m in range(modes):
        strips(h // STRIP, functools.partial(exits, m))
        for p in range(2):
            product[m, p] = mul_left(tab[0, p], tall_parts[m, p])
    for m in range(modes):
        strips(h // STRIP, functools.partial(columns, m))
        for q in range(2):
            far[m, q] = mul_right(wide_parts[m, q], tab[1, q])

    def powers(j):
        rows = at(j * STRIP)
        for q in range(2):
            total = None
            for m in range(modes):
                f = far[m, q, rows, :]
                f = f * f
                f = f[:, :h] + f[:, h:]
                total = f if m == 0 else total + f
            power[rows, slice(q * h, (q + 1) * h)] = total

    strips(frame // STRIP, powers)


def inverse_kernel(mode, last, tall, *refs):
    refs = list(refs)
    offsets, counts, tab, amp, probe = refs[:5]
    refs = refs[5:]
    slots = amp.shape[0]
    fars, patches = refs[:slots], refs[slots : 2 * slots]
    refs = refs[2 * slots :]
    if mode:
        factors_in, before = refs[:2]
        refs = refs[2:]
    else:
        powers, others = refs[:slots], refs[slots : 2 * slots]
        refs = refs[2 * slots :]
        factors_out = refs.pop(2)
    probe_grad, grads, tall_parts, wide_parts, product_wide, product_tall = refs
    frame = probe.shape[-1]
    h = frame // 2

    def factors(s, j):
        rows = at(j * STRIP)
        if mode:
            factor = factors_in[s, rows, :]
        else:
            factor = amp[s, rows, :] / (jnp.sqrt(powers[s][rows, :] + others[s][rows, :]) + 0.5)
            factors_out[s, rows, :] = factor
        for q in range(2):
            f = factor[:, q * h : (q + 1) * h]
            put(wide_parts, s, q, rows, fars[s][mode, q, rows, :] * jnp.concatenate([f, f], 1))

    def columns(s, j):
        for p in range(2):
            he, ho = (product_wide[s, q, at(p * h + j * STRIP), :] for q in range(2))
            for k in range(2):
                a, b = he[:, k * h : (k + 1) * h], ho[:, k * h : (k + 1) * h]
                put(tall_parts, s, p, at(k * h + j * STRIP), jnp.concatenate([a + b, a - b], 1))

    for s in range(slots):
        strips(frame // STRIP, functools.partial(factors, s))
        for q in range(2):
            product_wide[s, q] = mul_right(wide_parts[s, q], tab[0, q])
    for s in range(slots):
        strips(h // STRIP, functools.partial(columns, s))
        for p in range(2):
            product_tall[s, p] = mul_left(tab[1, p], tall_parts[s, p])
    key = chunk_key(ORDERS[mode])
    chunk = frame // CHUNKS
    core = lax.axis_index("row")
    first = left_half()

    def results(j):
        x = [
            [[product_tall[s, p, at(k * h + j * STRIP), :] for k in range(2)] for p in range(2)]
            for s in range(slots)
        ]
        for lower in range(2):
            rows = at(lower * h + j * STRIP)
            pr, pi = probe[mode, 0, rows, :], probe[mode, 1, rows, :]
            step = [None, None]
            window = [None, None]
            for s in range(slots):
                even, odd = x[s]
                xr, xi = (even[k] - odd[k] if lower else even[k] + odd[k] for k in range(2))
                live = (s < counts[0]).astype(f32)
                ar, ai = patches[s][0, rows, :], patches[s][1, rows, :]
                ur = (xr - (pr * ar - pi * ai)) * live
                ui = (xi - (pr * ai + pi * ar)) * live
                for k, g in enumerate((ar * ur + ai * ui, ar * ui - ai * ur)):
                    step[k] = g if s == 0 else step[k] + g
                for k, g in enumerate((pr * ur + pi * ui, pr * ui - pi * ur)):
                    if mode:
                        g = g + before[s, k, rows, :]
                    if not last or tall:
                        grads[s, k, rows, :] = g
                        continue
                    wide = 2 * grads.shape[-1]
                    g = jnp.concatenate([g, jnp.zeros((STRIP, wide - frame), f32)], 1)
                    g = pltpu.roll(g, corner(offsets, s, 1, wide - 2 * h, h), 1)
                    window[k] = g if s == 0 else window[k] + g
            start = lower * h + j * STRIP
            for k in range(2):
                probe_grad[(start // chunk) ^ key, k, at(start % chunk), :] = step[k]
                if last and not tall:
                    half = window[k].shape[1] // 2
                    grads[lower ^ core, first, k, at(j * STRIP), :] = window[k][:, :half]
                    grads[lower ^ core, 1 - first, k, at(j * STRIP), :] = window[k][:, half:]

    strips(h // STRIP, results)


def place_kernel(offsets, grads, out):
    slots, _, frame, _ = grads.shape
    _, _, _, hr, half = out.shape
    cols = 2 * half
    h = frame // 2
    size = cols - 2 * h
    core = lax.axis_index("row")
    first = left_half()
    for c in range(2):
        total = None
        for s in range(slots):
            g = jnp.concatenate([grads[s, c], jnp.zeros((2 * hr - frame, frame), f32)], 0)
            g = pltpu.roll(g, corner(offsets, s, 0, size, h), 0)
            g = jnp.concatenate([g, jnp.zeros((2 * hr, cols - frame), f32)], 1)
            g = pltpu.roll(g, corner(offsets, s, 1, size, h), 1)
            total = g if s == 0 else total + g
        for k in range(2):
            out[k ^ core, first, c] = total[k * hr : (k + 1) * hr, :half]
            out[k ^ core, 1 - first, c] = total[k * hr : (k + 1) * hr, half:]


def finish_kernel(n_pieces, coef, *refs):
    refs = list(refs)
    near, away, probe = refs[:3]
    streams = grouped(refs[3:], probe.shape[0], n_pieces)
    tile, new_probe = refs[-2:]
    update_probe(probe, streams, coef, new_probe)
    _, _, hr, half = near.shape
    core = lax.axis_index("row")
    first = left_half()
    for ref, part in ((near, core), (away, 1 - core)):
        rows = pl.ds(pl.multiple_of(part * hr, hr), hr)
        tile[:, rows, :half] = ref[first]
        tile[:, rows, half:] = ref[1 - first]


def vmem():
    return pl.BlockSpec(memory_space=pltpu.VMEM)


def call(kernel, outs, args, scratch=(), flops=0):
    size = sum(math.prod(a.shape) * a.dtype.itemsize for a in args)
    size += sum(math.prod(o) * 4 for o in outs)
    return pl.pallas_call(
        kernel,
        out_shape=[jax.ShapeDtypeStruct(o, f32) for o in outs],
        in_specs=[
            pl.BlockSpec(memory_space=pltpu.SMEM) if a.dtype == jnp.int32 else vmem() for a in args
        ],
        out_specs=[vmem() for _ in outs],
        scratch_shapes=list(scratch),
        cost_estimate=pl.CostEstimate(flops=flops, bytes_accessed=size, transcendentals=0),
        compiler_params=pltpu.CompilerParams(vmem_limit_bytes=40 * 1024 * 1024),
    )(*args)


def swap_rows(x):
    return lax.ppermute(x, "row", [(0, 1), (1, 0)])


def beside(x, inner, tiles):
    pairs = []
    for t in range(tiles):
        other = t + 1 if (t % 2 == 0) == inner else t - 1
        if 0 <= other < tiles and other // GX == t // GX:
            pairs.append((t, other))
    return lax.ppermute(x, "tile", pairs)


def swap_vertical(x, tiles):
    pairs = [(2 * t, 2 * (t - GX) + 1) for t in range(GX, tiles)]
    pairs += [(2 * t + 1, 2 * (t + GX)) for t in range(tiles - GX)]
    return lax.ppermute(x, ("tile", "row"), pairs)


def exchange(x, bit, tiles):
    return lax.ppermute(x, "tile", [(s, s ^ (1 << bit)) for s in range(tiles)])


def together(*groups):
    return lax.optimization_barrier(groups)


def halves(x, even, inner):
    half = x.shape[-1] // 2
    own_first = even == inner
    a, b = x[..., :half], x[..., half:]
    return jnp.where(own_first, a, b), jnp.where(own_first, b, a)


def joined(own, other, even, inner):
    own_first = even == inner
    return jnp.concatenate([jnp.where(own_first, own, other), jnp.where(own_first, other, own)], -1)


def window_parts(grad, even, wide):
    if wide:
        return [grad[0], grad[1]], [grad[0], grad[1]]
    return zip(*(halves(grad[k], even, k == 0) for k in range(2)))


def reduce_all(parts, grad, even, tiles, wide):
    bits = int(math.log2(tiles))
    stay, go = window_parts(grad, even, wide)
    held = list(parts)
    go, got = list(go), [None, None]
    for i in range(HALVINGS):
        n = held[0].shape[0] // 2
        held = [h[:n] + exchange(h[n:], o[i], tiles) for h, o in zip(held, ORDERS)]
        if i == 0:
            held, go[1] = together(held, go[1])
            got[1] = beside(go[1], False, tiles)
        else:
            held, go[0], got[1] = together(held, go[0], got[1])
            got[0] = beside(go[0], True, tiles)
    held = [h + exchange(h, o[-1], tiles) for h, o in zip(held, ORDERS)]
    held, got = together(held, got)
    for bit in range(len(ORDERS[0]), bits):
        held = [h + exchange(h, bit, tiles) for h in held]
    pieces = [[h] for h in held]
    for i in reversed(range(HALVINGS)):
        for p, o in zip(pieces, ORDERS):
            p.append(exchange(p[0] if len(p) == 1 else jnp.concatenate(p, 0), o[i], tiles))
        if i:
            (pieces,) = together(pieces)
    return pieces, jnp.stack([a + b for a, b in zip(stay, got)])


def per_device(object_tiles, probe_modes, amplitude, offsets, counts):
    own_tile = object_tiles[0]
    size = own_tile.shape[-1]
    frame = probe_modes.shape[-1]
    half = frame // 2
    tiles = lax.axis_size("tile")
    tall = tiles > GX
    slots = offsets.shape[0]
    modes = probe_modes.shape[0]
    core = lax.axis_index("row")
    even = lax.axis_index("tile") % 2 == 0
    hr = size // 2
    tab = jnp.asarray(tables(frame))
    perm = jnp.asarray(deinterleave(frame))
    coef = 4.0 / (slots * tiles)

    mine = lax.dynamic_slice(own_tile, (0, core * hr, 0), (2, hr, size))
    own = [jnp.where(even == inner, mine[:, :, half:], mine[:, :, :half]) for inner in (True, False)]
    got = [beside(own[1], False, tiles), beside(own[0], True, tiles)]
    (amp,) = call(amplitude_kernel, [amplitude.shape], [amplitude, perm])
    got, amp = together(got, amp)
    near = jnp.stack([joined(own[0], got[1], even, True), joined(own[1], got[0], even, False)])
    if tall:
        other = swap_vertical(near, tiles)
        near = jnp.where(core == 0, jnp.concatenate([other, near], 2), jnp.concatenate([near, other], 2))
    away = swap_rows(near)

    def scratch(count):
        return [pltpu.VMEM((count, 2, 2, frame, frame), bf16) for _ in range(2)]

    matmul = 4 * 2 * 3 * 4 * frame**3
    probe = probe_modes
    streams = None
    for iteration in range(ITERS):
        final = iteration + 1 == ITERS
        fars, powers, others, patches = [], [], [], []
        for s in range(slots):
            args = [offsets, near, away, probe, tab]
            outs = [(modes, 2, frame, frame), (frame, frame), (2, frame, frame)]
            count = 0
            if streams is not None:
                count = len(streams[0])
                args += [p for group in streams for p in group]
                outs.append(probe.shape)
                streams = None
            got = call(
                functools.partial(forward_kernel, s, count, coef, tall),
                outs,
                args,
                scratch(modes) + [pltpu.VMEM((modes, 2, frame, frame), f32)],
                matmul * modes,
            )
            if count:
                probe = got[3]
            fars.append(got[0])
            powers.append(got[1])
            patches.append(got[2])
            others.append(swap_rows(got[1]))
        before = factors = None
        parts = []
        for m in range(modes):
            last = m == modes - 1
            args = [offsets, counts, tab, amp, probe] + fars + patches
            args += [factors, before] if m else powers + others
            grads = (2,) + near.shape if last and not tall else (slots, 2, frame, frame)
            part = (CHUNKS, 2, frame // CHUNKS, frame)
            got = call(
                functools.partial(inverse_kernel, m, last, tall),
                [part, grads] if m else [part, grads, amp.shape],
                args,
                scratch(slots) + [pltpu.VMEM((slots, 2, frame, frame), f32) for _ in range(2)],
                matmul * slots,
            )
            parts.append(got[0])
            before = got[1]
            factors = got[2] if m == 0 else None
        if tall:
            (before,) = call(place_kernel, [(2,) + near.shape], [offsets, before])
        grad = before[0] + swap_rows(before[1])
        wide = tall or not final
        streams, total = reduce_all(parts, grad, even, tiles, wide)
        if tall:
            total = total + swap_vertical(total, tiles)
        if wide:
            near = near + total / MODES
        if final:
            near = jnp.stack([halves(near[k], even, k == 0)[0] for k in range(2)])
            if not wide:
                near = near + total / MODES
            if tall:
                near = jnp.where(core == 0, near[:, :, half:], near[:, :, : size - half])
        away = swap_rows(near)
    args = [near, away, probe] + [p for group in streams for p in group]
    tile, probe = call(
        functools.partial(finish_kernel, len(streams[0]), coef), [own_tile.shape, probe.shape], args
    )
    return (tile[None], probe)


def solution(mesh):
    return jax.shard_map(
        per_device,
        mesh=mesh,
        in_specs=(
            P(("scan", "tile"), None, None, None),
            P("row", None, None, None),
            P(("scan", "tile"), None, None),
            P(("scan", "tile"), None),
            P(("scan", "tile")),
        ),
        out_specs=(P(("scan", "tile"), None, None, None), P(("scan", "row"), None, None, None)),
        check_vma=False,
    )
```

```python
import functools
import math

import jax
import jax.numpy as jnp
import numpy as np
from jax import lax
from jax.experimental import pallas as pl
from jax.experimental.pallas import tpu as pltpu
from jax.sharding import PartitionSpec as P

MODES = 4
GX = 8
ITERS = 2
HALVINGS = 2
CHUNKS = 1 << HALVINGS
ORDERS = ((0, 1, 2), (1, 0, 2))
STRIP = 16
ORDERS = ((0, 1, 2), (1, 0, 2))

f32 = jnp.float32
bf16 = jnp.bfloat16


def tables(length):
    half = length // 2
    n = np.arange(half)
    out = []
    for odd in (0, 1):
        angle = 2.0 * math.pi * np.outer(2 * n + odd, n) / length
        c, s = np.cos(angle) / math.sqrt(length), np.sin(angle) / math.sqrt(length)
        out.append(np.block([[c, s], [-s, c]]))
    both = np.stack([np.stack(out), np.stack([m.T for m in out])]).astype(np.float32)
    high = both.astype(bf16)
    return np.stack([high, (both - high.astype(np.float32)).astype(bf16)], axis=2)


def deinterleave(length):
    half = length // 2
    out = np.zeros((length, length), np.float32)
    out[2 * np.arange(half), np.arange(half)] = 1.0
    out[2 * np.arange(half) + 1, half + np.arange(half)] = 1.0
    return np.stack([out, out.T]).astype(bf16)


def split(x):
    high = x.astype(bf16)
    return high, (x - high.astype(f32)).astype(bf16)


def dot(a, b):
    return jnp.dot(a, b, preferred_element_type=f32)


def mul_left(table, x):
    return dot(jnp.concatenate([table[0], table[1], table[0]], 1), jnp.concatenate([x[0], x[0], x[1]], 0))


def mul_right(x, table):
    return dot(jnp.concatenate([x[0], x[1], x[0]], 1), jnp.concatenate([table[0], table[0], table[1]], 0))


def put(ref, item, where, rows, x):
    for k, part in enumerate(split(x)):
        ref[item, where, k, rows, :] = part


def strips(count, body):
    for i in range(count):
        body(i)


def at(start, length=STRIP):
    return pl.ds(start if isinstance(start, int) else pl.multiple_of(start, STRIP), length)


def exact(x):
    high = x.astype(bf16)
    rest = x - high.astype(f32)
    mid = rest.astype(bf16)
    return high, mid, (rest - mid.astype(f32)).astype(bf16)


def amplitude_kernel(amp, perm, out):
    for s in range(amp.shape[0]):
        high, mid, low = exact(amp[s])
        rows = dot(perm[1], high) + (dot(perm[1], mid) + dot(perm[1], low))
        high, mid, low = exact(rows)
        out[s] = dot(high, perm[0]) + (dot(mid, perm[0]) + dot(low, perm[0]))


def chunk_key(order):
    t = lax.axis_index("tile")
    return sum(((t >> order[i]) & 1) << (HALVINGS - 1 - i) for i in range(HALVINGS))


def corner(offsets, slot, dim, size, margin):
    t = lax.axis_index("tile")
    along = lax.rem(t, GX) if dim else lax.div(t, GX)
    return offsets[slot, dim] - along * size + margin


def left_half():
    return 1 - lax.rem(lax.axis_index("tile"), 2)


def update_probe(old, streams, coef, out):
    rows = old.shape[2] // CHUNKS
    for mode, pieces in enumerate(streams):
        key = chunk_key(ORDERS[mode])
        rel = 0
        for piece in pieces:
            for k in range(piece.shape[0]):
                here = pl.ds(pl.multiple_of((rel ^ key) * rows, rows), rows)
                out[mode, :, here, :] = old[mode, :, here, :] + coef * piece[k]
                rel += 1


def grouped(refs, streams, per_stream):
    return [refs[i * per_stream : (i + 1) * per_stream] for i in range(streams)]


def shift_in(offsets, slot, near, away, patch, tall):
    frame = patch.shape[-1]
    h = frame // 2
    hr, cols = near.shape[2], 2 * near.shape[3]
    size = cols - 2 * h
    core = lax.axis_index("row")
    first = left_half()
    across = lax.rem(cols - corner(offsets, slot, 1, size, h), cols)

    def strip(ref, c, rows):
        x = jnp.concatenate([ref[first, c, rows, :], ref[1 - first, c, rows, :]], 1)
        return pltpu.roll(x, across, 1)[:, :frame]

    if tall:
        down = lax.rem(2 * hr - corner(offsets, slot, 0, size, h), 2 * hr)
        for c in range(2):
            halves = [strip(ref, c, slice(None)) for ref in (near, away)]
            both = [jnp.where(core == k, halves[0], halves[1]) for k in range(2)]
            patch[c] = pltpu.roll(jnp.concatenate(both, 0), down, 0)[:frame]
        return

    def body(j):
        for ref, half in ((near, core), (away, 1 - core)):
            for c in range(2):
                patch[c, at(half * hr + j * STRIP), :] = strip(ref, c, at(j * STRIP))

    strips(hr // STRIP, body)


def forward_kernel(slot, n_pieces, coef, tall, *refs):
    refs = list(refs)
    offsets, near, away, probe, tab = refs[:5]
    refs = refs[5:]
    modes = probe.shape[0]
    if n_pieces:
        streams = grouped(refs, modes, n_pieces)
        refs = refs[modes * n_pieces :]
        new_probe = refs.pop(3)
        update_probe(probe, streams, coef, new_probe)
        probe = new_probe
    far, power, patch, tall_parts, wide_parts, product = refs
    frame = probe.shape[-1]
    h = frame // 2
    shift_in(offsets, slot, near, away, patch, tall)

    def exits(m, j):
        pair = []
        for start in (j * STRIP, h + j * STRIP):
            rows = at(start)
            pr, pi = probe[m, 0, rows, :], probe[m, 1, rows, :]
            ar, ai = patch[0, rows, :], patch[1, rows, :]
            pair.append((pr * ar - pi * ai, pr * ai + pi * ar))
        for k in range(2):
            put(tall_parts, m, 0, at(k * h + j * STRIP), pair[0][k] + pair[1][k])
            put(tall_parts, m, 1, at(k * h + j * STRIP), pair[0][k] - pair[1][k])

    def columns(m, j):
        for p in range(2):
            y = [product[m, p, at(k * h + j * STRIP), :] for k in range(2)]
            rows = at(p * h + j * STRIP)
            put(wide_parts, m, 0, rows, jnp.concatenate([v[:, :h] + v[:, h:] for v in y], 1))
            put(wide_parts, m, 1, rows, jnp.concatenate([v[:, :h] - v[:, h:] for v in y], 1))

    for m in range(modes):
        strips(h // STRIP, functools.partial(exits, m))
        for p in range(2):
            product[m, p] = mul_left(tab[0, p], tall_parts[m, p])
    for m in range(modes):
        strips(h // STRIP, functools.partial(columns, m))
        for q in range(2):
            far[m, q] = mul_right(wide_parts[m, q], tab[1, q])

    def powers(j):
        rows = at(j * STRIP)
        for q in range(2):
            total = None
            for m in range(modes):
                f = far[m, q, rows, :]
                f = f * f
                f = f[:, :h] + f[:, h:]
                total = f if m == 0 else total + f
            power[rows, slice(q * h, (q + 1) * h)] = total

    strips(frame // STRIP, powers)


def inverse_kernel(mode, last, tall, *refs):
    refs = list(refs)
    offsets, counts, tab, amp, probe = refs[:5]
    refs = refs[5:]
    slots = amp.shape[0]
    fars, powers, others, patches = (refs[i * slots : (i + 1) * slots] for i in range(4))
    refs = refs[4 * slots :]
    before = refs.pop(0) if mode else None
    probe_grad, grads, tall_parts, wide_parts, product_wide, product_tall = refs
    frame = probe.shape[-1]
    h = frame // 2

    def factors(s, j):
        rows = at(j * STRIP)
        factor = amp[s, rows, :] / (jnp.sqrt(powers[s][rows, :] + others[s][rows, :]) + 0.5)
        for q in range(2):
            f = factor[:, q * h : (q + 1) * h]
            put(wide_parts, s, q, rows, fars[s][mode, q, rows, :] * jnp.concatenate([f, f], 1))

    def columns(s, j):
        for p in range(2):
            he, ho = (product_wide[s, q, at(p * h + j * STRIP), :] for q in range(2))
            for k in range(2):
                a, b = he[:, k * h : (k + 1) * h], ho[:, k * h : (k + 1) * h]
                put(tall_parts, s, p, at(k * h + j * STRIP), jnp.concatenate([a + b, a - b], 1))

    for s in range(slots):
        strips(frame // STRIP, functools.partial(factors, s))
        for q in range(2):
            product_wide[s, q] = mul_right(wide_parts[s, q], tab[0, q])
    for s in range(slots):
        strips(h // STRIP, functools.partial(columns, s))
        for p in range(2):
            product_tall[s, p] = mul_left(tab[1, p], tall_parts[s, p])
    key = chunk_key(ORDERS[mode])
    chunk = frame // CHUNKS
    core = lax.axis_index("row")
    first = left_half()

    def results(j):
        x = [
            [[product_tall[s, p, at(k * h + j * STRIP), :] for k in range(2)] for p in range(2)]
            for s in range(slots)
        ]
        for lower in range(2):
            rows = at(lower * h + j * STRIP)
            pr, pi = probe[mode, 0, rows, :], probe[mode, 1, rows, :]
            step = [None, None]
            window = [None, None]
            for s in range(slots):
                even, odd = x[s]
                xr, xi = (even[k] - odd[k] if lower else even[k] + odd[k] for k in range(2))
                live = (s < counts[0]).astype(f32)
                ar, ai = patches[s][0, rows, :], patches[s][1, rows, :]
                ur = (xr - (pr * ar - pi * ai)) * live
                ui = (xi - (pr * ai + pi * ar)) * live
                for k, g in enumerate((ar * ur + ai * ui, ar * ui - ai * ur)):
                    step[k] = g if s == 0 else step[k] + g
                for k, g in enumerate((pr * ur + pi * ui, pr * ui - pi * ur)):
                    if mode:
                        g = g + before[s, k, rows, :]
                    if not last or tall:
                        grads[s, k, rows, :] = g
                        continue
                    wide = 2 * grads.shape[-1]
                    g = jnp.concatenate([g, jnp.zeros((STRIP, wide - frame), f32)], 1)
                    g = pltpu.roll(g, corner(offsets, s, 1, wide - 2 * h, h), 1)
                    window[k] = g if s == 0 else window[k] + g
            start = lower * h + j * STRIP
            for k in range(2):
                probe_grad[(start // chunk) ^ key, k, at(start % chunk), :] = step[k]
                if last and not tall:
                    half = window[k].shape[1] // 2
                    grads[lower ^ core, first, k, at(j * STRIP), :] = window[k][:, :half]
                    grads[lower ^ core, 1 - first, k, at(j * STRIP), :] = window[k][:, half:]

    strips(h // STRIP, results)


def place_kernel(offsets, grads, out):
    slots, _, frame, _ = grads.shape
    _, _, _, hr, half = out.shape
    cols = 2 * half
    h = frame // 2
    size = cols - 2 * h
    core = lax.axis_index("row")
    first = left_half()
    for c in range(2):
        total = None
        for s in range(slots):
            g = jnp.concatenate([grads[s, c], jnp.zeros((2 * hr - frame, frame), f32)], 0)
            g = pltpu.roll(g, corner(offsets, s, 0, size, h), 0)
            g = jnp.concatenate([g, jnp.zeros((2 * hr, cols - frame), f32)], 1)
            g = pltpu.roll(g, corner(offsets, s, 1, size, h), 1)
            total = g if s == 0 else total + g
        for k in range(2):
            out[k ^ core, first, c] = total[k * hr : (k + 1) * hr, :half]
            out[k ^ core, 1 - first, c] = total[k * hr : (k + 1) * hr, half:]


def finish_kernel(n_pieces, coef, *refs):
    refs = list(refs)
    near, away, probe = refs[:3]
    streams = grouped(refs[3:], probe.shape[0], n_pieces)
    tile, new_probe = refs[-2:]
    update_probe(probe, streams, coef, new_probe)
    _, _, hr, half = near.shape
    core = lax.axis_index("row")
    first = left_half()
    for ref, part in ((near, core), (away, 1 - core)):
        rows = pl.ds(pl.multiple_of(part * hr, hr), hr)
        tile[:, rows, :half] = ref[first]
        tile[:, rows, half:] = ref[1 - first]


def vmem():
    return pl.BlockSpec(memory_space=pltpu.VMEM)


def call(kernel, outs, args, scratch=(), flops=0):
    size = sum(math.prod(a.shape) * a.dtype.itemsize for a in args)
    size += sum(math.prod(o) * 4 for o in outs)
    return pl.pallas_call(
        kernel,
        out_shape=[jax.ShapeDtypeStruct(o, f32) for o in outs],
        in_specs=[
            pl.BlockSpec(memory_space=pltpu.SMEM) if a.dtype == jnp.int32 else vmem() for a in args
        ],
        out_specs=[vmem() for _ in outs],
        scratch_shapes=list(scratch),
        cost_estimate=pl.CostEstimate(flops=flops, bytes_accessed=size, transcendentals=0),
        compiler_params=pltpu.CompilerParams(vmem_limit_bytes=40 * 1024 * 1024),
    )(*args)


def swap_rows(x):
    return lax.ppermute(x, "row", [(0, 1), (1, 0)])


def beside(x, inner, tiles):
    pairs = []
    for t in range(tiles):
        other = t + 1 if (t % 2 == 0) == inner else t - 1
        if 0 <= other < tiles and other // GX == t // GX:
            pairs.append((t, other))
    return lax.ppermute(x, "tile", pairs)


def swap_vertical(x, tiles):
    pairs = [(2 * t, 2 * (t - GX) + 1) for t in range(GX, tiles)]
    pairs += [(2 * t + 1, 2 * (t + GX)) for t in range(tiles - GX)]
    return lax.ppermute(x, ("tile", "row"), pairs)


def exchange(x, bit, tiles):
    return lax.ppermute(x, "tile", [(s, s ^ (1 << bit)) for s in range(tiles)])


def together(*groups):
    return lax.optimization_barrier(groups)


def halves(x, even, inner):
    half = x.shape[-1] // 2
    own_first = even == inner
    a, b = x[..., :half], x[..., half:]
    return jnp.where(own_first, a, b), jnp.where(own_first, b, a)


def joined(own, other, even, inner):
    own_first = even == inner
    return jnp.concatenate([jnp.where(own_first, own, other), jnp.where(own_first, other, own)], -1)


def window_parts(grad, even, wide):
    if wide:
        return [grad[0], grad[1]], [grad[0], grad[1]]
    return zip(*(halves(grad[k], even, k == 0) for k in range(2)))


def reduce_all(parts, grad, even, tiles, wide):
    bits = int(math.log2(tiles))
    stay, go = window_parts(grad, even, wide)
    held = list(parts)
    go, got = list(go), [None, None]
    for i in range(HALVINGS):
        n = held[0].shape[0] // 2
        held = [h[:n] + exchange(h[n:], o[i], tiles) for h, o in zip(held, ORDERS)]
        if i == 0:
            held, go[1] = together(held, go[1])
            got[1] = beside(go[1], False, tiles)
        else:
            (held,) = together(held)
    held = [h + exchange(h, o[-1], tiles) for h, o in zip(held, ORDERS)]
    held, go[0], got[1] = together(held, go[0], got[1])
    got[0] = beside(go[0], True, tiles)
    for bit in range(len(ORDERS[0]), bits):
        held = [h + exchange(h, bit, tiles) for h in held]
    pieces = [[h] for h in held]
    for i in reversed(range(HALVINGS)):
        for p, o in zip(pieces, ORDERS):
            p.append(exchange(p[0] if len(p) == 1 else jnp.concatenate(p, 0), o[i], tiles))
        if i:
            pieces, got = together(pieces, got)
    return pieces, jnp.stack([a + b for a, b in zip(stay, got)])


def per_device(object_tiles, probe_modes, amplitude, offsets, counts):
    own_tile = object_tiles[0]
    size = own_tile.shape[-1]
    frame = probe_modes.shape[-1]
    half = frame // 2
    tiles = lax.axis_size("tile")
    tall = tiles > GX
    slots = offsets.shape[0]
    modes = probe_modes.shape[0]
    core = lax.axis_index("row")
    even = lax.axis_index("tile") % 2 == 0
    hr = size // 2
    tab = jnp.asarray(tables(frame))
    perm = jnp.asarray(deinterleave(frame))
    coef = 4.0 / (slots * tiles)

    mine = lax.dynamic_slice(own_tile, (0, core * hr, 0), (2, hr, size))
    own = [jnp.where(even == inner, mine[:, :, half:], mine[:, :, :half]) for inner in (True, False)]
    got = [beside(own[1], False, tiles), beside(own[0], True, tiles)]
    near = jnp.stack([joined(own[0], got[1], even, True), joined(own[1], got[0], even, False)])
    if tall:
        other = swap_vertical(near, tiles)
        near = jnp.where(core == 0, jnp.concatenate([other, near], 2), jnp.concatenate([near, other], 2))
    (amp,) = call(amplitude_kernel, [amplitude.shape], [amplitude, perm])
    away = swap_rows(near)
    near, away, amp = together(near, away, amp)

    def scratch(count):
        return [pltpu.VMEM((count, 2, 2, frame, frame), bf16) for _ in range(2)]

    matmul = 4 * 2 * 3 * 4 * frame**3
    probe = probe_modes
    streams = None
    for iteration in range(ITERS):
        final = iteration + 1 == ITERS
        fars, powers, others, patches = [], [], [], []
        for s in range(slots):
            args = [offsets, near, away, probe, tab]
            outs = [(modes, 2, frame, frame), (frame, frame), (2, frame, frame)]
            count = 0
            if streams is not None:
                count = len(streams[0])
                args += [p for group in streams for p in group]
                outs.append(probe.shape)
                streams = None
            got = call(
                functools.partial(forward_kernel, s, count, coef, tall),
                outs,
                args,
                scratch(modes) + [pltpu.VMEM((modes, 2, frame, frame), f32)],
                matmul * modes,
            )
            if count:
                probe = got[3]
            fars.append(got[0])
            powers.append(got[1])
            patches.append(got[2])
            others.append(swap_rows(got[1]))
        before = None
        parts = []
        for m in range(modes):
            last = m == modes - 1
            args = [offsets, counts, tab, amp, probe] + fars + powers + others + patches
            if m:
                args.append(before)
            grads = (2,) + near.shape if last and not tall else (slots, 2, frame, frame)
            part = (CHUNKS, 2, frame // CHUNKS, frame)
            got = call(
                functools.partial(inverse_kernel, m, last, tall),
                [part, grads],
                args,
                scratch(slots) + [pltpu.VMEM((slots, 2, frame, frame), f32) for _ in range(2)],
                matmul * slots,
            )
            parts.append(got[0])
            before = got[1]
        if tall:
            (before,) = call(place_kernel, [(2,) + near.shape], [offsets, before])
        grad = before[0] + swap_rows(before[1])
        wide = tall or not final
        streams, total = reduce_all(parts, grad, even, tiles, wide)
        if tall:
            total = total + swap_vertical(total, tiles)
        if wide:
            near = near + total / MODES
        if final:
            near = jnp.stack([halves(near[k], even, k == 0)[0] for k in range(2)])
            if not wide:
                near = near + total / MODES
            if tall:
                near = jnp.where(core == 0, near[:, :, half:], near[:, :, : size - half])
        away = swap_rows(near)
    args = [near, away, probe] + [p for group in streams for p in group]
    tile, probe = call(
        functools.partial(finish_kernel, len(streams[0]), coef), [own_tile.shape, probe.shape], args
    )
    return (tile[None], probe)


def solution(mesh):
    return jax.shard_map(
        per_device,
        mesh=mesh,
        in_specs=(
            P(("scan", "tile"), None, None, None),
            P("row", None, None, None),
            P(("scan", "tile"), None, None),
            P(("scan", "tile"), None),
            P(("scan", "tile")),
        ),
        out_specs=(P(("scan", "tile"), None, None, None), P(("scan", "row"), None, None, None)),
        check_vma=False,
    )
```

```python
import functools
import math

import jax
import jax.numpy as jnp
import numpy as np
from jax import lax
from jax.experimental import pallas as pl
from jax.experimental.pallas import tpu as pltpu
from jax.sharding import PartitionSpec as P

MODES = 4
GX = 8
ITERS = 2
HALVINGS = 2
CHUNKS = 1 << HALVINGS
ORDERS = ((0, 1, 2), (1, 2, 0))
STRIP = 16
ORDERS = ((0, 1, 2), (1, 2, 0))

f32 = jnp.float32
bf16 = jnp.bfloat16


def tables(length):
    half = length // 2
    n = np.arange(half)
    out = []
    for odd in (0, 1):
        angle = 2.0 * math.pi * np.outer(2 * n + odd, n) / length
        c, s = np.cos(angle) / math.sqrt(length), np.sin(angle) / math.sqrt(length)
        out.append(np.block([[c, s], [-s, c]]))
    both = np.stack([np.stack(out), np.stack([m.T for m in out])]).astype(np.float32)
    high = both.astype(bf16)
    return np.stack([high, (both - high.astype(np.float32)).astype(bf16)], axis=2)


def deinterleave(length):
    half = length // 2
    out = np.zeros((length, length), np.float32)
    out[2 * np.arange(half), np.arange(half)] = 1.0
    out[2 * np.arange(half) + 1, half + np.arange(half)] = 1.0
    return np.stack([out, out.T]).astype(bf16)


def split(x):
    high = x.astype(bf16)
    return high, (x - high.astype(f32)).astype(bf16)


def dot(a, b):
    return jnp.dot(a, b, preferred_element_type=f32)


def mul_left(table, x):
    return dot(jnp.concatenate([table[0], table[1], table[0]], 1), jnp.concatenate([x[0], x[0], x[1]], 0))


def mul_right(x, table):
    return dot(jnp.concatenate([x[0], x[1], x[0]], 1), jnp.concatenate([table[0], table[0], table[1]], 0))


def put(ref, item, where, rows, x):
    for k, part in enumerate(split(x)):
        ref[item, where, k, rows, :] = part


def strips(count, body):
    for i in range(count):
        body(i)


def at(start, length=STRIP):
    return pl.ds(start if isinstance(start, int) else pl.multiple_of(start, STRIP), length)


def exact(x):
    high = x.astype(bf16)
    rest = x - high.astype(f32)
    mid = rest.astype(bf16)
    return high, mid, (rest - mid.astype(f32)).astype(bf16)


def amplitude_kernel(amp, perm, out):
    for s in range(amp.shape[0]):
        high, mid, low = exact(amp[s])
        rows = dot(perm[1], high) + (dot(perm[1], mid) + dot(perm[1], low))
        high, mid, low = exact(rows)
        out[s] = dot(high, perm[0]) + (dot(mid, perm[0]) + dot(low, perm[0]))


def chunk_key(order):
    t = lax.axis_index("tile")
    return sum(((t >> order[i]) & 1) << (HALVINGS - 1 - i) for i in range(HALVINGS))


def corner(offsets, slot, dim, size, margin):
    t = lax.axis_index("tile")
    along = lax.rem(t, GX) if dim else lax.div(t, GX)
    return offsets[slot, dim] - along * size + margin


def left_half():
    return 1 - lax.rem(lax.axis_index("tile"), 2)


def update_probe(old, streams, coef, out):
    rows = old.shape[2] // CHUNKS
    for mode, pieces in enumerate(streams):
        key = chunk_key(ORDERS[mode])
        rel = 0
        for piece in pieces:
            for k in range(piece.shape[0]):
                here = pl.ds(pl.multiple_of((rel ^ key) * rows, rows), rows)
                out[mode, :, here, :] = old[mode, :, here, :] + coef * piece[k]
                rel += 1


def grouped(refs, streams, per_stream):
    return [refs[i * per_stream : (i + 1) * per_stream] for i in range(streams)]


def shift_in(offsets, slot, near, away, patch, tall):
    frame = patch.shape[-1]
    h = frame // 2
    hr, cols = near.shape[2], 2 * near.shape[3]
    size = cols - 2 * h
    core = lax.axis_index("row")
    first = left_half()
    across = lax.rem(cols - corner(offsets, slot, 1, size, h), cols)

    def strip(ref, c, rows):
        x = jnp.concatenate([ref[first, c, rows, :], ref[1 - first, c, rows, :]], 1)
        return pltpu.roll(x, across, 1)[:, :frame]

    if tall:
        down = lax.rem(2 * hr - corner(offsets, slot, 0, size, h), 2 * hr)
        for c in range(2):
            halves = [strip(ref, c, slice(None)) for ref in (near, away)]
            both = [jnp.where(core == k, halves[0], halves[1]) for k in range(2)]
            patch[c] = pltpu.roll(jnp.concatenate(both, 0), down, 0)[:frame]
        return

    def body(j):
        for ref, half in ((near, core), (away, 1 - core)):
            for c in range(2):
                patch[c, at(half * hr + j * STRIP), :] = strip(ref, c, at(j * STRIP))

    strips(hr // STRIP, body)


def forward_kernel(slot, n_pieces, coef, tall, *refs):
    refs = list(refs)
    offsets, near, away, probe, tab = refs[:5]
    refs = refs[5:]
    modes = probe.shape[0]
    if n_pieces:
        streams = grouped(refs, modes, n_pieces)
        refs = refs[modes * n_pieces :]
        new_probe = refs.pop(3)
        update_probe(probe, streams, coef, new_probe)
        probe = new_probe
    far, power, patch, tall_parts, wide_parts, product = refs
    frame = probe.shape[-1]
    h = frame // 2
    shift_in(offsets, slot, near, away, patch, tall)

    def exits(m, j):
        pair = []
        for start in (j * STRIP, h + j * STRIP):
            rows = at(start)
            pr, pi = probe[m, 0, rows, :], probe[m, 1, rows, :]
            ar, ai = patch[0, rows, :], patch[1, rows, :]
            pair.append((pr * ar - pi * ai, pr * ai + pi * ar))
        for k in range(2):
            put(tall_parts, m, 0, at(k * h + j * STRIP), pair[0][k] + pair[1][k])
            put(tall_parts, m, 1, at(k * h + j * STRIP), pair[0][k] - pair[1][k])

    def columns(m, j):
        for p in range(2):
            y = [product[m, p, at(k * h + j * STRIP), :] for k in range(2)]
            rows = at(p * h + j * STRIP)
            put(wide_parts, m, 0, rows, jnp.concatenate([v[:, :h] + v[:, h:] for v in y], 1))
            put(wide_parts, m, 1, rows, jnp.concatenate([v[:, :h] - v[:, h:] for v in y], 1))

    for m in range(modes):
        strips(h // STRIP, functools.partial(exits, m))
        for p in range(2):
            product[m, p] = mul_left(tab[0, p], tall_parts[m, p])
    for m in range(modes):
        strips(h // STRIP, functools.partial(columns, m))
        for q in range(2):
            far[m, q] = mul_right(wide_parts[m, q], tab[1, q])

    def powers(j):
        rows = at(j * STRIP)
        for q in range(2):
            total = None
            for m in range(modes):
                f = far[m, q, rows, :]
                f = f * f
                f = f[:, :h] + f[:, h:]
                total = f if m == 0 else total + f
            power[rows, slice(q * h, (q + 1) * h)] = total

    strips(frame // STRIP, powers)


def inverse_kernel(mode, last, tall, *refs):
    refs = list(refs)
    offsets, counts, tab, amp, probe = refs[:5]
    refs = refs[5:]
    slots = amp.shape[0]
    fars, powers, others, patches = (refs[i * slots : (i + 1) * slots] for i in range(4))
    refs = refs[4 * slots :]
    before = refs.pop(0) if mode else None
    probe_grad, grads, tall_parts, wide_parts, product_wide, product_tall = refs
    frame = probe.shape[-1]
    h = frame // 2

    def factors(s, j):
        rows = at(j * STRIP)
        factor = amp[s, rows, :] / (jnp.sqrt(powers[s][rows, :] + others[s][rows, :]) + 0.5)
        for q in range(2):
            f = factor[:, q * h : (q + 1) * h]
            put(wide_parts, s, q, rows, fars[s][mode, q, rows, :] * jnp.concatenate([f, f], 1))

    def columns(s, j):
        for p in range(2):
            he, ho = (product_wide[s, q, at(p * h + j * STRIP), :] for q in range(2))
            for k in range(2):
                a, b = he[:, k * h : (k + 1) * h], ho[:, k * h : (k + 1) * h]
                put(tall_parts, s, p, at(k * h + j * STRIP), jnp.concatenate([a + b, a - b], 1))

    for s in range(slots):
        strips(frame // STRIP, functools.partial(factors, s))
        for q in range(2):
            product_wide[s, q] = mul_right(wide_parts[s, q], tab[0, q])
    for s in range(slots):
        strips(h // STRIP, functools.partial(columns, s))
        for p in range(2):
            product_tall[s, p] = mul_left(tab[1, p], tall_parts[s, p])
    key = chunk_key(ORDERS[mode])
    chunk = frame // CHUNKS
    core = lax.axis_index("row")
    first = left_half()

    def results(j):
        x = [
            [[product_tall[s, p, at(k * h + j * STRIP), :] for k in range(2)] for p in range(2)]
            for s in range(slots)
        ]
        for lower in range(2):
            rows = at(lower * h + j * STRIP)
            pr, pi = probe[mode, 0, rows, :], probe[mode, 1, rows, :]
            step = [None, None]
            window = [None, None]
            for s in range(slots):
                even, odd = x[s]
                xr, xi = (even[k] - odd[k] if lower else even[k] + odd[k] for k in range(2))
                live = (s < counts[0]).astype(f32)
                ar, ai = patches[s][0, rows, :], patches[s][1, rows, :]
                ur = (xr - (pr * ar - pi * ai)) * live
                ui = (xi - (pr * ai + pi * ar)) * live
                for k, g in enumerate((ar * ur + ai * ui, ar * ui - ai * ur)):
                    step[k] = g if s == 0 else step[k] + g
                for k, g in enumerate((pr * ur + pi * ui, pr * ui - pi * ur)):
                    if mode:
                        g = g + before[s, k, rows, :]
                    if not last or tall:
                        grads[s, k, rows, :] = g
                        continue
                    wide = 2 * grads.shape[-1]
                    g = jnp.concatenate([g, jnp.zeros((STRIP, wide - frame), f32)], 1)
                    g = pltpu.roll(g, corner(offsets, s, 1, wide - 2 * h, h), 1)
                    window[k] = g if s == 0 else window[k] + g
            start = lower * h + j * STRIP
            for k in range(2):
                probe_grad[(start // chunk) ^ key, k, at(start % chunk), :] = step[k]
                if last and not tall:
                    half = window[k].shape[1] // 2
                    grads[lower ^ core, first, k, at(j * STRIP), :] = window[k][:, :half]
                    grads[lower ^ core, 1 - first, k, at(j * STRIP), :] = window[k][:, half:]

    strips(h // STRIP, results)


def place_kernel(offsets, grads, out):
    slots, _, frame, _ = grads.shape
    _, _, _, hr, half = out.shape
    cols = 2 * half
    h = frame // 2
    size = cols - 2 * h
    core = lax.axis_index("row")
    first = left_half()
    for c in range(2):
        total = None
        for s in range(slots):
            g = jnp.concatenate([grads[s, c], jnp.zeros((2 * hr - frame, frame), f32)], 0)
            g = pltpu.roll(g, corner(offsets, s, 0, size, h), 0)
            g = jnp.concatenate([g, jnp.zeros((2 * hr, cols - frame), f32)], 1)
            g = pltpu.roll(g, corner(offsets, s, 1, size, h), 1)
            total = g if s == 0 else total + g
        for k in range(2):
            out[k ^ core, first, c] = total[k * hr : (k + 1) * hr, :half]
            out[k ^ core, 1 - first, c] = total[k * hr : (k + 1) * hr, half:]


def finish_kernel(n_pieces, coef, *refs):
    refs = list(refs)
    near, away, probe = refs[:3]
    streams = grouped(refs[3:], probe.shape[0], n_pieces)
    tile, new_probe = refs[-2:]
    update_probe(probe, streams, coef, new_probe)
    _, _, hr, half = near.shape
    core = lax.axis_index("row")
    first = left_half()
    for ref, part in ((near, core), (away, 1 - core)):
        rows = pl.ds(pl.multiple_of(part * hr, hr), hr)
        tile[:, rows, :half] = ref[first]
        tile[:, rows, half:] = ref[1 - first]


def vmem():
    return pl.BlockSpec(memory_space=pltpu.VMEM)


def call(kernel, outs, args, scratch=(), flops=0):
    size = sum(math.prod(a.shape) * a.dtype.itemsize for a in args)
    size += sum(math.prod(o) * 4 for o in outs)
    return pl.pallas_call(
        kernel,
        out_shape=[jax.ShapeDtypeStruct(o, f32) for o in outs],
        in_specs=[
            pl.BlockSpec(memory_space=pltpu.SMEM) if a.dtype == jnp.int32 else vmem() for a in args
        ],
        out_specs=[vmem() for _ in outs],
        scratch_shapes=list(scratch),
        cost_estimate=pl.CostEstimate(flops=flops, bytes_accessed=size, transcendentals=0),
        compiler_params=pltpu.CompilerParams(vmem_limit_bytes=40 * 1024 * 1024),
    )(*args)


def swap_rows(x):
    return lax.ppermute(x, "row", [(0, 1), (1, 0)])


def beside(x, inner, tiles):
    pairs = []
    for t in range(tiles):
        other = t + 1 if (t % 2 == 0) == inner else t - 1
        if 0 <= other < tiles and other // GX == t // GX:
            pairs.append((t, other))
    return lax.ppermute(x, "tile", pairs)


def swap_vertical(x, tiles):
    pairs = [(2 * t, 2 * (t - GX) + 1) for t in range(GX, tiles)]
    pairs += [(2 * t + 1, 2 * (t + GX)) for t in range(tiles - GX)]
    return lax.ppermute(x, ("tile", "row"), pairs)


def exchange(x, bit, tiles):
    return lax.ppermute(x, "tile", [(s, s ^ (1 << bit)) for s in range(tiles)])


def together(*groups):
    return lax.optimization_barrier(groups)


def halves(x, even, inner):
    half = x.shape[-1] // 2
    own_first = even == inner
    a, b = x[..., :half], x[..., half:]
    return jnp.where(own_first, a, b), jnp.where(own_first, b, a)


def joined(own, other, even, inner):
    own_first = even == inner
    return jnp.concatenate([jnp.where(own_first, own, other), jnp.where(own_first, other, own)], -1)


def window_parts(grad, even, wide):
    if wide:
        return [grad[0], grad[1]], [grad[0], grad[1]]
    return zip(*(halves(grad[k], even, k == 0) for k in range(2)))


def reduce_all(parts, grad, even, tiles, wide):
    bits = int(math.log2(tiles))
    stay, go = window_parts(grad, even, wide)
    held = list(parts)
    go, got = list(go), [None, None]
    for i in range(HALVINGS):
        n = held[0].shape[0] // 2
        held = [h[:n] + exchange(h[n:], o[i], tiles) for h, o in zip(held, ORDERS)]
        held, go[1 - i] = together(held, go[1 - i])
        got[1 - i] = beside(go[1 - i], i == 1, tiles)
    held = [h + exchange(h, o[-1], tiles) for h, o in zip(held, ORDERS)]
    held, got = together(held, got)
    for bit in range(len(ORDERS[0]), bits):
        held = [h + exchange(h, bit, tiles) for h in held]
    pieces = [[h] for h in held]
    for i in reversed(range(HALVINGS)):
        for p, o in zip(pieces, ORDERS):
            p.append(exchange(p[0] if len(p) == 1 else jnp.concatenate(p, 0), o[i], tiles))
        if i:
            (pieces,) = together(pieces)
    return pieces, jnp.stack([a + b for a, b in zip(stay, got)])


def per_device(object_tiles, probe_modes, amplitude, offsets, counts):
    own_tile = object_tiles[0]
    size = own_tile.shape[-1]
    frame = probe_modes.shape[-1]
    half = frame // 2
    tiles = lax.axis_size("tile")
    tall = tiles > GX
    slots = offsets.shape[0]
    modes = probe_modes.shape[0]
    core = lax.axis_index("row")
    even = lax.axis_index("tile") % 2 == 0
    hr = size // 2
    tab = jnp.asarray(tables(frame))
    perm = jnp.asarray(deinterleave(frame))
    coef = 4.0 / (slots * tiles)

    mine = lax.dynamic_slice(own_tile, (0, core * hr, 0), (2, hr, size))
    own = [jnp.where(even == inner, mine[:, :, half:], mine[:, :, :half]) for inner in (True, False)]
    got = [beside(own[1], False, tiles), beside(own[0], True, tiles)]
    near = jnp.stack([joined(own[0], got[1], even, True), joined(own[1], got[0], even, False)])
    if tall:
        other = swap_vertical(near, tiles)
        near = jnp.where(core == 0, jnp.concatenate([other, near], 2), jnp.concatenate([near, other], 2))
    (amp,) = call(amplitude_kernel, [amplitude.shape], [amplitude, perm])
    away = swap_rows(near)
    near, away, amp = together(near, away, amp)

    def scratch(count):
        return [pltpu.VMEM((count, 2, 2, frame, frame), bf16) for _ in range(2)]

    matmul = 4 * 2 * 3 * 4 * frame**3
    probe = probe_modes
    streams = None
    for iteration in range(ITERS):
        final = iteration + 1 == ITERS
        fars, powers, others, patches = [], [], [], []
        for s in range(slots):
            args = [offsets, near, away, probe, tab]
            outs = [(modes, 2, frame, frame), (frame, frame), (2, frame, frame)]
            count = 0
            if streams is not None:
                count = len(streams[0])
                args += [p for group in streams for p in group]
                outs.append(probe.shape)
                streams = None
            got = call(
                functools.partial(forward_kernel, s, count, coef, tall),
                outs,
                args,
                scratch(modes) + [pltpu.VMEM((modes, 2, frame, frame), f32)],
                matmul * modes,
            )
            if count:
                probe = got[3]
            fars.append(got[0])
            powers.append(got[1])
            patches.append(got[2])
            others.append(swap_rows(got[1]))
        before = None
        parts = []
        for m in range(modes):
            last = m == modes - 1
            args = [offsets, counts, tab, amp, probe] + fars + powers + others + patches
            if m:
                args.append(before)
            grads = (2,) + near.shape if last and not tall else (slots, 2, frame, frame)
            part = (CHUNKS, 2, frame // CHUNKS, frame)
            got = call(
                functools.partial(inverse_kernel, m, last, tall),
                [part, grads],
                args,
                scratch(slots) + [pltpu.VMEM((slots, 2, frame, frame), f32) for _ in range(2)],
                matmul * slots,
            )
            parts.append(got[0])
            before = got[1]
        if tall:
            (before,) = call(place_kernel, [(2,) + near.shape], [offsets, before])
        grad = before[0] + swap_rows(before[1])
        wide = tall or not final
        streams, total = reduce_all(parts, grad, even, tiles, wide)
        if tall:
            total = total + swap_vertical(total, tiles)
        if wide:
            near = near + total / MODES
        if final:
            near = jnp.stack([halves(near[k], even, k == 0)[0] for k in range(2)])
            if not wide:
                near = near + total / MODES
            if tall:
                near = jnp.where(core == 0, near[:, :, half:], near[:, :, : size - half])
        away = swap_rows(near)
    args = [near, away, probe] + [p for group in streams for p in group]
    tile, probe = call(
        functools.partial(finish_kernel, len(streams[0]), coef), [own_tile.shape, probe.shape], args
    )
    return (tile[None], probe)


def solution(mesh):
    return jax.shard_map(
        per_device,
        mesh=mesh,
        in_specs=(
            P(("scan", "tile"), None, None, None),
            P("row", None, None, None),
            P(("scan", "tile"), None, None),
            P(("scan", "tile"), None),
            P(("scan", "tile")),
        ),
        out_specs=(P(("scan", "tile"), None, None, None), P(("scan", "row"), None, None, None)),
        check_vma=False,
    )
```

```python
import functools
import math

import jax
import jax.numpy as jnp
import numpy as np
from jax import lax
from jax.experimental import pallas as pl
from jax.experimental.pallas import tpu as pltpu
from jax.sharding import PartitionSpec as P

MODES = 4
GX = 8
ITERS = 2
HALVINGS = 2
CHUNKS = 1 << HALVINGS
ORDERS = ((0, 1, 2), (1, 0, 2))
STRIP = 16
ORDERS = ((0, 1, 2), (1, 0, 2))

f32 = jnp.float32
bf16 = jnp.bfloat16


def tables(length):
    half = length // 2
    n = np.arange(half)
    out = []
    for odd in (0, 1):
        angle = 2.0 * math.pi * np.outer(2 * n + odd, n) / length
        c, s = np.cos(angle) / math.sqrt(length), np.sin(angle) / math.sqrt(length)
        out.append(np.block([[c, s], [-s, c]]))
    both = np.stack([np.stack(out), np.stack([m.T for m in out])]).astype(np.float32)
    high = both.astype(bf16)
    return np.stack([high, (both - high.astype(np.float32)).astype(bf16)], axis=2)


def deinterleave(length):
    half = length // 2
    out = np.zeros((length, length), np.float32)
    out[2 * np.arange(half), np.arange(half)] = 1.0
    out[2 * np.arange(half) + 1, half + np.arange(half)] = 1.0
    return np.stack([out, out.T]).astype(bf16)


def split(x):
    high = x.astype(bf16)
    return high, (x - high.astype(f32)).astype(bf16)


def dot(a, b):
    return jnp.dot(a, b, preferred_element_type=f32)


def mul_left(table, x):
    return dot(jnp.concatenate([table[0], table[1], table[0]], 1), jnp.concatenate([x[0], x[0], x[1]], 0))


def mul_right(x, table):
    return dot(jnp.concatenate([x[0], x[1], x[0]], 1), jnp.concatenate([table[0], table[0], table[1]], 0))


def put(ref, item, where, rows, x):
    for k, part in enumerate(split(x)):
        ref[item, where, k, rows, :] = part


def strips(count, body):
    for i in range(count):
        body(i)


def at(start, length=STRIP):
    return pl.ds(start if isinstance(start, int) else pl.multiple_of(start, STRIP), length)


def exact(x):
    high = x.astype(bf16)
    rest = x - high.astype(f32)
    mid = rest.astype(bf16)
    return high, mid, (rest - mid.astype(f32)).astype(bf16)


def amplitude_kernel(amp, perm, out):
    for s in range(amp.shape[0]):
        high, mid, low = exact(amp[s])
        rows = dot(perm[1], high) + (dot(perm[1], mid) + dot(perm[1], low))
        high, mid, low = exact(rows)
        out[s] = dot(high, perm[0]) + (dot(mid, perm[0]) + dot(low, perm[0]))


def chunk_key(order):
    t = lax.axis_index("tile")
    return sum(((t >> order[i]) & 1) << (HALVINGS - 1 - i) for i in range(HALVINGS))


def corner(offsets, slot, dim, size, margin):
    t = lax.axis_index("tile")
    along = lax.rem(t, GX) if dim else lax.div(t, GX)
    return offsets[slot, dim] - along * size + margin


def left_half():
    return 1 - lax.rem(lax.axis_index("tile"), 2)


def update_probe(old, streams, coef, out):
    rows = old.shape[2] // CHUNKS
    for mode, pieces in enumerate(streams):
        key = chunk_key(ORDERS[mode])
        rel = 0
        for piece in pieces:
            for k in range(piece.shape[0]):
                here = pl.ds(pl.multiple_of((rel ^ key) * rows, rows), rows)
                out[mode, :, here, :] = old[mode, :, here, :] + coef * piece[k]
                rel += 1


def grouped(refs, streams, per_stream):
    return [refs[i * per_stream : (i + 1) * per_stream] for i in range(streams)]


def shift_in(offsets, slot, near, away, patch, tall):
    frame = patch.shape[-1]
    h = frame // 2
    hr, cols = near.shape[2], 2 * near.shape[3]
    size = cols - 2 * h
    core = lax.axis_index("row")
    first = left_half()
    across = lax.rem(cols - corner(offsets, slot, 1, size, h), cols)

    def strip(ref, c, rows):
        x = jnp.concatenate([ref[first, c, rows, :], ref[1 - first, c, rows, :]], 1)
        return pltpu.roll(x, across, 1)[:, :frame]

    if tall:
        down = lax.rem(2 * hr - corner(offsets, slot, 0, size, h), 2 * hr)
        for c in range(2):
            halves = [strip(ref, c, slice(None)) for ref in (near, away)]
            both = [jnp.where(core == k, halves[0], halves[1]) for k in range(2)]
            patch[c] = pltpu.roll(jnp.concatenate(both, 0), down, 0)[:frame]
        return

    def body(j):
        for ref, half in ((near, core), (away, 1 - core)):
            for c in range(2):
                patch[c, at(half * hr + j * STRIP), :] = strip(ref, c, at(j * STRIP))

    strips(hr // STRIP, body)


def forward_kernel(slot, n_pieces, coef, tall, *refs):
    refs = list(refs)
    offsets, near, away, probe, tab = refs[:5]
    refs = refs[5:]
    modes = probe.shape[0]
    if n_pieces:
        streams = grouped(refs, modes, n_pieces)
        refs = refs[modes * n_pieces :]
        new_probe = refs.pop(3)
        update_probe(probe, streams, coef, new_probe)
        probe = new_probe
    far, power, patch, tall_parts, wide_parts, product = refs
    frame = probe.shape[-1]
    h = frame // 2
    shift_in(offsets, slot, near, away, patch, tall)

    def exits(m, j):
        pair = []
        for start in (j * STRIP, h + j * STRIP):
            rows = at(start)
            pr, pi = probe[m, 0, rows, :], probe[m, 1, rows, :]
            ar, ai = patch[0, rows, :], patch[1, rows, :]
            pair.append((pr * ar - pi * ai, pr * ai + pi * ar))
        for k in range(2):
            put(tall_parts, m, 0, at(k * h + j * STRIP), pair[0][k] + pair[1][k])
            put(tall_parts, m, 1, at(k * h + j * STRIP), pair[0][k] - pair[1][k])

    def columns(m, j):
        for p in range(2):
            y = [product[m, p, at(k * h + j * STRIP), :] for k in range(2)]
            rows = at(p * h + j * STRIP)
            put(wide_parts, m, 0, rows, jnp.concatenate([v[:, :h] + v[:, h:] for v in y], 1))
            put(wide_parts, m, 1, rows, jnp.concatenate([v[:, :h] - v[:, h:] for v in y], 1))

    for m in range(modes):
        strips(h // STRIP, functools.partial(exits, m))
        for p in range(2):
            product[m, p] = mul_left(tab[0, p], tall_parts[m, p])
    for m in range(modes):
        strips(h // STRIP, functools.partial(columns, m))
        for q in range(2):
            far[m, q] = mul_right(wide_parts[m, q], tab[1, q])

    def powers(j):
        rows = at(j * STRIP)
        for q in range(2):
            total = None
            for m in range(modes):
                f = far[m, q, rows, :]
                f = f * f
                f = f[:, :h] + f[:, h:]
                total = f if m == 0 else total + f
            power[rows, slice(q * h, (q + 1) * h)] = total

    strips(frame // STRIP, powers)


def inverse_kernel(mode, last, tall, *refs):
    refs = list(refs)
    offsets, counts, tab, amp, probe = refs[:5]
    refs = refs[5:]
    slots = amp.shape[0]
    fars, powers, others, patches = (refs[i * slots : (i + 1) * slots] for i in range(4))
    refs = refs[4 * slots :]
    before = refs.pop(0) if mode else None
    probe_grad, grads, tall_parts, wide_parts, product_wide, product_tall = refs
    frame = probe.shape[-1]
    h = frame // 2

    def factors(s, j):
        rows = at(j * STRIP)
        factor = amp[s, rows, :] / (jnp.sqrt(powers[s][rows, :] + others[s][rows, :]) + 0.5)
        for q in range(2):
            f = factor[:, q * h : (q + 1) * h]
            put(wide_parts, s, q, rows, fars[s][mode, q, rows, :] * jnp.concatenate([f, f], 1))

    def columns(s, j):
        for p in range(2):
            he, ho = (product_wide[s, q, at(p * h + j * STRIP), :] for q in range(2))
            for k in range(2):
                a, b = he[:, k * h : (k + 1) * h], ho[:, k * h : (k + 1) * h]
                put(tall_parts, s, p, at(k * h + j * STRIP), jnp.concatenate([a + b, a - b], 1))

    for s in range(slots):
        strips(frame // STRIP, functools.partial(factors, s))
        for q in range(2):
            product_wide[s, q] = mul_right(wide_parts[s, q], tab[0, q])
    for s in range(slots):
        strips(h // STRIP, functools.partial(columns, s))
        for p in range(2):
            product_tall[s, p] = mul_left(tab[1, p], tall_parts[s, p])
    key = chunk_key(ORDERS[mode])
    chunk = frame // CHUNKS
    core = lax.axis_index("row")
    first = left_half()

    def results(j):
        x = [
            [[product_tall[s, p, at(k * h + j * STRIP), :] for k in range(2)] for p in range(2)]
            for s in range(slots)
        ]
        for lower in range(2):
            rows = at(lower * h + j * STRIP)
            pr, pi = probe[mode, 0, rows, :], probe[mode, 1, rows, :]
            step = [None, None]
            window = [None, None]
            for s in range(slots):
                even, odd = x[s]
                xr, xi = (even[k] - odd[k] if lower else even[k] + odd[k] for k in range(2))
                live = (s < counts[0]).astype(f32)
                ar, ai = patches[s][0, rows, :], patches[s][1, rows, :]
                ur = (xr - (pr * ar - pi * ai)) * live
                ui = (xi - (pr * ai + pi * ar)) * live
                for k, g in enumerate((ar * ur + ai * ui, ar * ui - ai * ur)):
                    step[k] = g if s == 0 else step[k] + g
                for k, g in enumerate((pr * ur + pi * ui, pr * ui - pi * ur)):
                    if mode:
                        g = g + before[s, k, rows, :]
                    if not last or tall:
                        grads[s, k, rows, :] = g
                        continue
                    wide = 2 * grads.shape[-1]
                    g = jnp.concatenate([g, jnp.zeros((STRIP, wide - frame), f32)], 1)
                    g = pltpu.roll(g, corner(offsets, s, 1, wide - 2 * h, h), 1)
                    window[k] = g if s == 0 else window[k] + g
            start = lower * h + j * STRIP
            for k in range(2):
                probe_grad[(start // chunk) ^ key, k, at(start % chunk), :] = step[k]
                if last and not tall:
                    half = window[k].shape[1] // 2
                    grads[lower ^ core, first, k, at(j * STRIP), :] = window[k][:, :half]
                    grads[lower ^ core, 1 - first, k, at(j * STRIP), :] = window[k][:, half:]

    strips(h // STRIP, results)


def place_kernel(offsets, grads, out):
    slots, _, frame, _ = grads.shape
    _, _, _, hr, half = out.shape
    cols = 2 * half
    h = frame // 2
    size = cols - 2 * h
    core = lax.axis_index("row")
    first = left_half()
    for c in range(2):
        total = None
        for s in range(slots):
            g = jnp.concatenate([grads[s, c], jnp.zeros((2 * hr - frame, frame), f32)], 0)
            g = pltpu.roll(g, corner(offsets, s, 0, size, h), 0)
            g = jnp.concatenate([g, jnp.zeros((2 * hr, cols - frame), f32)], 1)
            g = pltpu.roll(g, corner(offsets, s, 1, size, h), 1)
            total = g if s == 0 else total + g
        for k in range(2):
            out[k ^ core, first, c] = total[k * hr : (k + 1) * hr, :half]
            out[k ^ core, 1 - first, c] = total[k * hr : (k + 1) * hr, half:]


def finish_kernel(n_pieces, coef, *refs):
    refs = list(refs)
    near, away, probe = refs[:3]
    streams = grouped(refs[3:], probe.shape[0], n_pieces)
    tile, new_probe = refs[-2:]
    update_probe(probe, streams, coef, new_probe)
    _, _, hr, half = near.shape
    core = lax.axis_index("row")
    first = left_half()
    for ref, part in ((near, core), (away, 1 - core)):
        rows = pl.ds(pl.multiple_of(part * hr, hr), hr)
        tile[:, rows, :half] = ref[first]
        tile[:, rows, half:] = ref[1 - first]


def vmem():
    return pl.BlockSpec(memory_space=pltpu.VMEM)


def call(kernel, outs, args, scratch=(), flops=0):
    size = sum(math.prod(a.shape) * a.dtype.itemsize for a in args)
    size += sum(math.prod(o) * 4 for o in outs)
    return pl.pallas_call(
        kernel,
        out_shape=[jax.ShapeDtypeStruct(o, f32) for o in outs],
        in_specs=[
            pl.BlockSpec(memory_space=pltpu.SMEM) if a.dtype == jnp.int32 else vmem() for a in args
        ],
        out_specs=[vmem() for _ in outs],
        scratch_shapes=list(scratch),
        cost_estimate=pl.CostEstimate(flops=flops, bytes_accessed=size, transcendentals=0),
        compiler_params=pltpu.CompilerParams(vmem_limit_bytes=40 * 1024 * 1024),
    )(*args)


def swap_rows(x):
    return lax.ppermute(x, "row", [(0, 1), (1, 0)])


def beside(x, inner, tiles):
    pairs = []
    for t in range(tiles):
        other = t + 1 if (t % 2 == 0) == inner else t - 1
        if 0 <= other < tiles and other // GX == t // GX:
            pairs.append((t, other))
    return lax.ppermute(x, "tile", pairs)


def swap_vertical(x, tiles):
    pairs = [(2 * t, 2 * (t - GX) + 1) for t in range(GX, tiles)]
    pairs += [(2 * t + 1, 2 * (t + GX)) for t in range(tiles - GX)]
    return lax.ppermute(x, ("tile", "row"), pairs)


def exchange(x, bit, tiles):
    return lax.ppermute(x, "tile", [(s, s ^ (1 << bit)) for s in range(tiles)])


def together(*groups):
    return lax.optimization_barrier(groups)


def halves(x, even, inner):
    half = x.shape[-1] // 2
    own_first = even == inner
    a, b = x[..., :half], x[..., half:]
    return jnp.where(own_first, a, b), jnp.where(own_first, b, a)


def joined(own, other, even, inner):
    own_first = even == inner
    return jnp.concatenate([jnp.where(own_first, own, other), jnp.where(own_first, other, own)], -1)


def window_parts(grad, even, wide):
    if wide:
        return [grad[0], grad[1]], [grad[0], grad[1]]
    return zip(*(halves(grad[k], even, k == 0) for k in range(2)))


def reduce_all(parts, grad, even, tiles, wide):
    bits = int(math.log2(tiles))
    stay, go = window_parts(grad, even, wide)
    held = list(parts)
    go, got = list(go), [None, None]
    for i in range(HALVINGS):
        n = held[0].shape[0] // 2
        held = [h[:n] + exchange(h[n:], o[i], tiles) for h, o in zip(held, ORDERS)]
        held, go[1 - i] = together(held, go[1 - i])
        got[1 - i] = beside(go[1 - i], i == 1, tiles)
    held = [h + exchange(h, o[-1], tiles) for h, o in zip(held, ORDERS)]
    held, got = together(held, got)
    for bit in range(len(ORDERS[0]), bits):
        held = [h + exchange(h, bit, tiles) for h in held]
    pieces = [[h] for h in held]
    for i in reversed(range(HALVINGS)):
        for p, o in zip(pieces, ORDERS):
            p.append(exchange(p[0] if len(p) == 1 else jnp.concatenate(p, 0), o[i], tiles))
    return pieces, jnp.stack([a + b for a, b in zip(stay, got)])


def per_device(object_tiles, probe_modes, amplitude, offsets, counts):
    own_tile = object_tiles[0]
    size = own_tile.shape[-1]
    frame = probe_modes.shape[-1]
    half = frame // 2
    tiles = lax.axis_size("tile")
    tall = tiles > GX
    slots = offsets.shape[0]
    modes = probe_modes.shape[0]
    core = lax.axis_index("row")
    even = lax.axis_index("tile") % 2 == 0
    hr = size // 2
    tab = jnp.asarray(tables(frame))
    perm = jnp.asarray(deinterleave(frame))
    coef = 4.0 / (slots * tiles)

    mine = lax.dynamic_slice(own_tile, (0, core * hr, 0), (2, hr, size))
    own = [jnp.where(even == inner, mine[:, :, half:], mine[:, :, :half]) for inner in (True, False)]
    got = [beside(own[1], False, tiles), beside(own[0], True, tiles)]
    near = jnp.stack([joined(own[0], got[1], even, True), joined(own[1], got[0], even, False)])
    if tall:
        other = swap_vertical(near, tiles)
        near = jnp.where(core == 0, jnp.concatenate([other, near], 2), jnp.concatenate([near, other], 2))
    (amp,) = call(amplitude_kernel, [amplitude.shape], [amplitude, perm])
    away = swap_rows(near)
    near, away, amp = together(near, away, amp)

    def scratch(count):
        return [pltpu.VMEM((count, 2, 2, frame, frame), bf16) for _ in range(2)]

    matmul = 4 * 2 * 3 * 4 * frame**3
    probe = probe_modes
    streams = None
    for iteration in range(ITERS):
        final = iteration + 1 == ITERS
        fars, powers, others, patches = [], [], [], []
        for s in range(slots):
            args = [offsets, near, away, probe, tab]
            outs = [(modes, 2, frame, frame), (frame, frame), (2, frame, frame)]
            count = 0
            if streams is not None:
                count = len(streams[0])
                args += [p for group in streams for p in group]
                outs.append(probe.shape)
                streams = None
            got = call(
                functools.partial(forward_kernel, s, count, coef, tall),
                outs,
                args,
                scratch(modes) + [pltpu.VMEM((modes, 2, frame, frame), f32)],
                matmul * modes,
            )
            if count:
                probe = got[3]
            fars.append(got[0])
            powers.append(got[1])
            patches.append(got[2])
            others.append(swap_rows(got[1]))
        before = None
        parts = []
        for m in range(modes):
            last = m == modes - 1
            args = [offsets, counts, tab, amp, probe] + fars + powers + others + patches
            if m:
                args.append(before)
            grads = (2,) + near.shape if last and not tall else (slots, 2, frame, frame)
            part = (CHUNKS, 2, frame // CHUNKS, frame)
            got = call(
                functools.partial(inverse_kernel, m, last, tall),
                [part, grads],
                args,
                scratch(slots) + [pltpu.VMEM((slots, 2, frame, frame), f32) for _ in range(2)],
                matmul * slots,
            )
            parts.append(got[0])
            before = got[1]
        if tall:
            (before,) = call(place_kernel, [(2,) + near.shape], [offsets, before])
        grad = before[0] + swap_rows(before[1])
        wide = tall or not final
        streams, total = reduce_all(parts, grad, even, tiles, wide)
        if tall:
            total = total + swap_vertical(total, tiles)
        if wide:
            near = near + total / MODES
        if final:
            near = jnp.stack([halves(near[k], even, k == 0)[0] for k in range(2)])
            if not wide:
                near = near + total / MODES
            if tall:
                near = jnp.where(core == 0, near[:, :, half:], near[:, :, : size - half])
        away = swap_rows(near)
    args = [near, away, probe] + [p for group in streams for p in group]
    tile, probe = call(
        functools.partial(finish_kernel, len(streams[0]), coef), [own_tile.shape, probe.shape], args
    )
    return (tile[None], probe)


def solution(mesh):
    return jax.shard_map(
        per_device,
        mesh=mesh,
        in_specs=(
            P(("scan", "tile"), None, None, None),
            P("row", None, None, None),
            P(("scan", "tile"), None, None),
            P(("scan", "tile"), None),
            P(("scan", "tile")),
        ),
        out_specs=(P(("scan", "tile"), None, None, None), P(("scan", "row"), None, None, None)),
        check_vma=False,
    )
```
